32 devices in a mesh: dp: 4 (over y, core), expert: 8 (over z, x).
Axes of the slice: x: 2, y: 2, z: 4, core: 2. Of those that a mesh axis runs over, the one named last changes fastest.
Arguments:
- tokens: bfloat16 [4096, 2048], P(('dp', 'expert')), may hold values from -6 to 6
- attention_gain: bfloat16 [2048], replicated, may hold values from 0.5 to 1.5
- query_weight: bfloat16 [2048, 2048], P(None, 'expert'), may hold values from -0.125 to 0.125
- query_bias: bfloat16 [2048], P('expert'), may hold values from -3 to 3
- key_weight: bfloat16 [2048, 2048], P(None, 'expert'), may hold values from -0.125 to 0.125
- key_bias: bfloat16 [2048], P('expert'), may hold values from -3 to 3
- value_weight: bfloat16 [2048, 2048], P(None, 'expert'), may hold values from -0.125 to 0.125
- value_bias: bfloat16 [2048], P('expert'), may hold values from -3 to 3
- output_weight: bfloat16 [2048, 2048], P(None, 'expert'), may hold values from -0.5 to 0.5
- feedforward_gain: bfloat16 [2048], replicated, may hold values from 0.5 to 1.5
- shared_gate_weight: bfloat16 [2048, 5632], P(None, 'expert'), may hold values from -0.125 to 0.125
- shared_up_weight: bfloat16 [2048, 5632], P(None, 'expert'), may hold values from -0.125 to 0.125
- shared_down_weight: bfloat16 [2048, 5632], P(None, 'expert'), may hold values from -0.078125 to 0.078125
- shared_switch: bfloat16 [2048], replicated, may hold values from -0.125 to 0.125
- router_weight: bfloat16 [2048, 8], replicated, may hold values from -0.0625 to 0.0625
- expert_in: bfloat16 [8, 2048, 2816], P('expert'), may hold values from -0.125 to 0.125
- expert_out: bfloat16 [8, 2048, 1408], P('expert'), may hold values from -1.25 to 1.25
- routes: int32 [4096, 4], P(('dp', 'expert')), may hold values from 0 to 7, all different within a row; in each aligned block of 128 rows (0 to 127, 128 to 255, ...) at most 128 rows name the same one
- cotangent: bfloat16 [4096, 2048], P(('dp', 'expert')), may hold values from -6 to 6
Outputs:
- layer_out: bfloat16 [4096, 2048], P(('dp', 'expert'))
- grad_tokens: float32 [4096, 2048], P(('dp', 'expert'))
- grad_attention_gain: float32 [2048], replicated
- grad_query_weight: float32 [2048, 2048], P('dp', 'expert')
- grad_query_bias: float32 [2048], P('expert')
- grad_key_weight: float32 [2048, 2048], P('dp', 'expert')
- grad_key_bias: float32 [2048], P('expert')
- grad_value_weight: float32 [2048, 2048], P('dp', 'expert')
- grad_value_bias: float32 [2048], P('expert')
- grad_output_weight: float32 [2048, 2048], P('dp', 'expert')
- grad_feedforward_gain: float32 [2048], replicated
- grad_shared_gate_weight: float32 [2048, 5632], P('dp', 'expert')
- grad_shared_up_weight: float32 [2048, 5632], P('dp', 'expert')
- grad_shared_down_weight: float32 [2048, 5632], P('dp', 'expert')
- grad_shared_switch: float32 [2048], replicated
- grad_router_weight: float32 [2048, 8], replicated
- grad_expert_in: float32 [8, 2048, 2816], P('expert', 'dp')
- grad_expert_out: float32 [8, 2048, 1408], P('expert', 'dp')
The draws below stay inside these ranges and needn't reach their ends.
Inputs may be any that keep to these rules, and one draw needn't show every extreme that they name: `routes`: each token names 4 different experts. Among the rows of one device (aligned blocks of 128 tokens) no expert is named more than 128 times, a bound that some block reaches.
All inputs are finite; a program needn't handle non-finite values.
Results may differ from the reference program's by a relative error of at most 0.03.
Values may be sent and summed in bfloat16 or wider, within the bound.
No kernel may reach another device: no remote copies, remote signals or barrier semaphores. Data moves between devices by JAX's collectives and lax.ppermute only.
A program may use at most 256 MiB of HBM per device.

```python
import math
from functools import partial
import jax
import jax.numpy as jnp
import numpy as np
from jax import lax

D = 2048
H = 16
HD = 128
FF = 1408
SFF = 5632
TOP = 4
TOK_DEV = 128
LENGTH = 1024
TOKENS = 4096
EXPERTS = 8
CAP = 128
N_DP = 4


def block_scale(own_key, shape, pieces, least, high):
    loudness, own = 1.0, jax.random.fold_in(own_key, 6)
    for axis_at, blocks in pieces:
        draws = jnp.exp(jax.random.uniform(jax.random.fold_in(own, axis_at), (blocks,), jnp.float32, least / len(pieces), high / len(pieces)))
        loudness = loudness * jnp.repeat(draws, shape[axis_at] // blocks).reshape([-1 if axis == axis_at else 1 for axis in range(len(shape))])
    return loudness


def deal_out(key, own, number, rows, count, top, limit, lean):
    order = jax.random.permutation(key, count)
    heavy_load, usual = shares(count, rows * top, limit, lean, True), shares(count, rows * top, limit, lean, False)
    places = jnp.arange(count)

    def named(lengths, rotation):
        used = int((lengths > 0).sum())
        fixed = max(1, used // 4)
        passed = fixed + (places - fixed + rotation * (used - fixed)) % max(1, count - fixed)
        return jnp.zeros((count,), jnp.int32).at[order[jnp.where(places < fixed, places, passed)]].set(jnp.asarray(lengths, jnp.int32))

    lengths = jnp.where(number % 4 == 0, named(heavy_load, number // 4), named(usual, number - number // 4 - 1))
    mixed = jax.random.permutation(jax.random.fold_in(own, 3), count)
    giver, receiver = mixed[0:count // 2 * 2:2], mixed[1:count // 2 * 2:2]
    room = jnp.minimum(lengths[giver] - 1, limit - lengths[receiver]) // 2
    room = jnp.where((giver == order[0]) | (receiver == order[0]) | (lengths[receiver] == 0), 0, jnp.maximum(room, 0))
    passed = jax.random.randint(jax.random.fold_in(own, 4), (count // 2,), 0, 1 << 20) % (room + 1)
    lengths = lengths.at[giver].add(-passed).at[receiver].add(passed)
    items = jnp.searchsorted(jnp.cumsum(lengths), jnp.arange(rows * top), side="right").astype(jnp.int32)
    grid = items.reshape(top, rows).T
    grid = grid[jax.random.permutation(jax.random.fold_in(own, 1), rows)]
    rotation = jax.random.randint(jax.random.fold_in(own, 2), (rows, 1), 0, top)
    return jnp.take_along_axis(grid, (jnp.arange(top)[None, :] + rotation) % top, axis=1)


def shares(amount, total, bound, lean, full):
    weights = [(1 << 20) // math.isqrt(standing ** lean) + 1 for standing in range(1, amount + 1)]
    largest = bound if full else min(bound, max(-(-total // amount), total * weights[0] // sum(weights)))
    least = 1 if total - largest >= amount - 1 else 0
    counts, surplus = [largest] + [least] * (amount - 1), total - largest - least * (amount - 1)
    while surplus > 0:
        candidates = [i for i in range(1, amount) if counts[i] < largest] or [i for i in range(1, amount) if counts[i] < bound]
        pool, remaining = sum([weights[i] for i in candidates]), surplus
        for i in candidates:
            more = min(bound - counts[i], max(1, remaining * weights[i] // pool), surplus)
            counts[i] = counts[i] + more
            surplus = surplus - more
    return np.array(counts)


def normal_values(stream_key, dims, width, reach, pieces=(), held_as=jnp.bfloat16):
    gain = block_scale(stream_key, dims, pieces, -0.22, 0.18) if pieces else 1.0
    drawn = jax.random.normal(stream_key, dims, jnp.float32) * width * gain
    return jnp.minimum(jnp.maximum(drawn, -reach), reach).astype(held_as)


def setup_inputs(seed: int = 0) -> dict:
    key_of = jax.random.split(jax.random.key(seed), 20)
    tokens = normal_values(key_of[0], (TOKENS, D), 1.0, 6.0, ((0, 32),))
    attention_gain = jnp.clip(1.0 + 0.1 * jax.random.normal(key_of[1], (D,), jnp.float32), 0.5, 1.5).astype(jnp.bfloat16)
    query_weight = normal_values(key_of[2], (D, H * HD), D ** -0.5, 0.125, ((1, 8),))
    query_bias = normal_values(key_of[3], (H * HD,), 0.5, 3.0, ((0, 8),))
    key_weight = normal_values(key_of[4], (D, H * HD), D ** -0.5, 0.125, ((1, 8),))
    key_bias = normal_values(key_of[5], (H * HD,), 0.5, 3.0, ((0, 8),))
    value_weight = normal_values(key_of[6], (D, H * HD), D ** -0.5, 0.125, ((1, 8),))
    value_bias = normal_values(key_of[7], (H * HD,), 0.5, 3.0, ((0, 8),))
    output_weight = normal_values(key_of[8], (D, H * HD), (H * HD // 16) ** -0.5, 0.5, ((1, 8),))
    feedforward_gain = jnp.clip(1.0 + 0.1 * jax.random.normal(key_of[9], (D,), jnp.float32), 0.5, 1.5).astype(jnp.bfloat16)
    shared_gate_weight = normal_values(key_of[10], (D, SFF), D ** -0.5, 0.125, ((1, 8),))
    shared_up_weight = normal_values(key_of[11], (D, SFF), D ** -0.5, 0.125, ((1, 8),))
    shared_down_weight = normal_values(key_of[12], (D, SFF), SFF ** -0.5, 0.078125, ((1, 8),))
    shared_switch = normal_values(key_of[13], (D,), D ** -0.5, 0.125)
    router_weight = normal_values(key_of[14], (D, EXPERTS), (4 * D) ** -0.5, 0.0625)
    expert_in = normal_values(key_of[15], (EXPERTS, D, 2 * FF), D ** -0.5, 0.125, ((0, 8),))
    expert_out = normal_values(key_of[16], (EXPERTS, D, FF), (max(FF // 64, 1)) ** -0.5, 1.25, ((0, 8),))
    routes_keys = jax.random.split(jax.random.fold_in(key_of[17], 1), TOKENS // TOK_DEV)
    routes_turns = jax.random.permutation(jax.random.fold_in(key_of[17], 3), TOKENS // TOK_DEV)
    routes = jax.vmap(lambda own, number: deal_out(jax.random.fold_in(key_of[17], 2), own, number, TOK_DEV, EXPERTS, TOP, CAP, 1))(routes_keys, routes_turns).reshape((TOKENS, TOP))
    cotangent = normal_values(key_of[18], (TOKENS, D), 1.0, 6.0, ((0, 32),))
    return dict(tokens=tokens, attention_gain=attention_gain, query_weight=query_weight, query_bias=query_bias, key_weight=key_weight, key_bias=key_bias, value_weight=value_weight, value_bias=value_bias, output_weight=output_weight, feedforward_gain=feedforward_gain, shared_gate_weight=shared_gate_weight, shared_up_weight=shared_up_weight, shared_down_weight=shared_down_weight, shared_switch=shared_switch, router_weight=router_weight, expert_in=expert_in, expert_out=expert_out, routes=routes, cotangent=cotangent)


EPSILON = 1e-06
THETA = 1000000.0
HIGHEST = lax.Precision.HIGHEST

@jax.custom_vjp
def low(v):
    return lax.optimization_barrier(v.astype(jnp.bfloat16)).astype(jnp.float32)

@jax.custom_vjp
def low_back(v):
    return v

def low_keep(v):
    return (low(v), None)

def low_pass(kept, grad):
    return (grad,)

def back_keep(v):
    return (v, None)

def back_low(kept, grad):
    return (low(grad),)
low.defvjp(low_keep, low_pass)
low_back.defvjp(back_keep, back_low)

def product(left_side, right_side):
    return jnp.dot(left_side, right_side, precision=HIGHEST)

def turn_half(values):
    middle = values.shape[-1] // 2
    return jnp.concatenate([-values[..., middle:], values[..., :middle]], -1)

def rope_tables(length, head_width):
    middle = head_width // 2
    inverse = THETA ** (-(jnp.arange(middle, dtype=jnp.float32) * 2.0 / head_width))
    angles = jnp.arange(length, dtype=jnp.float32)[:, None] * inverse[None, :]
    return (jnp.concatenate([jnp.cos(angles)] * 2, -1), jnp.concatenate([jnp.sin(angles)] * 2, -1))

def rotate(values, cosine_table, sine_table):
    return values * cosine_table[:, None, :] + turn_half(values) * sine_table[:, None, :]

def rms_scale(values):
    return lax.rsqrt(lax.optimization_barrier(jnp.mean(values * values, -1, keepdims=True)) + EPSILON)

def softmax_rows(scores):
    row_peak = lax.optimization_barrier(jnp.max(scores, -1, keepdims=True))
    raised = jnp.exp(scores - row_peak)
    return raised / lax.optimization_barrier(jnp.sum(raised, -1, keepdims=True))

def sequence_attention(packed):
    queries, key_rows, value_rows = packed
    block_rows = min(512, LENGTH)
    block_count = LENGTH // block_rows
    query_blocks = queries.reshape(block_count, block_rows, H, HD)
    starts = jnp.arange(block_count, dtype=jnp.int32) * block_rows

    def one_block(inputs):
        query_block, row_start = inputs
        raw_scores = jnp.einsum('qhd,khd->hqk', query_block, key_rows, precision=HIGHEST)
        rows_at = row_start + jnp.arange(block_rows, dtype=jnp.int32)
        causal = jnp.arange(LENGTH, dtype=jnp.int32)[None, None, :] <= rows_at[None, :, None]
        scores = jnp.where(causal, low_back(raw_scores) * HD ** (-0.5), -jnp.inf)
        probs = low(softmax_rows(scores))
        return jnp.einsum('hqk,khd->qhd', probs, value_rows, precision=HIGHEST)
    outputs = lax.map(jax.checkpoint(one_block), (query_blocks, starts))
    return outputs.reshape(LENGTH, H, HD)

def expert_block(packed):
    row_block, weight_in, weight_out = packed
    joined = product(row_block, weight_in)
    gate_pre = low_back(joined[:, :FF])
    up_pre = low_back(joined[:, FF:])
    hidden = low(jax.nn.silu(gate_pre) * up_pre)
    return low(low_back(product(hidden, weight_out.T)))

def routed_experts(h_ffn, routes, expert_in, expert_out):
    device_count = TOKENS // TOK_DEV
    flat_routes = routes.reshape(-1)
    onehot_hits = (flat_routes[:, None] == jnp.arange(EXPERTS, dtype=jnp.int32)[None, :]).astype(jnp.int32)
    onehot_hits = onehot_hits.reshape(device_count, TOK_DEV * TOP, EXPERTS)
    before = jnp.cumsum(onehot_hits, 1) - onehot_hits
    slot_ids = lax.optimization_barrier(jnp.sum(before * onehot_hits, -1)).reshape(-1)
    owners = (jnp.arange(TOKENS * TOP, dtype=jnp.int32) // (TOK_DEV * TOP)).astype(jnp.int32)
    places = (flat_routes * device_count + owners) * CAP + slot_ids
    copies = low_back(jnp.repeat(h_ffn, TOP, axis=0))
    buffer = jnp.zeros((EXPERTS * device_count * CAP, D), jnp.float32).at[places].set(copies)
    buffer = buffer.reshape(EXPERTS, device_count * CAP, D)
    results = lax.map(jax.checkpoint(expert_block), (buffer, expert_in, expert_out))
    return results.reshape(-1, D)[places].reshape(TOKENS, TOP, D)

def block_layer(routes, x_float, attention_gain, query_weight, query_bias, key_weight, key_bias, value_weight, value_bias, output_weight, feedforward_gain, shared_gate_weight, shared_up_weight, shared_down_weight, shared_switch, router_weight, expert_in, expert_out):
    cosine_table, sine_table = rope_tables(LENGTH, HD)
    h_attn = low(x_float * rms_scale(x_float) * attention_gain)

    def split_heads(values):
        return values.reshape(N_DP, LENGTH, H, HD)
    q_rot = low(rotate(split_heads(low_back(product(h_attn, query_weight) + query_bias)), cosine_table, sine_table))
    k_rot = low(rotate(split_heads(low_back(product(h_attn, key_weight) + key_bias)), cosine_table, sine_table))
    v_low = low(low_back(split_heads(product(h_attn, value_weight) + value_bias)))
    attended = lax.map(sequence_attention, (q_rot, k_rot, v_low)).reshape(TOKENS, H * HD)
    att_low = low(low_back(attended))
    attention = low_back(product(att_low, output_weight.T))
    residual = x_float + attention
    h_ffn = low(residual * rms_scale(residual) * feedforward_gain)
    gate_pre = low_back(product(h_ffn, shared_gate_weight))
    up_pre = low_back(product(h_ffn, shared_up_weight))
    shared_hidden = low(jax.nn.silu(gate_pre) * up_pre)
    shared = low_back(product(shared_hidden, shared_down_weight.T))
    switch = jax.nn.sigmoid(product(h_ffn, shared_switch))
    router_probs = softmax_rows(product(h_ffn, router_weight))
    gate_probs = jnp.take_along_axis(router_probs, routes, 1)
    routed = routed_experts(h_ffn, routes, expert_in, expert_out)
    return residual + switch[:, None] * shared + lax.optimization_barrier(jnp.sum(gate_probs[:, :, None] * routed, 1))

def reference(tokens, attention_gain, query_weight, query_bias, key_weight, key_bias, value_weight, value_bias, output_weight, feedforward_gain, shared_gate_weight, shared_up_weight, shared_down_weight, shared_switch, router_weight, expert_in, expert_out, routes, cotangent):
    floats = [argument.astype(jnp.float32) for argument in (tokens, attention_gain, query_weight, query_bias, key_weight, key_bias, value_weight, value_bias, output_weight, feedforward_gain, shared_gate_weight, shared_up_weight, shared_down_weight, shared_switch, router_weight, expert_in, expert_out)]
    layer_out, pullback = jax.vjp(partial(block_layer, routes), *floats)
    gradients = pullback(cotangent.astype(jnp.float32))
    return (layer_out.astype(jnp.bfloat16), gradients[0], gradients[1], gradients[2], gradients[3], gradients[4], gradients[5], gradients[6], gradients[7], gradients[8], gradients[9], gradients[10], gradients[11], gradients[12], gradients[13], gradients[14], gradients[15], gradients[16])
```

```python
import functools

import jax
import jax.numpy as jnp
from jax import lax
from jax.experimental import pallas as pl
from jax.experimental.pallas import tpu as pltpu
from jax.sharding import PartitionSpec as P

HD = 128
EPSILON = 1e-06
THETA = 1000000.0
HIGHEST = lax.Precision.HIGHEST
BF = jnp.bfloat16
F32 = jnp.float32


def rope_tables(length):
    middle = HD // 2
    inverse = THETA ** (-(jnp.arange(middle, dtype=F32) * 2.0 / HD))
    angles = jnp.arange(length, dtype=F32)[:, None] * inverse[None, :]
    sine = jnp.sin(angles)
    return (jnp.concatenate([jnp.cos(angles)] * 2, -1), jnp.concatenate([-sine, sine], -1))


def rms_scale(values):
    return lax.rsqrt(jnp.mean(values * values, -1, keepdims=True) + EPSILON)


def plain_dot(left_side, right_side):
    return jnp.dot(left_side, right_side, preferred_element_type=F32)


def right_dot(left_side, right_side):
    return lax.dot_general(
        left_side, right_side, (((1,), (1,)), ((), ())), preferred_element_type=F32
    )


def left_dot(left_side, right_side):
    return lax.dot_general(
        left_side, right_side, (((0,), (0,)), ((), ())), preferred_element_type=F32
    )


def ring_order(count):
    wide = 2 if count <= 8 else 4
    tall = count // wide
    order = [z * wide for z in range(tall)]
    for z in range(tall - 1, -1, -1):
        row = list(range(1, wide))
        if (tall - 1 - z) % 2:
            row = row[::-1]
        order += [z * wide + x for x in row]
    return order


class Ring:
    def __init__(self, count):
        self.count = count
        self.half = count // 2
        order = ring_order(count)
        self.forward = [(order[i], order[(i + 1) % count]) for i in range(count)]
        self.backward = [(order[i], order[(i - 1) % count]) for i in range(count)]
        place = [0] * count
        for at, device in enumerate(order):
            place[device] = at
        distances = [0]
        for step in range(1, self.half):
            distances += [-step, step]
        distances.append(self.half)
        here = jnp.array(place, jnp.int32)[lax.axis_index("expert")]
        around = (here + jnp.array(distances, jnp.int32) + count) % count
        self.block_of_slot = jnp.array(order, jnp.int32)[around]
        hits = self.block_of_slot[None, :] == jnp.arange(count, dtype=jnp.int32)[:, None]
        self.slot_of_block = jnp.sum(hits * jnp.arange(count, dtype=jnp.int32)[None, :], 1)

    def slot(self, distance):
        if distance == self.half:
            return self.count - 1
        return 2 * abs(distance) - (distance < 0)

    def gather(self, block):
        middle = block.shape[0] // 2
        pieces = [block]
        ahead = behind = block
        for step in range(1, self.half):
            ahead = lax.ppermute(ahead, "expert", self.forward)
            behind = lax.ppermute(behind, "expert", self.backward)
            pieces += [ahead, behind]
        pieces.append(lax.ppermute(ahead[:middle], "expert", self.forward))
        pieces.append(lax.ppermute(behind[middle:], "expert", self.backward))
        return jnp.concatenate(pieces, 0)

    def scatter_sum(self, partial, held=BF):
        rows = partial.shape[0] // self.count
        middle = rows // 2

        def own(distance):
            start = self.slot(distance) * rows
            return partial[start : start + rows]

        far = own(self.half).astype(held)
        ahead = lax.ppermute(far[:middle], "expert", self.forward)
        behind = lax.ppermute(far[middle:], "expert", self.backward)
        for step in range(self.half - 1, 0, -1):
            up = own(step).astype(F32)
            down = own(-step).astype(F32)
            if step == self.half - 1:
                up = jnp.concatenate([up[:middle] + ahead.astype(F32), up[middle:]], 0)
                down = jnp.concatenate([down[:middle], down[middle:] + behind.astype(F32)], 0)
            else:
                up = up + ahead.astype(F32)
                down = down + behind.astype(F32)
            ahead = lax.ppermute(up.astype(held), "expert", self.forward)
            behind = lax.ppermute(down.astype(held), "expert", self.backward)
        return own(0).astype(F32) + ahead.astype(F32) + behind.astype(F32)


def cube_sum(values, axis):
    count = lax.axis_size(axis)
    step = 1
    while step < count:
        values = values + lax.ppermute(values, axis, [(i, i ^ step) for i in range(count)])
        step *= 2
    return values


def split_cores(values):
    count = lax.axis_size("dp")
    core = lax.axis_index("dp") % 2
    columns = values.shape[1] // count
    even = [values[:, i * columns : (i + 1) * columns] for i in range(0, count, 2)]
    odd = [values[:, i * columns : (i + 1) * columns] for i in range(1, count, 2)]
    even = jnp.concatenate(even, 1)
    odd = jnp.concatenate(odd, 1)
    return jnp.where(core == 0, odd, even), jnp.where(core == 0, even, odd)


def pair_sum(left_sides, right_side):
    count = lax.axis_size("dp")
    tall = count // 2
    far = lax.axis_index("dp") // 2
    other, own = left_sides
    rows = other.shape[1] // tall
    arrived = lax.ppermute(
        left_dot(other, right_side).astype(BF), "dp", [(i, i ^ 1) for i in range(count)]
    )
    both = left_dot(own, right_side) + arrived.astype(F32)

    def pick(which):
        return lax.dynamic_slice_in_dim(both, which * rows, rows, 0)

    total = pick(far)
    for step in range(1, tall):
        moves = [(i, (i // 2 + step) % tall * 2 + i % 2) for i in range(count)]
        out = pick((far + step) % tall).astype(BF)
        total = total + lax.ppermute(out, "dp", moves).astype(F32)
    return total


WHOLE = pl.BlockSpec(memory_space=pltpu.VMEM)


def params(mebibytes):
    return pltpu.CompilerParams(vmem_limit_bytes=mebibytes * 1024 * 1024)


def cost(flops, nbytes):
    return pl.CostEstimate(flops=int(flops), bytes_accessed=int(nbytes), transcendentals=0)


def turned(values, cosine, sine):
    return values * cosine + pltpu.roll(values, HD // 2, 1) * sine


def project_kernel(block_rows, places, h_ref, wq, wk, wv, bq, bk, bv, cos, sin, q_ref, k_ref, v_ref):
    step = pl.program_id(0)
    per_step = h_ref.shape[0] // block_rows
    h = h_ref[...]
    q = plain_dot(h, wq[...]) + bq[...].astype(F32)
    k = plain_dot(h, wk[...]) + bk[...].astype(F32)
    v = plain_dot(h, wv[...]) + bv[...].astype(F32)
    for part in range(per_step):
        start = places[step * per_step + part] * block_rows
        rows = pl.ds(pl.multiple_of(start, block_rows), block_rows)
        near = slice(part * block_rows, (part + 1) * block_rows)
        cosine, sine = cos[rows, :], sin[rows, :]
        for head in range(q.shape[1] // HD):
            cols = slice(head * HD, (head + 1) * HD)
            q_ref[rows, cols] = turned(q[near, cols], cosine, sine).astype(BF)
            k_ref[rows, cols] = turned(k[near, cols], cosine, sine).astype(BF)
        v_ref[rows, :] = v[near].astype(BF)


def project(ring, h_all, weights, biases, tables):
    length, width = h_all.shape
    cols = weights[0].shape[1]
    block_rows = length // ring.count
    step_rows = 2 * block_rows
    shape = jax.ShapeDtypeStruct((length, cols), BF)
    return pl.pallas_call(
        functools.partial(project_kernel, block_rows),
        out_shape=(shape,) * 3,
        grid_spec=pltpu.PrefetchScalarGridSpec(
            num_scalar_prefetch=1,
            grid=(length // step_rows,),
            in_specs=[pl.BlockSpec((step_rows, width), lambda i, places: (i, 0))]
            + [pl.BlockSpec((width, cols), lambda i, places: (0, 0))] * 3
            + [pl.BlockSpec((1, cols), lambda i, places: (0, 0))] * 3
            + [pl.BlockSpec((length, HD), lambda i, places: (0, 0))] * 2,
            out_specs=[pl.BlockSpec((length, cols), lambda i, places: (0, 0))] * 3,
        ),
        compiler_params=params(40),
        cost_estimate=cost(6 * length * width * cols, 2 * length * width + 6 * width * cols),
        name="project",
    )(ring.block_of_slot, h_all, *weights, *[b[None] for b in biases], *tables)


def attend_kernel(block_rows, wide, slots, q_ref, k_ref, v_ref, out_ref):
    length, cols = q_ref.shape
    scale = HD ** (-0.5)
    at_row = lax.broadcasted_iota(jnp.int32, (wide, wide), 0)
    at_col = lax.broadcasted_iota(jnp.int32, (wide, wide), 1)
    allowed = at_col <= at_row
    for head in range(cols // HD):
        hs = slice(head * HD, (head + 1) * HD)
        for i in range(length // wide):
            low, high = i * wide, (i + 1) * wide
            q = q_ref[low:high, hs]
            near = right_dot(q, k_ref[low:high, hs]) * scale
            near = jnp.where(allowed, near, -jnp.inf)
            peak = jnp.max(near, 1, keepdims=True)
            if i:
                past = right_dot(q, k_ref[:low, hs]) * scale
                peak = jnp.maximum(peak, jnp.max(past, 1, keepdims=True))
                past = jnp.exp(past - peak)
            near = jnp.exp(near - peak)
            total = jnp.sum(near, 1, keepdims=True)
            if i:
                total = total + jnp.sum(past, 1, keepdims=True)
            share = 1.0 / total
            out = plain_dot((near * share).astype(BF), v_ref[low:high, hs])
            if i:
                out = out + plain_dot((past * share).astype(BF), v_ref[:low, hs])
            out = out.astype(BF)
            for part in range(wide // block_rows):
                slot = slots[i * (wide // block_rows) + part]
                rows = pl.ds(pl.multiple_of(slot * block_rows, block_rows), block_rows)
                out_ref[rows, hs] = out[part * block_rows : (part + 1) * block_rows]


def attend(ring, q, k, v):
    length, cols = q.shape
    return pl.pallas_call(
        functools.partial(attend_kernel, length // ring.count, 2 * (length // ring.count)),
        out_shape=jax.ShapeDtypeStruct((length, cols), BF),
        in_specs=[pl.BlockSpec(memory_space=pltpu.SMEM)] + [WHOLE] * 3,
        out_specs=WHOLE,
        compiler_params=params(40),
        cost_estimate=cost(2 * length * length * cols, 8 * length * cols),
        name="attend",
    )(ring.slot_of_block, q, k, v)


def attend_back_kernel(
    block_rows, wide, slots, q_ref, k_ref, v_ref, g_ref, cos, sin, dq_ref, dk_ref, dv_ref, k_sum, v_sum
):
    length, cols = q_ref.shape
    scale = HD ** (-0.5)
    at_key = lax.broadcasted_iota(jnp.int32, (wide, wide), 0)
    at_query = lax.broadcasted_iota(jnp.int32, (wide, wide), 1)
    allowed = at_key <= at_query
    per = wide // block_rows

    def put(ref, low, hs, values):
        for part in range(per):
            slot = slots[low // block_rows + part]
            rows = pl.ds(pl.multiple_of(slot * block_rows, block_rows), block_rows)
            ref[rows, hs] = values[part * block_rows : (part + 1) * block_rows].astype(BF)

    def back(values, low, high):
        return values * cos[low:high] - pltpu.roll(values, HD // 2, 1) * sin[low:high]

    for head in range(cols // HD):
        hs = slice(head * HD, (head + 1) * HD)
        for i in range(length // wide):
            low, high = i * wide, (i + 1) * wide
            q = q_ref[low:high, hs]
            g = g_ref[low:high, hs]
            spans = [(low, high)] + ([(0, low)] if i else [])
            scores = [right_dot(k_ref[a:b, hs], q) * scale for a, b in spans]
            scores[0] = jnp.where(allowed, scores[0], -jnp.inf)
            peak = functools.reduce(jnp.maximum, [jnp.max(s, 0, keepdims=True) for s in scores])
            probs = [jnp.exp(s - peak) for s in scores]
            total = sum(jnp.sum(p, 0, keepdims=True) for p in probs)
            share = 1.0 / total
            probs = [p * share for p in probs]
            grads = [right_dot(v_ref[a:b, hs], g) for a, b in spans]
            mean = sum(jnp.sum(p * d, 0, keepdims=True) for p, d in zip(probs, grads))
            draws = [(p * (d - mean) * scale).astype(BF) for p, d in zip(probs, grads)]
            dq = sum(left_dot(d, k_ref[a:b, hs]) for d, (a, b) in zip(draws, spans))
            put(dq_ref, low, hs, back(dq, low, high))
            for at, (a, b) in enumerate(spans):
                dv = plain_dot(probs[at].astype(BF), g)
                dk = plain_dot(draws[at], q)
                if at == 0:
                    v_sum[a:b, hs] = dv
                    k_sum[a:b, hs] = dk
                else:
                    v_sum[a:b, hs] += dv
                    k_sum[a:b, hs] += dk
        for i in range(length // wide):
            low, high = i * wide, (i + 1) * wide
            put(dk_ref, low, hs, back(k_sum[low:high, hs], low, high))
            put(dv_ref, low, hs, v_sum[low:high, hs])


def attend_back(ring, q, k, v, grad, tables):
    length, cols = q.shape
    return pl.pallas_call(
        functools.partial(attend_back_kernel, length // ring.count, 2 * (length // ring.count)),
        out_shape=(jax.ShapeDtypeStruct((length, cols), BF),) * 3,
        in_specs=[pl.BlockSpec(memory_space=pltpu.SMEM)] + [WHOLE] * 6,
        out_specs=(WHOLE,) * 3,
        scratch_shapes=[pltpu.VMEM((length, cols), F32)] * 2,
        compiler_params=params(48),
        cost_estimate=cost(5 * length * length * cols, 16 * length * cols),
        name="attend_back",
    )(ring.slot_of_block, q, k, v, grad, *tables)


def reorder_dot_kernel(block_rows, places, h_ref, w_ref, out_ref):
    step = pl.program_id(0)
    per_step = h_ref.shape[0] // block_rows
    out = plain_dot(h_ref[...], w_ref[...]).astype(BF)
    for part in range(per_step):
        start = places[step * per_step + part] * block_rows
        rows = pl.ds(pl.multiple_of(start, block_rows), block_rows)
        out_ref[rows, :] = out[part * block_rows : (part + 1) * block_rows]


def reorder_dot(ring, h_all, weight):
    length, width = h_all.shape
    cols = weight.shape[1]
    block_rows = length // ring.count
    step_rows = 2 * block_rows
    return pl.pallas_call(
        functools.partial(reorder_dot_kernel, block_rows),
        out_shape=jax.ShapeDtypeStruct((length, cols), BF),
        grid_spec=pltpu.PrefetchScalarGridSpec(
            num_scalar_prefetch=1,
            grid=(length // step_rows,),
            in_specs=[
                pl.BlockSpec((step_rows, width), lambda i, places: (i, 0)),
                pl.BlockSpec((width, cols), lambda i, places: (0, 0)),
            ],
            out_specs=pl.BlockSpec((length, cols), lambda i, places: (0, 0)),
        ),
        compiler_params=params(40),
        cost_estimate=cost(2 * length * width * cols, 2 * length * width + 2 * width * cols),
        name="reorder_dot",
    )(ring.block_of_slot, h_all, weight)


def gated(gate_pre, up_pre, back, scale):
    sigmoid = 1.0 / (1.0 + jnp.exp(-gate_pre))
    silu = gate_pre * sigmoid
    hidden = silu * up_pre
    scaled = scale * back
    grad_gate = scaled * up_pre * sigmoid * (1.0 + gate_pre * (1.0 - sigmoid))
    return hidden, scale * hidden, grad_gate, scaled * silu


def expert_kernel(h_ref, wa_ref, wb_ref, back_ref, gate_ref, hid_ref, da_ref, db_ref, sum_ref):
    wide = wa_ref.shape[1]
    rows_at_once = 256
    weights = jnp.concatenate([wa_ref[...], wb_ref[...]], 1)

    @pl.when(pl.program_id(0) == 0)
    def _():
        sum_ref[...] = jnp.zeros_like(sum_ref)

    for start in range(0, h_ref.shape[0], rows_at_once):
        rows = slice(start, start + rows_at_once)
        both = plain_dot(h_ref[rows], weights)
        back = back_ref[rows].astype(F32)
        hidden, scaled, da, db = gated(both[:, :wide], both[:, wide:], back, gate_ref[rows])
        sum_ref[rows] += hidden * back
        hid_ref[rows] = scaled.astype(BF)
        da_ref[rows] = da.astype(BF)
        db_ref[rows] = db.astype(BF)


def expert_units(h_all, weight_in, back, gate):
    length, width = h_all.shape
    units = back.shape[1]
    wide = 128
    tiles = units // wide
    tile = pl.BlockSpec((length, wide), lambda j: (0, j))
    shape = jax.ShapeDtypeStruct((length, units), BF)
    return pl.pallas_call(
        expert_kernel,
        out_shape=(shape,) * 3 + (jax.ShapeDtypeStruct((length, wide), F32),),
        grid=(tiles,),
        in_specs=[
            pl.BlockSpec((length, width), lambda j: (0, 0)),
            pl.BlockSpec((width, wide), lambda j: (0, j)),
            pl.BlockSpec((width, wide), lambda j: (0, j + tiles)),
            tile,
            pl.BlockSpec((length, 1), lambda j: (0, 0)),
        ],
        out_specs=(tile,) * 3 + (pl.BlockSpec((length, wide), lambda j: (0, 0)),),
        compiler_params=params(48),
        cost_estimate=cost(
            4 * length * width * units, 2 * length * width + 4 * width * units + 8 * length * units
        ),
        name="expert_units",
    )(h_all, weight_in, weight_in, back, gate)


def shared_kernel(h_ref, wg_ref, wu_ref, back_ref, scale_ref, hid_ref, dg_ref, du_ref, sum_ref):
    h = h_ref[...]
    back = back_ref[...].astype(F32)
    hidden, scaled, dg, du = gated(
        plain_dot(h, wg_ref[...]), plain_dot(h, wu_ref[...]), back, scale_ref[...]
    )
    sum_ref[...] = jnp.sum(hidden * back, 1, keepdims=True)
    hid_ref[...] = scaled.astype(BF)
    dg_ref[...] = dg.astype(BF)
    du_ref[...] = du.astype(BF)


def shared_units(h_all, weight_gate, weight_up, back, scale):
    length, width = h_all.shape
    units = back.shape[1]
    rows = 256
    tile = pl.BlockSpec((rows, units), lambda i: (i, 0))
    column = pl.BlockSpec((rows, 1), lambda i: (i, 0))
    weight = pl.BlockSpec((width, units), lambda i: (0, 0))
    shape = jax.ShapeDtypeStruct((length, units), BF)
    return pl.pallas_call(
        shared_kernel,
        out_shape=(shape,) * 3 + (jax.ShapeDtypeStruct((length, 1), F32),),
        grid=(length // rows,),
        in_specs=[pl.BlockSpec((rows, width), lambda i: (i, 0)), weight, weight, tile, column],
        out_specs=(tile,) * 3 + (column,),
        compiler_params=params(48),
        cost_estimate=cost(
            4 * length * width * units, 2 * length * width + 4 * width * units + 8 * length * units
        ),
        name="shared_units",
    )(h_all, weight_gate, weight_up, back, scale)


def shards(
    tokens,
    attention_gain,
    query_weight,
    query_bias,
    key_weight,
    key_bias,
    value_weight,
    value_bias,
    output_weight,
    feedforward_gain,
    shared_gate_weight,
    shared_up_weight,
    shared_down_weight,
    shared_switch,
    router_weight,
    expert_in,
    expert_out,
    routes,
    cotangent,
):
    tok_rows, model_width = tokens.shape
    groups = lax.axis_size("expert")
    me = lax.axis_index("expert")
    ring = Ring(groups)
    length = tok_rows * groups
    experts = router_weight.shape[1]
    weight_in = expert_in[0]
    weight_out = expert_out[0]
    tables = rope_tables(length)
    x_float = tokens.astype(F32)
    rms_attn = rms_scale(x_float)
    unit_attn = x_float * rms_attn
    gain_attn = attention_gain.astype(F32)
    h_attn = (unit_attn * gain_attn).astype(BF)
    h_attn_all = ring.gather(h_attn)
    lanes = jnp.arange(128, dtype=jnp.int32)
    picked = jnp.sum((routes[:, :, None] == lanes[None, None, :]).astype(F32), 1)
    picked_all = ring.gather(picked.astype(BF))
    late_cotangent, h_attn_all = lax.optimization_barrier((cotangent, h_attn_all))
    cotangent_all = ring.gather(late_cotangent)

    q_rot, k_rot, v_low = project(
        ring,
        h_attn_all,
        (query_weight, key_weight, value_weight),
        (query_bias, key_bias, value_bias),
        tables,
    )
    att_low = attend(ring, q_rot, k_rot, v_low)
    attention_own = ring.scatter_sum(right_dot(att_low, output_weight).astype(BF))
    residual = x_float + attention_own
    rms_ffn = rms_scale(residual)
    unit_ffn = residual * rms_ffn
    gain_ffn = feedforward_gain.astype(F32)
    h_ffn = (unit_ffn * gain_ffn).astype(BF)
    h_ffn_all = ring.gather(h_ffn)

    back_shared = plain_dot(cotangent_all, shared_down_weight).astype(BF)
    back_expert = plain_dot(cotangent_all, weight_out).astype(BF)

    def route(rows):
        switch = jax.nn.sigmoid(plain_dot(rows, shared_switch))
        logits = plain_dot(rows, router_weight)
        raised = jnp.exp(logits - jnp.max(logits, -1, keepdims=True))
        return switch, raised / jnp.sum(raised, -1, keepdims=True)

    switch_all, probs_all = route(h_ffn_all)
    mine = (lanes == me).astype(F32)
    picked_here = jnp.sum(picked_all.astype(F32) * mine, 1, keepdims=True)
    gate_here = jnp.sum(probs_all * mine[:experts], 1, keepdims=True) * picked_here
    expert_hidden, grad_gate_e, grad_up_e, gate_sums = expert_units(
        h_ffn_all, weight_in, back_expert, gate_here
    )
    shared_hidden, grad_gate_s, grad_up_s, switch_sums = shared_units(
        h_ffn_all, shared_gate_weight, shared_up_weight, back_shared, switch_all[:, None]
    )
    gate_sums = jnp.sum(gate_sums, 1, keepdims=True) * picked_here
    small = gate_sums * mine + switch_sums * (lanes == experts).astype(F32)
    small = ring.scatter_sum(small, F32)

    grad_ffn_part = (
        right_dot(grad_gate_s, shared_gate_weight)
        + right_dot(grad_up_s, shared_up_weight)
        + right_dot(jnp.concatenate([grad_gate_e, grad_up_e], 1), weight_in)
    ).astype(BF)
    grad_ffn = ring.scatter_sum(grad_ffn_part)

    switch, router_probs = route(h_ffn)
    grad_probs = small[:, :experts]
    grad_logits = router_probs * (
        grad_probs - jnp.sum(router_probs * grad_probs, -1, keepdims=True)
    )
    grad_switch = small[:, experts] * switch * (1.0 - switch)
    h_float = h_ffn.astype(F32)
    grad_ffn = grad_ffn + jnp.dot(grad_logits, router_weight.astype(F32).T, precision=HIGHEST)
    grad_ffn = grad_ffn + grad_switch[:, None] * shared_switch.astype(F32)
    grad_router_part = jnp.dot(grad_logits.T, h_float, precision=HIGHEST)
    grad_switch_row = jnp.dot(grad_switch, h_float, precision=HIGHEST)
    grad_ffn_gain_part = jnp.sum(grad_ffn * unit_ffn, 0)
    early = jnp.concatenate(
        [grad_router_part, grad_switch_row[None], grad_ffn_gain_part[None]], 0
    )
    early = cube_sum(cube_sum(early, "expert"), "dp")

    grad_out = cotangent.astype(F32)
    grad_unit_ffn = grad_ffn * gain_ffn
    grad_residual = grad_out + rms_ffn * (
        grad_unit_ffn - unit_ffn * jnp.mean(grad_unit_ffn * unit_ffn, -1, keepdims=True)
    )
    attention_grad = grad_residual.astype(BF)
    attention_grad_all = ring.gather(attention_grad)

    layer_part = (
        right_dot(shared_hidden, shared_down_weight) + right_dot(expert_hidden, weight_out)
    ).astype(BF)
    layer_part, attention_grad_all = lax.optimization_barrier((layer_part, attention_grad_all))
    layer_out = (residual + ring.scatter_sum(layer_part)).astype(BF)

    grad_att = reorder_dot(ring, attention_grad_all, output_weight)
    grad_query, grad_key, grad_value = attend_back(ring, q_rot, k_rot, v_low, grad_att, tables)
    grad_attn_part = (
        right_dot(grad_query, query_weight)
        + right_dot(grad_key, key_weight)
        + right_dot(grad_value, value_weight)
    )
    grad_gain_part = jnp.sum(grad_attn_part * h_attn_all.astype(F32), 0) / gain_attn
    grad_attention_gain = cube_sum(
        cube_sum(grad_gain_part.reshape(-1, 128), "expert"), "dp"
    ).reshape(-1)
    grad_attn_in = ring.scatter_sum(grad_attn_part.astype(BF))
    grad_unit_attn = grad_attn_in * gain_attn
    grad_tokens = grad_residual + rms_attn * (
        grad_unit_attn - unit_attn * jnp.mean(grad_unit_attn * unit_attn, -1, keepdims=True)
    )
    biases = jnp.stack(
        [
            jnp.sum(grad_query.astype(F32), 0),
            jnp.sum(grad_key.astype(F32), 0),
            jnp.sum(grad_value.astype(F32), 0),
        ]
    )
    biases = cube_sum(biases, "dp")
    h_attn_split = split_cores(h_attn_all)
    h_ffn_split = split_cores(h_ffn_all)
    cotangent_split = split_cores(cotangent_all)
    return (
        layer_out,
        grad_tokens,
        grad_attention_gain,
        pair_sum(h_attn_split, grad_query),
        biases[0],
        pair_sum(h_attn_split, grad_key),
        biases[1],
        pair_sum(h_attn_split, grad_value),
        biases[2],
        pair_sum(split_cores(attention_grad_all), att_low),
        early[experts + 1],
        pair_sum(h_ffn_split, grad_gate_s),
        pair_sum(h_ffn_split, grad_up_s),
        pair_sum(cotangent_split, shared_hidden),
        early[experts],
        early[:experts].T,
        jnp.concatenate(
            [pair_sum(h_ffn_split, grad_gate_e), pair_sum(h_ffn_split, grad_up_e)], 1
        )[None],
        pair_sum(cotangent_split, expert_hidden)[None],
    )


def solution(mesh):
    return jax.shard_map(
        shards,
        mesh=mesh,
        in_specs=(
            P(("dp", "expert"), None),
            P(),
            P(None, "expert"),
            P("expert"),
            P(None, "expert"),
            P("expert"),
            P(None, "expert"),
            P("expert"),
            P(None, "expert"),
            P(),
            P(None, "expert"),
            P(None, "expert"),
            P(None, "expert"),
            P(),
            P(),
            P("expert", None, None),
            P("expert", None, None),
            P(("dp", "expert"), None),
            P(("dp", "expert"), None),
        ),
        out_specs=(
            P(("dp", "expert"), None),
            P(("dp", "expert"), None),
            P(),
            P("dp", "expert"),
            P("expert"),
            P("dp", "expert"),
            P("expert"),
            P("dp", "expert"),
            P("expert"),
            P("dp", "expert"),
            P(),
            P("dp", "expert"),
            P("dp", "expert"),
            P("dp", "expert"),
            P(),
            P(),
            P("expert", "dp", None),
            P("expert", "dp", None),
        ),
        check_vma=False,
    )
```

```python
import functools

import jax
import jax.numpy as jnp
from jax import lax
from jax.experimental import pallas as pl
from jax.experimental.pallas import tpu as pltpu
from jax.sharding import PartitionSpec as P

HD = 128
EPSILON = 1e-06
THETA = 1000000.0
HIGHEST = lax.Precision.HIGHEST
BF = jnp.bfloat16
F32 = jnp.float32


def rope_tables(length):
    middle = HD // 2
    inverse = THETA ** (-(jnp.arange(middle, dtype=F32) * 2.0 / HD))
    angles = jnp.arange(length, dtype=F32)[:, None] * inverse[None, :]
    sine = jnp.sin(angles)
    return (jnp.concatenate([jnp.cos(angles)] * 2, -1), jnp.concatenate([-sine, sine], -1))


def rms_scale(values):
    return lax.rsqrt(jnp.mean(values * values, -1, keepdims=True) + EPSILON)


def plain_dot(left_side, right_side):
    return jnp.dot(left_side, right_side, preferred_element_type=F32)


def right_dot(left_side, right_side):
    return lax.dot_general(
        left_side, right_side, (((1,), (1,)), ((), ())), preferred_element_type=F32
    )


def left_dot(left_side, right_side):
    return lax.dot_general(
        left_side, right_side, (((0,), (0,)), ((), ())), preferred_element_type=F32
    )


def ring_order(count):
    wide = 2 if count <= 8 else 4
    tall = count // wide
    order = [z * wide for z in range(tall)]
    for z in range(tall - 1, -1, -1):
        row = list(range(1, wide))
        if (tall - 1 - z) % 2:
            row = row[::-1]
        order += [z * wide + x for x in row]
    return order


class Ring:
    def __init__(self, count):
        self.count = count
        self.half = count // 2
        place = lax.axis_index("dp").astype(jnp.int32)
        self.core = jnp.stack([place % 2, place // 2])
        order = ring_order(count)
        self.forward = [(order[i], order[(i + 1) % count]) for i in range(count)]
        self.backward = [(order[i], order[(i - 1) % count]) for i in range(count)]
        place = [0] * count
        for at, device in enumerate(order):
            place[device] = at
        distances = []
        for step in range(1, self.half):
            distances += [-step, step]
        distances += [0, self.half]
        here = jnp.array(place, jnp.int32)[lax.axis_index("expert")]
        around = (here + jnp.array(distances, jnp.int32) + count) % count
        self.block_of_slot = jnp.array(order, jnp.int32)[around]
        hits = self.block_of_slot[None, :] == jnp.arange(count, dtype=jnp.int32)[:, None]
        self.slot_of_block = jnp.sum(hits * jnp.arange(count, dtype=jnp.int32)[None, :], 1)

    def slot(self, distance):
        if distance in (0, self.half):
            return self.count - 2 + (distance > 0)
        return 2 * abs(distance) - 2 + (distance > 0)


def after(values, *others):
    return lax.optimization_barrier((values, others))[0]


def move(ring, rounds, *others):
    up, down = zip(*[each.outgoing() for each in rounds])
    rows = [piece.shape[0] for piece in up]
    if len(rounds) > 1:
        up, down = jnp.concatenate(up, 0), jnp.concatenate(down, 0)
    else:
        up, down = up[0], down[0]
    up, down = after((up, down), *others)
    ahead = lax.ppermute(up, "expert", ring.forward)
    behind = lax.ppermute(down, "expert", ring.backward)
    at = 0
    for each, count in zip(rounds, rows):
        if len(rounds) > 1:
            each.arrive(ahead[at : at + count], behind[at : at + count])
        else:
            each.arrive(ahead, behind)
        at += count
    return (ahead, behind)


class Gather:
    def __init__(self, ring, block):
        self.ring = ring
        self.pieces = [block]
        self.ahead = self.behind = block
        self.at = 0

    def outgoing(self):
        self.at += 1
        if self.at < self.ring.half:
            return self.ahead, self.behind
        middle = self.pieces[0].shape[0] // 2
        return self.ahead[:middle], self.behind[middle:]

    def arrive(self, ahead, behind):
        self.ahead, self.behind = ahead, behind
        self.pieces += [ahead, behind]

    def step(self, *others):
        return move(self.ring, [self], *others)

    def chunk(self, which):
        if which < self.ring.half - 1:
            return self.pieces[2 * which + 1 : 2 * which + 3]
        return [self.pieces[0]] + self.pieces[-2:]

    def rest(self):
        while self.at < self.ring.half:
            self.step()
        return self.pieces[1:-2] + [self.pieces[0]] + self.pieces[-2:]


class Scatter:
    def __init__(self, ring, chunks, rows):
        self.ring = ring
        self.chunks = chunks
        self.rows = rows
        self.at = ring.half

    def own(self, distance):
        slot = self.ring.slot(distance)
        slots = self.ring.count // len(self.chunks)
        start = slot % slots * self.rows
        return self.chunks[slot // slots][start : start + self.rows]

    def outgoing(self):
        middle = self.rows // 2
        at = self.at
        self.at -= 1
        if at == self.ring.half:
            far = self.own(at)
            return far[:middle], far[middle:]
        up = self.own(at).astype(F32)
        down = self.own(-at).astype(F32)
        if at == self.ring.half - 1:
            up = jnp.concatenate([up[:middle] + self.ahead.astype(F32), up[middle:]], 0)
            down = jnp.concatenate([down[:middle], down[middle:] + self.behind.astype(F32)], 0)
        else:
            up = up + self.ahead.astype(F32)
            down = down + self.behind.astype(F32)
        return up.astype(BF), down.astype(BF)

    def arrive(self, ahead, behind):
        self.ahead, self.behind = ahead, behind

    def step(self, *others):
        return move(self.ring, [self], *others)

    def rest(self, *others):
        while self.at:
            self.step()
        return after(self.own(0), *others).astype(F32) + self.ahead.astype(F32) + self.behind.astype(F32)


def cube_steps(axis):
    count = lax.axis_size(axis)
    step, moves = 1, []
    while step < count:
        moves.append((axis, [(i, i ^ step) for i in range(count)]))
        step *= 2
    return moves


class PairSum:
    def __init__(self, splits, rights):
        self.splits = splits
        self.rights = rights
        self.tall = len(splits[0]) - 1

    def lefts(self, which, *others):
        return after([split[which] for split in self.splits], *others)

    def cores(self, *others, time=0):
        count = lax.axis_size("dp")
        (sent,) = pair_dot(self.lefts(0, *others), self.rights, [], BF, 1, time)
        self.arrived = lax.ppermute(sent, "dp", [(i, i ^ 1) for i in range(count)])
        return sent

    def chips(self, *others, time=0):
        count = lax.axis_size("dp")
        size = self.splits[0][1].shape[1]
        self.parts = []
        out = others
        for step in range(1, self.tall):
            adds = [(self.arrived, step * size)]
            (out,) = pair_dot(self.lefts(1 + step, *others), self.rights, adds, BF, 1, time)
            moves = [(i, (i // 2 + step) % self.tall * 2 + i % 2) for i in range(count)]
            self.parts.append(lax.ppermute(out, "dp", moves))
        return out

    def total(self, *others, time=0, outs=1, turned_rows=0):
        adds = [(self.arrived, 0)] + [(part, 0) for part in self.parts]
        lefts = self.lefts(1, *others)
        return pair_dot(lefts, self.rights, adds, F32, outs, time, turned_rows)


WHOLE = pl.BlockSpec(memory_space=pltpu.VMEM)
ANY = pl.BlockSpec(memory_space=pl.ANY)
SCALARS = pl.BlockSpec(memory_space=pltpu.SMEM)


class Copies:
    def __init__(self, sems):
        self.sems = sems
        self.count = 0

    def start(self, source, target):
        copy = pltpu.make_async_copy(source, target, self.sems.at[self.count])
        self.count += 1
        copy.start()
        return copy


def tiles_of(columns, wide):
    return [(low, min(low + wide, columns)) for low in range(0, columns, wide)]


def bring(copies, pieces, rows_ref):
    at, started = 0, []
    for piece in pieces:
        rows = slice(at, at + piece.shape[0])
        started.append(copies.start(piece, rows_ref.at[rows]))
        at += piece.shape[0]
    return started


def chunks_of(pieces, brought, wide):
    at, left = 0, list(zip(pieces, brought))
    for low in range(0, sum(piece.shape[0] for piece in pieces), wide):
        waits = []
        while left and at < low + wide:
            piece, copy = left.pop(0)
            at += piece.shape[0]
            waits.append(copy)
        yield slice(low, low + wide), waits


def params(mebibytes):
    return pltpu.CompilerParams(vmem_limit_bytes=mebibytes * 1024 * 1024)


def cost(time):
    return pl.CostEstimate(flops=int(1e9 * time) + 1, bytes_accessed=1, transcendentals=0)


def split_shapes(rows, width):
    count = lax.axis_size("dp")
    widths = [width // 2] + [width // count] * (count // 2)
    return tuple(jax.ShapeDtypeStruct((rows, w), BF) for w in widths)


def put_split(place, row_ref, refs, rows=slice(None)):
    core, far = place[0], place[1]
    other_ref, own_refs = refs[0], refs[1:]
    columns, tall = own_refs[0].shape[1], len(own_refs)
    for part in range(tall):
        chip = lax.rem(far + part, tall)
        at = pl.multiple_of((2 * chip + 1 - core) * columns, columns)
        there = slice(part * columns, (part + 1) * columns)
        other_ref[rows, there] = row_ref[rows, pl.ds(at, columns)]
        at = pl.multiple_of((2 * chip + core) * columns, columns)
        own_refs[part][rows, :] = row_ref[rows, pl.ds(at, columns)]


def turned(values, cosine, sine):
    return values * cosine + pltpu.roll(values, HD // 2, 1) * sine


def project_kernel(pieces, splits, places, place, *refs):
    parts, refs = refs[:pieces], refs[pieces:]
    hbm, refs = refs[:8], refs[8:]
    outs, refs = refs[:3], refs[3:]
    split_hbm, refs = refs[: splits + 1], refs[splits + 1 :]
    q_ref, k_ref, v_ref = outs
    h_ref, refs = refs[0], refs[1:]
    split_ref, refs = refs[:splits], refs[splits:]
    w_ref, bq, bk, bv, cos, sin, sems = refs
    cols = bq.shape[1]
    copies = Copies(sems)
    targets = [w_ref.at[:, at * cols : (at + 1) * cols] for at in range(3)]
    of_weights = [copies.start(a, b) for a, b in zip(hbm, targets + [bq, bk, bv, cos, sin])]
    brought = bring(copies, parts, h_ref)
    block_rows = h_ref.shape[0] // places.shape[0]
    for copy in of_weights:
        copy.wait()
    kept = []
    sources = [h_ref] + list(split_ref)
    targets = [split_hbm[-1]] + list(split_hbm[:-1])
    for chunk, waits in chunks_of(parts, brought, 2 * block_rows):
        for copy in waits:
            copy.wait()
        put_split(place, h_ref, split_ref, chunk)
        kept += [copies.start(a.at[chunk], b.at[chunk]) for a, b in zip(sources, targets)]
        qkv = plain_dot(h_ref[chunk], w_ref[...])
        q = qkv[:, :cols] + bq[...].astype(F32)
        k = qkv[:, cols : 2 * cols] + bk[...].astype(F32)
        v = qkv[:, 2 * cols :] + bv[...].astype(F32)
        for part in range(2):
            start = places[chunk.start // block_rows + part] * block_rows
            rows = pl.ds(pl.multiple_of(start, block_rows), block_rows)
            near = slice(part * block_rows, (part + 1) * block_rows)
            cosine, sine = cos[rows, :], sin[rows, :]
            for head in range(cols // HD):
                hs = slice(head * HD, (head + 1) * HD)
                q_ref[rows, hs] = turned(q[near, hs], cosine, sine).astype(BF)
                k_ref[rows, hs] = turned(k[near, hs], cosine, sine).astype(BF)
            v_ref[rows, :] = v[near].astype(BF)
    for copy in kept:
        copy.wait()


def project(ring, parts, weights, biases, tables, time=3):
    width, cols = weights[0].shape
    length = sum(part.shape[0] for part in parts)
    shape = jax.ShapeDtypeStruct((length, cols), BF)
    split = split_shapes(length, width)
    pieces = len(parts)
    return pl.pallas_call(
        functools.partial(project_kernel, pieces, len(split)),
        out_shape=(shape,) * 3 + split + (jax.ShapeDtypeStruct((length, width), BF),),
        in_specs=[SCALARS] * 2 + [ANY] * (pieces + 8),
        out_specs=(WHOLE,) * 3 + (ANY,) * (len(split) + 1),
        scratch_shapes=[pltpu.VMEM((length, width), BF)]
        + [pltpu.VMEM(part.shape, BF) for part in split]
        + [pltpu.VMEM((width, 3 * cols), BF)]
        + [pltpu.VMEM((1, cols), BF)] * 3
        + [pltpu.VMEM((length, HD), F32)] * 2
        + [pltpu.SemaphoreType.DMA((pieces + 8 + ring.half * (len(split) + 1),))],
        compiler_params=params(52),
        cost_estimate=cost(time),
        name="project",
    )(ring.block_of_slot, ring.core, *parts, *weights, *[b[None] for b in biases], *tables)


def bring_all(sources, targets, sems):
    copies = Copies(sems)
    for copy in [copies.start(source, target) for source, target in zip(sources, targets)]:
        copy.wait()


def attend_kernel(
    block_rows, wide, slots, q_hbm, k_hbm, v_hbm, out_ref, q_ref, k_ref, v_ref, sems
):
    bring_all((q_hbm, k_hbm, v_hbm), (q_ref, k_ref, v_ref), sems)
    length, cols = q_ref.shape
    scale = HD ** (-0.5)
    at_row = lax.broadcasted_iota(jnp.int32, (wide, wide), 0)
    at_col = lax.broadcasted_iota(jnp.int32, (wide, wide), 1)
    allowed = at_col <= at_row
    for head in range(cols // HD):
        hs = slice(head * HD, (head + 1) * HD)
        for i in range(length // wide):
            low, high = i * wide, (i + 1) * wide
            q = q_ref[low:high, hs]
            near = right_dot(q, k_ref[low:high, hs]) * scale
            near = jnp.where(allowed, near, -jnp.inf)
            peak = jnp.max(near, 1, keepdims=True)
            if i:
                past = right_dot(q, k_ref[:low, hs]) * scale
                peak = jnp.maximum(peak, jnp.max(past, 1, keepdims=True))
                past = jnp.exp(past - peak)
            near = jnp.exp(near - peak)
            total = jnp.sum(near, 1, keepdims=True)
            if i:
                total = total + jnp.sum(past, 1, keepdims=True)
            share = 1.0 / total
            out = plain_dot((near * share).astype(BF), v_ref[low:high, hs])
            if i:
                out = out + plain_dot((past * share).astype(BF), v_ref[:low, hs])
            out = out.astype(BF)
            for part in range(wide // block_rows):
                slot = slots[i * (wide // block_rows) + part]
                rows = pl.ds(pl.multiple_of(slot * block_rows, block_rows), block_rows)
                out_ref[rows, hs] = out[part * block_rows : (part + 1) * block_rows]


def attend(ring, q, k, v, time=3):
    length, cols = q.shape
    return pl.pallas_call(
        functools.partial(attend_kernel, length // ring.count, 2 * (length // ring.count)),
        out_shape=jax.ShapeDtypeStruct((length, cols), BF),
        in_specs=[SCALARS] + [ANY] * 3,
        out_specs=WHOLE,
        scratch_shapes=[pltpu.VMEM((length, cols), BF)] * 3 + [pltpu.SemaphoreType.DMA((3,))],
        compiler_params=params(40),
        cost_estimate=cost(time),
        name="attend",
    )(ring.slot_of_block, q, k, v)


def attend_back_kernel(
    block_rows, wide, slots, q_hbm, k_hbm, v_hbm, g_hbm, cos_hbm, sin_hbm, out_ref, bias_ref,
    q_ref, k_ref, v_ref, g_ref, cos, sin, k_sum, v_sum, sems,
):
    sources = (q_hbm, k_hbm, v_hbm, g_hbm, cos_hbm, sin_hbm)
    bring_all(sources, (q_ref, k_ref, v_ref, g_ref, cos, sin), sems)
    length, cols = q_ref.shape
    scale = HD ** (-0.5)
    at_key = lax.broadcasted_iota(jnp.int32, (wide, wide), 0)
    at_query = lax.broadcasted_iota(jnp.int32, (wide, wide), 1)
    allowed = at_key <= at_query
    per = wide // block_rows
    bias_ref[...] = jnp.zeros_like(bias_ref)

    def put(which, low, head, values):
        hs = slice(which * cols + head * HD, which * cols + (head + 1) * HD)
        values = values.astype(BF)
        bias_ref[:, hs] += jnp.sum(values.astype(F32), 0, keepdims=True)
        for part in range(per):
            slot = slots[low // block_rows + part]
            rows = pl.ds(pl.multiple_of(slot * block_rows, block_rows), block_rows)
            out_ref[rows, hs] = values[part * block_rows : (part + 1) * block_rows]

    def back(values, low, high):
        return values * cos[low:high] - pltpu.roll(values, HD // 2, 1) * sin[low:high]

    for head in range(cols // HD):
        hs = slice(head * HD, (head + 1) * HD)
        for i in range(length // wide):
            low, high = i * wide, (i + 1) * wide
            q = q_ref[low:high, hs]
            g = g_ref[low:high, hs]
            spans = [(low, high)] + ([(0, low)] if i else [])
            scores = [right_dot(k_ref[a:b, hs], q) * scale for a, b in spans]
            scores[0] = jnp.where(allowed, scores[0], -jnp.inf)
            peak = functools.reduce(jnp.maximum, [jnp.max(s, 0, keepdims=True) for s in scores])
            probs = [jnp.exp(s - peak) for s in scores]
            total = sum(jnp.sum(p, 0, keepdims=True) for p in probs)
            share = 1.0 / total
            probs = [p * share for p in probs]
            grads = [right_dot(v_ref[a:b, hs], g) for a, b in spans]
            mean = sum(jnp.sum(p * d, 0, keepdims=True) for p, d in zip(probs, grads))
            draws = [(p * (d - mean) * scale).astype(BF) for p, d in zip(probs, grads)]
            dq = sum(left_dot(d, k_ref[a:b, hs]) for d, (a, b) in zip(draws, spans))
            put(0, low, head, back(dq, low, high))
            for at, (a, b) in enumerate(spans):
                dv = plain_dot(probs[at].astype(BF), g)
                dk = plain_dot(draws[at], q)
                if at == 0:
                    v_sum[a:b, hs] = dv
                    k_sum[a:b, hs] = dk
                else:
                    v_sum[a:b, hs] += dv
                    k_sum[a:b, hs] += dk
        for i in range(length // wide):
            low, high = i * wide, (i + 1) * wide
            put(1, low, head, back(k_sum[low:high, hs], low, high))
            put(2, low, head, v_sum[low:high, hs])


def attend_back(ring, q, k, v, grad, tables, time=20):
    length, cols = q.shape
    return pl.pallas_call(
        functools.partial(attend_back_kernel, length // ring.count, 2 * (length // ring.count)),
        out_shape=(
            jax.ShapeDtypeStruct((length, 3 * cols), BF),
            jax.ShapeDtypeStruct((1, 3 * cols), F32),
        ),
        in_specs=[SCALARS] + [ANY] * 6,
        out_specs=(WHOLE,) * 2,
        scratch_shapes=[pltpu.VMEM((length, cols), BF)] * 4
        + [pltpu.VMEM((length, HD), F32)] * 2
        + [pltpu.VMEM((length, cols), F32)] * 2
        + [pltpu.SemaphoreType.DMA((6,))],
        compiler_params=params(48),
        cost_estimate=cost(time),
        name="attend_back",
    )(ring.slot_of_block, q, k, v, grad, *tables)


def attend_in_kernel(
    d_hbm, wq_hbm, wk_hbm, wv_hbm, h_hbm, gain_ref, out_hbm, gain_out,
    d_ref, wq_ref, wk_ref, wv_ref, h_ref, out_ref, sems,
):
    cols = wq_ref.shape[1]
    copies = Copies(sems)
    of_d = copies.start(d_hbm, d_ref)
    tiles = tiles_of(h_ref.shape[1], 512)
    weights = ((wq_hbm, wq_ref), (wk_hbm, wk_ref), (wv_hbm, wv_ref))
    of_tiles = [
        [copies.start(a.at[low:high], b.at[low:high]) for a, b in weights]
        + [copies.start(h_hbm.at[:, low:high], h_ref.at[:, low:high])]
        for low, high in tiles
    ]
    of_d.wait()
    kept = []
    for started, (low, high) in zip(of_tiles, tiles):
        for copy in started[:-1]:
            copy.wait()
        out = right_dot(d_ref[:, :cols], wq_ref[low:high])
        out = out + right_dot(d_ref[:, cols : 2 * cols], wk_ref[low:high])
        out = out + right_dot(d_ref[:, 2 * cols :], wv_ref[low:high])
        out_ref[:, low:high] = out.astype(BF)
        kept.append(copies.start(out_ref.at[:, low:high], out_hbm.at[:, low:high]))
        started[-1].wait()
        products = out * h_ref[:, low:high].astype(F32)
        gain_out[:, low:high] = jnp.sum(products, 0, keepdims=True) / gain_ref[:, low:high]
    for copy in kept:
        copy.wait()


def attend_in(grads, weights, h_all, gain, time=1):
    length, cols = grads.shape
    width = h_all.shape[1]
    return pl.pallas_call(
        attend_in_kernel,
        out_shape=(
            jax.ShapeDtypeStruct((length, width), BF),
            jax.ShapeDtypeStruct((1, width), F32),
        ),
        in_specs=[ANY] * 5 + [WHOLE],
        out_specs=(ANY, WHOLE),
        scratch_shapes=[pltpu.VMEM((length, cols), BF)]
        + [pltpu.VMEM((width, cols // 3), BF)] * 3
        + [
            pltpu.VMEM((length, width), BF),
            pltpu.VMEM((length, width), BF),
            pltpu.SemaphoreType.DMA((1 + 5 * len(tiles_of(width, 512)),)),
        ],
        compiler_params=params(48),
        cost_estimate=cost(time),
        name="attend_in",
    )(grads, *weights, h_all, gain)


def reorder_dot_kernel(pieces, splits, places, place, *refs):
    parts, refs = refs[:pieces], refs[pieces:]
    w_hbm, out_ref, refs = refs[0], refs[1], refs[2:]
    split_hbm, refs = refs[:splits], refs[splits:]
    h_ref, split_ref, w_ref = refs[0], refs[1 : 1 + splits], refs[1 + splits]
    copies = Copies(refs[-1])
    of_weight = copies.start(w_hbm, w_ref)
    brought = bring(copies, parts, h_ref)
    block_rows = h_ref.shape[0] // places.shape[0]
    of_weight.wait()
    kept = []
    for chunk, waits in chunks_of(parts, brought, 2 * block_rows):
        for copy in waits:
            copy.wait()
        put_split(place, h_ref, split_ref, chunk)
        kept += [copies.start(a.at[chunk], b.at[chunk]) for a, b in zip(split_ref, split_hbm)]
        out = plain_dot(h_ref[chunk], w_ref[...]).astype(BF)
        for part in range(2):
            start = places[chunk.start // block_rows + part] * block_rows
            rows = pl.ds(pl.multiple_of(start, block_rows), block_rows)
            out_ref[rows, :] = out[part * block_rows : (part + 1) * block_rows]
    for copy in kept:
        copy.wait()


def reorder_dot(ring, parts, weight, time=10):
    width, cols = weight.shape
    length = sum(part.shape[0] for part in parts)
    split = split_shapes(length, width)
    pieces = len(parts)
    return pl.pallas_call(
        functools.partial(reorder_dot_kernel, pieces, len(split)),
        out_shape=(jax.ShapeDtypeStruct((length, cols), BF),) + split,
        in_specs=[SCALARS] * 2 + [ANY] * (pieces + 1),
        out_specs=(WHOLE,) + (ANY,) * len(split),
        scratch_shapes=[pltpu.VMEM((length, width), BF)]
        + [pltpu.VMEM(part.shape, BF) for part in split]
        + [
            pltpu.VMEM((width, cols), BF),
            pltpu.SemaphoreType.DMA((pieces + 1 + ring.half * len(split),)),
        ],
        compiler_params=params(52),
        cost_estimate=cost(time),
        name="reorder_dot",
    )(ring.block_of_slot, ring.core, *parts, weight)


def gated(gate_pre, up_pre, back, scale):
    sigmoid = 0.5 + 0.5 * jnp.tanh(0.5 * gate_pre)
    silu = gate_pre * sigmoid
    hidden = silu * up_pre
    scaled = scale * back
    grad_gate = scaled * up_pre * (sigmoid + silu * (1.0 - sigmoid))
    return hidden, scale * hidden, grad_gate, scaled * silu


def back_kernel(pieces, which, split, place, *refs):
    parts, refs = refs[:pieces], refs[pieces:]
    wo_hbm, wd_hbm = refs[:2]
    refs = refs[-(2 * split + 6) :]
    back_e_ref, back_s_ref = refs[:2]
    kept_hbm, kept_ref = refs[2 : 2 + split], refs[2 + split : 2 + 2 * split]
    rows_ref, wo_ref, wd_ref, sems = refs[-4:]
    rows, width = rows_ref.shape
    copies = Copies(sems)
    brought = bring(copies, parts, rows_ref)
    tiles = tiles_of(wo_ref.shape[1], 512)
    of_e = [copies.start(wo_hbm.at[:, a:b], wo_ref.at[:, a:b]) for a, b in tiles]
    of_s = copies.start(wd_hbm, wd_ref)
    for copy in brought:
        copy.wait()
    put_split(place, rows_ref, kept_ref)
    chunk = slice(which * rows, (which + 1) * rows)
    kept = [copies.start(ref, hbm.at[chunk]) for ref, hbm in zip(kept_ref, kept_hbm)]
    for copy, (a, b) in zip(of_e, tiles):
        copy.wait()
        back_e_ref[:, a:b] = plain_dot(rows_ref[...], wo_ref[:, a:b]).astype(BF)
    of_s.wait()
    back_s_ref[...] = right_dot(rows_ref[...], wd_ref[...]).astype(BF)
    for copy in kept:
        copy.wait()


def back_units(ring, which, parts, weight_out, weight_down, kept, time=6):
    width, units = weight_out.shape
    shared = weight_down.shape[0]
    rows = sum(part.shape[0] for part in parts)
    pieces = len(parts)
    first = pieces + 3
    split = split_shapes(rows * ring.half, width)
    return pl.pallas_call(
        functools.partial(back_kernel, pieces, which, len(split)),
        out_shape=(
            jax.ShapeDtypeStruct((rows, units), BF),
            jax.ShapeDtypeStruct((rows, shared), BF),
        )
        + split,
        in_specs=[SCALARS] + [ANY] * (pieces + 2 + len(kept)),
        out_specs=(WHOLE, WHOLE) + (ANY,) * len(split),
        scratch_shapes=[pltpu.VMEM((rows, part.shape[1]), BF) for part in split]
        + [
            pltpu.VMEM((rows, width), BF),
            pltpu.VMEM((width, units), BF),
            pltpu.VMEM((shared, width), BF),
            pltpu.SemaphoreType.DMA((pieces + len(tiles_of(units, 512)) + 1 + len(split),)),
        ],
        input_output_aliases={first + at: 2 + at for at in range(len(kept))},
        compiler_params=params(48),
        cost_estimate=cost(time),
        name="back_units",
    )(ring.core, *parts, weight_out, weight_down, *kept)


UNIT_TILE = 512


def units_kernel(pieces, which, experts, count, me_ref, place, *refs):
    parts, refs = refs[:pieces], refs[pieces:]
    wi_hbm, wg_hbm, wu_hbm, back_e_hbm, back_s_hbm = refs[:5]
    refs = refs[-(2 * count + 9) :]
    small_ref = refs[0]
    kept_hbm, kept_ref = refs[1 : 1 + count], refs[1 + count : 1 + 2 * count]
    hid_e_ref, hid_s_ref, both_ref, both_s_ref = kept_ref[:4]
    h_ref, wi_ref, wg_ref, wu_ref, back_e_ref, back_s_ref, sum_ref, sems = refs[-8:]
    rows = h_ref.shape[0]
    width, units = wi_ref.shape[0], wi_ref.shape[1] // 2
    me = me_ref[0]
    copies = Copies(sems)
    brought = bring(copies, parts, h_ref)
    tiles = tiles_of(units, UNIT_TILE)
    of_e = []
    for a, b in tiles:
        of_e.append(
            (
                copies.start(wi_hbm.at[:, a:b], wi_ref.at[:, 2 * a : a + b]),
                copies.start(wi_hbm.at[:, units + a : units + b], wi_ref.at[:, a + b : 2 * b]),
            )
        )
        if a == 0:
            of_back_e = copies.start(back_e_hbm, back_e_ref)
    of_s = [
        copies.start(wg_hbm, wg_ref),
        copies.start(wu_hbm, wu_ref),
        copies.start(back_s_hbm, back_s_ref),
    ]
    chunk = slice(which * rows, (which + 1) * rows)
    started = []

    def keep(*places):
        for at in places:
            started.append(copies.start(kept_ref[at], kept_hbm[at].at[chunk]))

    def scale_of(low, high):
        aux = h_ref[:, width:].astype(F32)
        lane = lax.broadcasted_iota(jnp.int32, aux.shape, 1)
        return jnp.sum(jnp.where((lane == low) | (lane == high), aux, 0.0), 1, keepdims=True)

    for copy in brought:
        copy.wait()
    put_split(place, h_ref, kept_ref[4:])
    keep(*range(4, count))
    gate = scale_of(me, experts + me)
    h = h_ref[:, :width]
    sum_ref[...] = jnp.zeros_like(sum_ref)
    for which_tile, (a, b) in enumerate(tiles):
        for copy in of_e[which_tile]:
            copy.wait()
        if a == 0:
            of_back_e.wait()
        both = plain_dot(h, wi_ref[:, 2 * a : 2 * b])
        back = back_e_ref[:, a:b].astype(F32)
        hidden, scaled, da, db = gated(both[:, : b - a], both[:, b - a :], back, gate)
        products = hidden * back
        for low in range(0, b - a, 128):
            sum_ref[...] += products[:, low : low + 128]
        hid_e_ref[:, a:b] = scaled.astype(BF)
        both_ref[:, a:b] = da.astype(BF)
        both_ref[:, units + a : units + b] = db.astype(BF)
    keep(0, 2)
    for copy in of_s:
        copy.wait()
    switch = scale_of(2 * experts, 3 * experts)
    back = back_s_ref[...].astype(F32)
    hidden, scaled, dg, du = gated(
        right_dot(h, wg_ref[...]), right_dot(h, wu_ref[...]), back, switch
    )
    hid_s_ref[...] = jnp.zeros_like(hid_s_ref)
    hid_s_ref[:, : scaled.shape[1]] = scaled.astype(BF)
    shared = dg.shape[1]
    both_s_ref[:, :shared] = dg.astype(BF)
    both_s_ref[:, shared:] = du.astype(BF)
    keep(1, 3)
    of_switch = jnp.sum(hidden * back, 1, keepdims=True)
    of_gate = jnp.sum(sum_ref[...], 1, keepdims=True)
    lane = lax.broadcasted_iota(jnp.int32, small_ref.shape, 1)
    small = jnp.zeros(small_ref.shape, F32)
    for value, first in ((of_gate, 0), (of_switch, 2 * experts)):
        high = value.astype(BF).astype(F32)
        small = small + jnp.where(lane == first + me, high, 0.0)
        small = small + jnp.where(lane == first + experts + me, value - high, 0.0)
    small_ref[...] = small.astype(BF)
    for copy in started:
        copy.wait()


def hidden_units(
    ring, which, me, experts, parts, weight_in, weight_gate, weight_up, back_e, back_s, kept,
    time=6,
):
    rows, units = back_e.shape
    shared = back_s.shape[1]
    width = weight_in.shape[0]
    pieces = len(parts)
    first = pieces + 7
    columns = [units, -(-shared // 128) * 128, 2 * units, 2 * shared]
    columns += [part.shape[1] for part in split_shapes(rows, width)]
    copies = pieces + 2 * len(tiles_of(units, UNIT_TILE)) + 4 + len(columns)
    return pl.pallas_call(
        functools.partial(units_kernel, pieces, which, experts, len(columns)),
        out_shape=(jax.ShapeDtypeStruct((rows, 128), BF),)
        + tuple(jax.ShapeDtypeStruct((rows * ring.half, c), BF) for c in columns),
        in_specs=[SCALARS] * 2 + [ANY] * (pieces + 5 + len(kept)),
        out_specs=(WHOLE,) + (ANY,) * len(columns),
        scratch_shapes=[pltpu.VMEM((rows, c), BF) for c in columns]
        + [
            pltpu.VMEM((rows, width + 128), BF),
            pltpu.VMEM((width, 2 * units), BF),
            pltpu.VMEM((shared, width), BF),
            pltpu.VMEM((shared, width), BF),
            pltpu.VMEM((rows, units), BF),
            pltpu.VMEM((rows, shared), BF),
            pltpu.VMEM((rows, 128), F32),
            pltpu.SemaphoreType.DMA((copies,)),
        ],
        input_output_aliases={first + at: 1 + at for at in range(len(kept))},
        compiler_params=params(52),
        cost_estimate=cost(time),
        name="hidden_units",
    )(
        me,
        ring.core,
        *parts,
        weight_in,
        weight_gate,
        weight_up,
        back_e,
        back_s,
        *kept,
    )


IN_TILE = 512


def units_in_kernel(
    which, both_hbm, both_s_hbm, small_ref, wi_hbm, wg_hbm, wu_hbm, out_ref,
    both_ref, both_s_ref, wi_ref, ws_ref, sems,
):
    rows = both_ref.shape[0]
    width, shared = wi_ref.shape[0], ws_ref.shape[0] // 2
    copies = Copies(sems)
    chunk = slice(which * rows, (which + 1) * rows)
    brought = [
        copies.start(both_hbm.at[chunk], both_ref),
        copies.start(both_s_hbm.at[chunk], both_s_ref),
    ]
    tiles = tiles_of(width, IN_TILE)
    weights = [
        [
            copies.start(wi_hbm.at[a:b], wi_ref.at[a:b]),
            copies.start(wg_hbm.at[:, a:b], ws_ref.at[:shared, a:b]),
            copies.start(wu_hbm.at[:, a:b], ws_ref.at[shared:, a:b]),
        ]
        for a, b in tiles
    ]
    out_ref[:, width:] = small_ref[...]
    for copy in brought:
        copy.wait()
    for started, (a, b) in zip(weights, tiles):
        for copy in started:
            copy.wait()
        out = right_dot(both_ref[...], wi_ref[a:b])
        out = out + plain_dot(both_s_ref[...], ws_ref[:, a:b])
        out_ref[:, a:b] = out.astype(BF)


def units_in(which, both, both_s, small, weight_in, weight_gate, weight_up, time):
    joined, joined_s = both.shape[1], both_s.shape[1]
    rows = small.shape[0]
    width = weight_in.shape[0]
    return pl.pallas_call(
        functools.partial(units_in_kernel, which),
        out_shape=jax.ShapeDtypeStruct((rows, width + 128), BF),
        in_specs=[ANY] * 2 + [WHOLE] + [ANY] * 3,
        out_specs=WHOLE,
        scratch_shapes=[
            pltpu.VMEM((rows, joined), BF),
            pltpu.VMEM((rows, joined_s), BF),
            pltpu.VMEM((width, joined), BF),
            pltpu.VMEM((joined_s, width), BF),
            pltpu.SemaphoreType.DMA((2 + 3 * len(tiles_of(width, IN_TILE)),)),
        ],
        compiler_params=params(48),
        cost_estimate=cost(time),
        name="units_in",
    )(both, both_s, small, weight_in, weight_gate, weight_up)


def pair_kernel(pairs, first_rows, outs, turned_rows, *refs):
    adds = len(first_rows)
    lefts_hbm, rights_hbm = refs[:pairs], refs[pairs : 2 * pairs]
    refs = refs[2 * pairs :]
    adds_hbm, outs_hbm = refs[:adds], refs[adds : adds + outs]
    refs = refs[adds + outs :]
    lefts_ref, rights_ref = refs[:pairs], refs[pairs : 2 * pairs]
    refs = refs[2 * pairs :]
    adds_ref, outs_ref = refs[:adds], refs[adds : adds + outs]
    copies = Copies(refs[-1])
    rows = lefts_ref[0].shape[1]
    tiles = pair_tiles([ref.shape[1] for ref in rights_ref], 1 if turned_rows else outs)
    of_lefts = [None] * pairs
    of_tiles = []
    for pair, low, a, b in tiles:
        if of_lefts[pair] is None:
            of_lefts[pair] = copies.start(lefts_hbm[pair], lefts_ref[pair])
        near = slice(a - low, b - low)
        started = [copies.start(rights_hbm[pair].at[:, near], rights_ref[pair].at[:, near])]
        for first, hbm, ref in zip(first_rows, adds_hbm, adds_ref):
            started.append(copies.start(hbm.at[first : first + rows, a:b], ref.at[:, a:b]))
        of_tiles.append(started)
    started = []
    for at, (pair, low, a, b) in enumerate(tiles):
        if of_lefts[pair] is not None:
            of_lefts[pair].wait()
            of_lefts[pair] = None
        for copy in of_tiles[at]:
            copy.wait()
        out = left_dot(lefts_ref[pair][...], rights_ref[pair][:, a - low : b - low])
        for ref in adds_ref:
            out = out + ref[:, a:b].astype(F32)
        if turned_rows:
            out = out.T
            for which, target in enumerate(outs_ref):
                low = which * turned_rows
                first, last = max(a, low), min(b, low + turned_rows)
                if first < last:
                    target[first - low : last - low] = out[first - a : last - a]
            continue
        wide = outs_ref[0].shape[1]
        target, hbm = outs_ref[a // wide], outs_hbm[a // wide]
        near = slice(a % wide, a % wide + b - a)
        target[:, near] = out.astype(target.dtype)
        started.append(copies.start(target.at[:, near], hbm.at[:, near]))
    if turned_rows:
        started = [copies.start(target, hbm) for target, hbm in zip(outs_ref, outs_hbm)]
    for copy in started:
        copy.wait()


def pair_tiles(widths, outs):
    wide = sum(widths) // outs
    tiles, low = [], 0
    for pair, width in enumerate(widths):
        a = low
        while a < low + width:
            b = min(a + 512, low + width, (a // wide + 1) * wide)
            tiles.append((pair, low, a, b))
            a = b
        low += width
    return tiles


def pair_dot(lefts, rights, adds, held, outs=1, time=0, turned_rows=0):
    length, rows = lefts[0].shape
    widths = [right.shape[1] for right in rights]
    columns = sum(widths)
    tiles = len(pair_tiles(widths, 1 if turned_rows else outs))
    pairs = len(lefts)
    shape = (turned_rows, rows) if turned_rows else (rows, columns // outs)
    return pl.pallas_call(
        functools.partial(
            pair_kernel, pairs, [first for _, first in adds], outs, turned_rows
        ),
        out_shape=(jax.ShapeDtypeStruct(shape, held),) * outs,
        in_specs=[ANY] * (2 * pairs + len(adds)),
        out_specs=(ANY,) * outs,
        scratch_shapes=[pltpu.VMEM((length, rows), BF)] * pairs
        + [pltpu.VMEM((length, width), BF) for width in widths]
        + [pltpu.VMEM((rows, columns), BF)] * len(adds)
        + [pltpu.VMEM(shape, held)] * outs
        + [pltpu.SemaphoreType.DMA((pairs + outs + tiles * (2 + len(adds)),))],
        compiler_params=params(52),
        cost_estimate=cost(time),
        name="pair_dot",
    )(*lefts, *rights, *[values for values, _ in adds])


def layer_kernel(low, he_hbm, hs_hbm, wo_hbm, wd_hbm, out_ref, he_ref, hs_ref, wo_ref, wd_ref, sems):
    rows = slice(low, low + he_ref.shape[0])
    copies = Copies(sems)
    brought = [
        copies.start(he_hbm.at[rows], he_ref),
        copies.start(hs_hbm.at[rows], hs_ref),
    ]
    tiles = tiles_of(wo_ref.shape[0], IN_TILE)
    weights = [
        (
            copies.start(wo_hbm.at[a:b], wo_ref.at[a:b]),
            copies.start(wd_hbm.at[:, a:b], wd_ref.at[:, a:b]),
        )
        for a, b in tiles
    ]
    for copy in brought:
        copy.wait()
    for started, (a, b) in zip(weights, tiles):
        for copy in started:
            copy.wait()
        out = right_dot(he_ref[...], wo_ref[a:b]) + plain_dot(hs_ref[:, : wd_ref.shape[0]], wd_ref[:, a:b])
        out_ref[:, a:b] = out.astype(BF)


def layer_part(low, high, hid_e, hid_s, weight_out, weight_down, time):
    width, units = weight_out.shape
    shared = weight_down.shape[0]
    rows = high - low
    return pl.pallas_call(
        functools.partial(layer_kernel, low),
        out_shape=jax.ShapeDtypeStruct((rows, width), BF),
        in_specs=[ANY] * 4,
        out_specs=WHOLE,
        scratch_shapes=[
            pltpu.VMEM((rows, units), BF),
            pltpu.VMEM((rows, hid_s.shape[1]), BF),
            pltpu.VMEM((width, units), BF),
            pltpu.VMEM((shared, width), BF),
            pltpu.SemaphoreType.DMA((2 + 2 * len(tiles_of(width, IN_TILE)),)),
        ],
        compiler_params=params(48),
        cost_estimate=cost(time),
        name="layer_part",
    )(hid_e, hid_s, weight_out, weight_down)


def routing_kernel(
    experts, x_ref, own_ref, ahead_ref, behind_ref, gain_ref, head_ref, picked_ref,
    residual_ref, sent_ref, routing_ref,
):
    width = x_ref.shape[1]
    residual = x_ref[...].astype(F32) + own_ref[...].astype(F32)
    residual = residual + ahead_ref[...].astype(F32) + behind_ref[...].astype(F32)
    h = (residual * rms_scale(residual) * gain_ref[...].astype(F32)).astype(BF)
    scores = right_dot(h, head_ref[...])
    lane = lax.broadcasted_iota(jnp.int32, scores.shape, 1)
    is_expert = lane < experts
    raised = jnp.where(is_expert, scores, -jnp.inf)
    raised = jnp.exp(raised - jnp.max(raised, 1, keepdims=True))
    probs = raised / jnp.sum(raised, 1, keepdims=True)
    switch = jnp.where(lane == 2 * experts, 1.0 / (1.0 + jnp.exp(-scores)), 0.0)
    values = probs * picked_ref[...] + switch
    high = values.astype(BF).astype(F32)
    rest = pltpu.roll(values - high, experts, 1)
    residual_ref[...] = residual
    routing_ref[...] = probs + switch
    sent_ref[:, :width] = h
    sent_ref[:, width:] = (high + rest).astype(BF)


def routing(experts, x, own, ahead, behind, gain, head, picked, time=0):
    rows, width = x.shape
    return pl.pallas_call(
        functools.partial(routing_kernel, experts),
        out_shape=(
            jax.ShapeDtypeStruct((rows, width), F32),
            jax.ShapeDtypeStruct((rows, width + 128), BF),
            jax.ShapeDtypeStruct((rows, 128), F32),
        ),
        in_specs=[WHOLE] * 7,
        out_specs=(WHOLE,) * 3,
        compiler_params=params(40),
        cost_estimate=cost(time),
        name="routing",
    )(x, own, ahead, behind, gain, head, picked)


def shards(
    tokens,
    attention_gain,
    query_weight,
    query_bias,
    key_weight,
    key_bias,
    value_weight,
    value_bias,
    output_weight,
    feedforward_gain,
    shared_gate_weight,
    shared_up_weight,
    shared_down_weight,
    shared_switch,
    router_weight,
    expert_in,
    expert_out,
    routes,
    cotangent,
):
    tok_rows, model_width = tokens.shape
    groups = lax.axis_size("expert")
    me = lax.axis_index("expert").astype(jnp.int32)[None]
    ring = Ring(groups)
    length = tok_rows * groups
    experts = router_weight.shape[1]
    weight_in = expert_in[0]
    weight_out = expert_out[0]
    weight_gate = shared_gate_weight.T
    weight_up = shared_up_weight.T
    weight_down = shared_down_weight.T
    x_float = tokens.astype(F32)
    rms_attn = rms_scale(x_float)
    unit_attn = x_float * rms_attn
    gain_attn = attention_gain.astype(F32)
    h_attn = (unit_attn * gain_attn).astype(BF)

    lanes = jnp.arange(128, dtype=jnp.int32)
    picked = jnp.sum((routes[:, :, None] == lanes).astype(F32), 1)
    head = jnp.concatenate(
        [
            router_weight.T,
            jnp.zeros((experts, model_width), BF),
            shared_switch[None],
            jnp.zeros((127 - 2 * experts, model_width), BF),
        ],
        0,
    )

    gather_attn = Gather(ring, h_attn)
    last = gather_attn.step()
    tables = rope_tables(length)
    last = gather_attn.step(tables, head, picked)
    h_attn_parts = gather_attn.rest()
    gather_cot = Gather(ring, after(cotangent, *gather_attn.pieces[-2:]))
    of_cot = gather_cot.step()

    q_rot, k_rot, v_low, *h_attn_split, h_attn_all = project(
        ring,
        h_attn_parts,
        (query_weight, key_weight, value_weight),
        (query_bias, key_bias, value_bias),
        tables,
    )
    att_low = attend(ring, q_rot, k_rot, v_low)
    sum_att = Scatter(
        ring, [right_dot(after(att_low, of_cot), output_weight).astype(BF)], tok_rows
    )
    backs = []
    cotangent_split = []

    def next_back(*others):
        which = len(backs)
        parts = after(gather_cot.chunk(which), *others)
        new = back_units(ring, which, parts, weight_out, weight_down, cotangent_split)
        cotangent_split[:] = new[2:]
        backs.append(new[:2])
        return new[:2]

    befores = [sum_att.chunks, move(ring, [sum_att, gather_cot])]
    while sum_att.at:
        busy = next_back(befores[-2])
        rounds = [sum_att] + [gather_cot] * (gather_cot.at < ring.half)
        befores.append(move(ring, rounds, busy))
    busy = next_back(befores[-2])

    residual, h_sent, routed = routing(
        experts,
        tokens,
        sum_att.own(0),
        sum_att.ahead,
        after(sum_att.behind, busy),
        feedforward_gain[None],
        head,
        picked,
    )
    gain_ffn = feedforward_gain.astype(F32)

    gather_ffn = Gather(ring, h_sent)
    last = gather_ffn.step()
    busy = ()
    smalls = []
    kept = []

    def next_units(*others):
        which = len(smalls)
        parts = after(gather_ffn.chunk(which), *others)
        small, *new = hidden_units(
            ring,
            which,
            me,
            experts,
            parts,
            weight_in,
            weight_gate,
            weight_up,
            *backs[which],
            kept,
        )
        kept[:] = new
        smalls.append(small)
        return small

    while gather_ffn.at < ring.half:
        last = gather_ffn.step(busy)
        busy = next_units()
    next_units()
    hid_e, hid_s, grad_joined, grad_shared, *h_ffn_split = kept

    def chunk_in(which, time, *others):
        return units_in(
            which,
            *after((grad_joined, grad_shared), *others),
            smalls[which],
            weight_in,
            weight_gate,
            weight_up,
            time,
        )

    out_e = PairSum([cotangent_split], [hid_e])
    out_s = PairSum([cotangent_split], [hid_s])
    in_e = PairSum([h_ffn_split], [grad_joined])
    in_s = PairSum([h_ffn_split], [grad_shared])
    half_rows = length // 2

    def layer_rows(low, time, *others):
        return layer_part(
            low, low + half_rows, *after((hid_e, hid_s), *others), weight_out, weight_down, time
        )

    chunks = [None] * ring.half
    layer_parts = [None, None]
    busy = in_e.cores()
    chunks[-1] = chunk_in(ring.half - 1, 70, busy)
    sum_ffn = Scatter(ring, chunks, tok_rows)
    befores = [chunks[-1], sum_ffn.step()]
    busy = chunks[-1]
    works = [(6, in_e.chips), (6, out_e.cores), (12, out_s.cores)]
    for at, which in enumerate(range(ring.half - 2, -1, -1)):
        time, work = works[at] if at < len(works) else (6, None)
        chunks[which] = chunk_in(which, time, busy, befores[-2])
        busy = chunks[which]
        if work is not None:
            busy = (busy, work(busy))
        befores.append(sum_ffn.step(busy))
    layer_parts[1] = layer_rows(half_rows, 12, befores[-2], busy)
    grad_sum = sum_ffn.rest(layer_parts[1])

    rms_ffn = rms_scale(residual)
    unit_ffn = residual * rms_ffn
    small = grad_sum[:, model_width:]
    router_probs = routed[:, :experts]
    switch = routed[:, 2 * experts]
    grad_probs = picked[:, :experts] * (small[:, :experts] + small[:, experts : 2 * experts])
    grad_logits = router_probs * (
        grad_probs - jnp.sum(router_probs * grad_probs, -1, keepdims=True)
    )
    grad_switch = jnp.sum(small[:, 2 * experts : 4 * experts], 1) * switch * (1.0 - switch)
    h_float = h_sent[:, :model_width].astype(F32)
    grad_ffn = grad_sum[:, :model_width]
    grad_ffn = grad_ffn + jnp.dot(grad_logits, router_weight.astype(F32).T, precision=HIGHEST)
    grad_ffn = grad_ffn + grad_switch[:, None] * shared_switch.astype(F32)
    grad_out = cotangent.astype(F32)
    grad_unit_ffn = grad_ffn * gain_ffn
    grad_residual = grad_out + rms_ffn * (
        grad_unit_ffn - unit_ffn * jnp.mean(grad_unit_ffn * unit_ffn, -1, keepdims=True)
    )
    attention_grad = grad_residual.astype(BF)

    gather_grad = Gather(ring, attention_grad)
    first = gather_grad.step()
    layer_parts[0] = layer_rows(0, 12, attention_grad)
    busy = out_e.chips(layer_parts[0])
    second = gather_grad.step(busy)
    totals = in_e.total(first, busy, time=7.5)
    busy = out_s.chips(totals)
    third = gather_grad.step(busy)
    busy = in_s.cores(second, busy, time=7.5)
    last = gather_grad.step(busy)
    while gather_grad.at < ring.half:
        last = gather_grad.step()
    attention_grad_parts = gather_grad.rest()
    sum_layer = Scatter(ring, layer_parts, tok_rows)
    of_layer = sum_layer.step(last)
    grad_att, *grad_split = reorder_dot(
        ring, after(attention_grad_parts, totals), output_weight
    )
    grads, biases = attend_back(ring, q_rot, k_rot, v_low, grad_att, tables)
    attn_part, gain_part = attend_in(
        after(grads, of_layer),
        (query_weight, key_weight, value_weight),
        h_attn_all,
        gain_attn[None],
    )
    sum_attn = Scatter(ring, [attn_part], tok_rows)
    first = move(ring, [sum_attn, sum_layer])

    grad_router_part = jnp.dot(grad_logits.T, h_float, precision=HIGHEST)
    grad_switch_row = jnp.dot(grad_switch, h_float, precision=HIGHEST)
    grad_ffn_gain_part = jnp.sum(grad_ffn * unit_ffn, 0)
    sums = jnp.concatenate(
        [gain_part, grad_switch_row[None], grad_ffn_gain_part[None], grad_router_part], 0
    )
    in_qkvo = PairSum([h_attn_split, grad_split], [grads, att_low])
    packed = jnp.concatenate([sums.reshape(-1), biases[0]]).reshape(-1, 128)
    for axis, moves in cube_steps("dp"):
        packed = packed + lax.ppermute(packed, axis, moves)
    totals += out_e.total(attn_part, time=6)
    busy = in_qkvo.cores(totals)
    sums = packed.reshape(-1)[: sums.size].reshape(sums.shape)
    rounds = [sum_attn, sum_layer]
    befores = [attn_part, first]
    shared_cols = shared_gate_weight.shape[1]
    while sum_layer.at:
        befores.append(move(ring, rounds, busy))
        if len(befores) == 3:
            busy = in_s.chips(befores[-2], busy, time=6)
            totals += out_s.total(busy, turned_rows=shared_cols)
            busy = totals
        elif len(befores) == 4:
            busy = in_qkvo.chips(befores[-2], totals, time=6)
    last = sum_attn.step()
    totals += in_s.total(befores[-1], busy, time=3, outs=2, turned_rows=shared_cols)
    while sum_attn.at:
        last = sum_attn.step()
    for axis, moves in cube_steps("expert"):
        sums = sums + lax.ppermute(after(sums, last), axis, moves)
    biases = packed.reshape(-1)[sums.size :].reshape(3, -1)

    layer_out = (residual + sum_layer.rest()).astype(BF)
    grad_attn_in = sum_attn.rest()
    grad_unit_attn = grad_attn_in * gain_attn
    grad_tokens = grad_residual + rms_attn * (
        grad_unit_attn - unit_attn * jnp.mean(grad_unit_attn * unit_attn, -1, keepdims=True)
    )
    qkv = in_qkvo.total(last, outs=4)
    return (
        layer_out,
        grad_tokens,
        sums[0],
        qkv[0],
        biases[0],
        qkv[1],
        biases[1],
        qkv[2],
        biases[2],
        qkv[3],
        sums[2],
        totals[3].T,
        totals[4].T,
        totals[2].T,
        sums[1],
        sums[3:].T,
        totals[0][None],
        totals[1][None],
    )


def solution(mesh):
    return jax.shard_map(
        shards,
        mesh=mesh,
        in_specs=(
            P(("dp", "expert"), None),
            P(),
            P(None, "expert"),
            P("expert"),
            P(None, "expert"),
            P("expert"),
            P(None, "expert"),
            P("expert"),
            P(None, "expert"),
            P(),
            P(None, "expert"),
            P(None, "expert"),
            P(None, "expert"),
            P(),
            P(),
            P("expert", None, None),
            P("expert", None, None),
            P(("dp", "expert"), None),
            P(("dp", "expert"), None),
        ),
        out_specs=(
            P(("dp", "expert"), None),
            P(("dp", "expert"), None),
            P(),
            P("dp", "expert"),
            P("expert"),
            P("dp", "expert"),
            P("expert"),
            P("dp", "expert"),
            P("expert"),
            P("dp", "expert"),
            P(),
            P("dp", "expert"),
            P("dp", "expert"),
            P("dp", "expert"),
            P(),
            P(),
            P("expert", "dp", None),
            P("expert", "dp", None),
        ),
        check_vma=False,
    )
```

```python
import functools

import jax
import jax.numpy as jnp
from jax import lax
from jax.experimental import pallas as pl
from jax.experimental.pallas import tpu as pltpu
from jax.sharding import PartitionSpec as P

HD = 128
EPSILON = 1e-06
THETA = 1000000.0
BF = jnp.bfloat16
F32 = jnp.float32


def rope_tables(length):
    middle = HD // 2
    inverse = THETA ** (-(jnp.arange(middle, dtype=F32) * 2.0 / HD))
    angles = jnp.arange(length, dtype=F32)[:, None] * inverse[None, :]
    sine = jnp.sin(angles)
    return (jnp.concatenate([jnp.cos(angles)] * 2, -1), jnp.concatenate([-sine, sine], -1))


def rms_scale(values):
    return lax.rsqrt(jnp.mean(values * values, -1, keepdims=True) + EPSILON)


def plain_dot(left_side, right_side):
    return jnp.dot(left_side, right_side, preferred_element_type=F32)


def right_dot(left_side, right_side):
    return lax.dot_general(
        left_side, right_side, (((1,), (1,)), ((), ())), preferred_element_type=F32
    )


def left_dot(left_side, right_side):
    return lax.dot_general(
        left_side, right_side, (((0,), (0,)), ((), ())), preferred_element_type=F32
    )


def ring_order(count):
    wide = 2 if count <= 8 else 4
    tall = count // wide
    order = [z * wide for z in range(tall)]
    for z in range(tall - 1, -1, -1):
        row = list(range(1, wide))
        if (tall - 1 - z) % 2:
            row = row[::-1]
        order += [z * wide + x for x in row]
    return order


class Ring:
    def __init__(self, count):
        self.count = count
        self.half = count // 2
        place = lax.axis_index("dp").astype(jnp.int32)
        self.core = jnp.stack([place % 2, place // 2])
        order = ring_order(count)
        self.forward = [(order[i], order[(i + 1) % count]) for i in range(count)]
        self.backward = [(order[i], order[(i - 1) % count]) for i in range(count)]
        place = [0] * count
        for at, device in enumerate(order):
            place[device] = at
        distances = []
        for step in range(1, self.half):
            distances += [-step, step]
        distances += [0, self.half]
        here = jnp.array(place, jnp.int32)[lax.axis_index("expert")]
        around = (here + jnp.array(distances, jnp.int32) + count) % count
        self.block_of_slot = jnp.array(order, jnp.int32)[around]
        hits = self.block_of_slot[None, :] == jnp.arange(count, dtype=jnp.int32)[:, None]
        self.slot_of_block = jnp.sum(hits * jnp.arange(count, dtype=jnp.int32)[None, :], 1)

    def slot(self, distance):
        if distance in (0, self.half):
            return self.count - 2 + (distance > 0)
        return 2 * abs(distance) - 2 + (distance > 0)


def after(values, *others):
    return lax.optimization_barrier((values, others))[0]


def move(ring, rounds, *others):
    up, down = zip(*[each.outgoing() for each in rounds])
    rows = [piece.shape[0] for piece in up]
    if len(rounds) > 1:
        up, down = jnp.concatenate(up, 0), jnp.concatenate(down, 0)
    else:
        up, down = up[0], down[0]
    up, down = after((up, down), *others)
    ahead = lax.ppermute(up, "expert", ring.forward)
    behind = lax.ppermute(down, "expert", ring.backward)
    at = 0
    for each, count in zip(rounds, rows):
        if len(rounds) > 1:
            each.arrive(ahead[at : at + count], behind[at : at + count])
        else:
            each.arrive(ahead, behind)
        at += count
    return (ahead, behind)


class Gather:
    def __init__(self, ring, block):
        self.ring = ring
        self.pieces = [block]
        self.ahead = self.behind = block
        self.at = 0

    def outgoing(self):
        self.at += 1
        if self.at < self.ring.half:
            return self.ahead, self.behind
        middle = self.pieces[0].shape[0] // 2
        return self.ahead[:middle], self.behind[middle:]

    def arrive(self, ahead, behind):
        self.ahead, self.behind = ahead, behind
        self.pieces += [ahead, behind]

    def step(self, *others):
        return move(self.ring, [self], *others)

    def chunk(self, which):
        if which < self.ring.half - 1:
            return self.pieces[2 * which + 1 : 2 * which + 3]
        return [self.pieces[0]] + self.pieces[-2:]

    def rest(self):
        while self.at < self.ring.half:
            self.step()
        return self.pieces[1:-2] + [self.pieces[0]] + self.pieces[-2:]


class Scatter:
    def __init__(self, ring, chunks, rows):
        self.ring = ring
        self.chunks = chunks
        self.rows = rows
        self.at = ring.half

    def own(self, distance):
        slot = self.ring.slot(distance)
        slots = self.ring.count // len(self.chunks)
        start = slot % slots * self.rows
        return self.chunks[slot // slots][start : start + self.rows]

    def outgoing(self):
        middle = self.rows // 2
        at = self.at
        self.at -= 1
        if at == self.ring.half:
            far = self.own(at)
            return far[:middle], far[middle:]
        up = self.own(at).astype(F32)
        down = self.own(-at).astype(F32)
        if at == self.ring.half - 1:
            up = jnp.concatenate([up[:middle] + self.ahead.astype(F32), up[middle:]], 0)
            down = jnp.concatenate([down[:middle], down[middle:] + self.behind.astype(F32)], 0)
        else:
            up = up + self.ahead.astype(F32)
            down = down + self.behind.astype(F32)
        return up.astype(BF), down.astype(BF)

    def arrive(self, ahead, behind):
        self.ahead, self.behind = ahead, behind

    def step(self, *others):
        return move(self.ring, [self], *others)

    def rest(self, *others):
        while self.at:
            self.step()
        return after(self.own(0), *others).astype(F32) + self.ahead.astype(F32) + self.behind.astype(F32)


def cube_steps(axis):
    count = lax.axis_size(axis)
    step, moves = 1, []
    while step < count:
        moves.append((axis, [(i, i ^ step) for i in range(count)]))
        step *= 2
    return moves


class PairSum:
    def __init__(self, splits, rights):
        self.splits = splits
        self.rights = rights
        self.tall = len(splits[0]) - 1

    def lefts(self, which, *others):
        return after([split[which] for split in self.splits], *others)

    def cores(self, *others, time=0):
        count = lax.axis_size("dp")
        (sent,) = pair_dot(self.lefts(0, *others), self.rights, [], BF, 1, time)
        self.arrived = lax.ppermute(sent, "dp", [(i, i ^ 1) for i in range(count)])
        return sent

    def chips(self, *others, time=0):
        count = lax.axis_size("dp")
        size = self.splits[0][1].shape[1]
        self.parts = []
        out = others
        for step in range(1, self.tall):
            adds = [(self.arrived, step * size)]
            (out,) = pair_dot(self.lefts(1 + step, *others), self.rights, adds, BF, 1, time)
            moves = [(i, (i // 2 + step) % self.tall * 2 + i % 2) for i in range(count)]
            self.parts.append(lax.ppermute(out, "dp", moves))
        return out

    def total(self, *others, time=0, outs=1, turned_rows=0):
        adds = [(self.arrived, 0)] + [(part, 0) for part in self.parts]
        lefts = self.lefts(1, *others)
        return pair_dot(lefts, self.rights, adds, F32, outs, time, turned_rows)


WHOLE = pl.BlockSpec(memory_space=pltpu.VMEM)
ANY = pl.BlockSpec(memory_space=pl.ANY)
SCALARS = pl.BlockSpec(memory_space=pltpu.SMEM)


class Copies:
    def __init__(self, sems):
        self.sems = sems
        self.count = 0

    def start(self, source, target):
        copy = pltpu.make_async_copy(source, target, self.sems.at[self.count])
        self.count += 1
        copy.start()
        return copy


def tiles_of(columns, wide):
    return [(low, min(low + wide, columns)) for low in range(0, columns, wide)]


def bring(copies, pieces, rows_ref):
    at, started = 0, []
    for piece in pieces:
        rows = slice(at, at + piece.shape[0])
        started.append(copies.start(piece, rows_ref.at[rows]))
        at += piece.shape[0]
    return started


def chunks_of(pieces, brought, wide):
    at, left = 0, list(zip(pieces, brought))
    for low in range(0, sum(piece.shape[0] for piece in pieces), wide):
        waits = []
        while left and at < low + wide:
            piece, copy = left.pop(0)
            at += piece.shape[0]
            waits.append(copy)
        yield slice(low, low + wide), waits


def params(mebibytes):
    return pltpu.CompilerParams(vmem_limit_bytes=mebibytes * 1024 * 1024)


def cost(time):
    return pl.CostEstimate(flops=int(1e9 * time) + 1, bytes_accessed=1, transcendentals=0)


def split_shapes(rows, width):
    count = lax.axis_size("dp")
    widths = [width // 2] + [width // count] * (count // 2)
    return tuple(jax.ShapeDtypeStruct((rows, w), BF) for w in widths)


def put_split(place, row_ref, refs, rows=slice(None)):
    core, far = place[0], place[1]
    other_ref, own_refs = refs[0], refs[1:]
    columns, tall = own_refs[0].shape[1], len(own_refs)
    for part in range(tall):
        chip = lax.rem(far + part, tall)
        at = pl.multiple_of((2 * chip + 1 - core) * columns, columns)
        there = slice(part * columns, (part + 1) * columns)
        other_ref[rows, there] = row_ref[rows, pl.ds(at, columns)]
        at = pl.multiple_of((2 * chip + core) * columns, columns)
        own_refs[part][rows, :] = row_ref[rows, pl.ds(at, columns)]


def turned(values, cosine, sine):
    return values * cosine + pltpu.roll(values, HD // 2, 1) * sine


def project_kernel(pieces, splits, places, place, *refs):
    parts, refs = refs[:pieces], refs[pieces:]
    hbm, refs = refs[:8], refs[8:]
    outs, refs = refs[:3], refs[3:]
    split_hbm, refs = refs[: splits + 1], refs[splits + 1 :]
    q_ref, k_ref, v_ref = outs
    h_ref, refs = refs[0], refs[1:]
    split_ref, refs = refs[:splits], refs[splits:]
    w_ref, bq, bk, bv, cos, sin, sems = refs
    cols = bq.shape[1]
    copies = Copies(sems)
    targets = [w_ref.at[:, at * cols : (at + 1) * cols] for at in range(3)]
    of_weights = [copies.start(a, b) for a, b in zip(hbm, targets + [bq, bk, bv, cos, sin])]
    brought = bring(copies, parts, h_ref)
    block_rows = h_ref.shape[0] // places.shape[0]
    for copy in of_weights:
        copy.wait()
    kept = []
    sources = [h_ref] + list(split_ref)
    targets = [split_hbm[-1]] + list(split_hbm[:-1])
    for chunk, waits in chunks_of(parts, brought, 2 * block_rows):
        for copy in waits:
            copy.wait()
        put_split(place, h_ref, split_ref, chunk)
        kept += [copies.start(a.at[chunk], b.at[chunk]) for a, b in zip(sources, targets)]
        qkv = plain_dot(h_ref[chunk], w_ref[...])
        q = qkv[:, :cols] + bq[...].astype(F32)
        k = qkv[:, cols : 2 * cols] + bk[...].astype(F32)
        v = qkv[:, 2 * cols :] + bv[...].astype(F32)
        for part in range(2):
            start = places[chunk.start // block_rows + part] * block_rows
            rows = pl.ds(pl.multiple_of(start, block_rows), block_rows)
            near = slice(part * block_rows, (part + 1) * block_rows)
            cosine, sine = cos[rows, :], sin[rows, :]
            for head in range(cols // HD):
                hs = slice(head * HD, (head + 1) * HD)
                q_ref[rows, hs] = turned(q[near, hs], cosine, sine).astype(BF)
                k_ref[rows, hs] = turned(k[near, hs], cosine, sine).astype(BF)
            v_ref[rows, :] = v[near].astype(BF)
    for copy in kept:
        copy.wait()


def project(ring, parts, weights, biases, tables, time=3):
    width, cols = weights[0].shape
    length = sum(part.shape[0] for part in parts)
    shape = jax.ShapeDtypeStruct((length, cols), BF)
    split = split_shapes(length, width)
    pieces = len(parts)
    return pl.pallas_call(
        functools.partial(project_kernel, pieces, len(split)),
        out_shape=(shape,) * 3 + split + (jax.ShapeDtypeStruct((length, width), BF),),
        in_specs=[SCALARS] * 2 + [ANY] * (pieces + 8),
        out_specs=(WHOLE,) * 3 + (ANY,) * (len(split) + 1),
        scratch_shapes=[pltpu.VMEM((length, width), BF)]
        + [pltpu.VMEM(part.shape, BF) for part in split]
        + [pltpu.VMEM((width, 3 * cols), BF)]
        + [pltpu.VMEM((1, cols), BF)] * 3
        + [pltpu.VMEM((length, HD), F32)] * 2
        + [pltpu.SemaphoreType.DMA((pieces + 8 + ring.half * (len(split) + 1),))],
        compiler_params=params(52),
        cost_estimate=cost(time),
        name="project",
    )(ring.block_of_slot, ring.core, *parts, *weights, *[b[None] for b in biases], *tables)


def bring_all(sources, targets, sems):
    copies = Copies(sems)
    for copy in [copies.start(source, target) for source, target in zip(sources, targets)]:
        copy.wait()


def attend_kernel(
    block_rows, wide, slots, q_hbm, k_hbm, v_hbm, out_ref, q_ref, k_ref, v_ref, sems
):
    bring_all((q_hbm, k_hbm, v_hbm), (q_ref, k_ref, v_ref), sems)
    length, cols = q_ref.shape
    scale = HD ** (-0.5)
    at_row = lax.broadcasted_iota(jnp.int32, (wide, wide), 0)
    at_col = lax.broadcasted_iota(jnp.int32, (wide, wide), 1)
    allowed = at_col <= at_row
    for head in range(cols // HD):
        hs = slice(head * HD, (head + 1) * HD)
        for i in range(length // wide):
            low, high = i * wide, (i + 1) * wide
            q = q_ref[low:high, hs]
            near = right_dot(q, k_ref[low:high, hs]) * scale
            near = jnp.where(allowed, near, -jnp.inf)
            peak = jnp.max(near, 1, keepdims=True)
            if i:
                past = right_dot(q, k_ref[:low, hs]) * scale
                peak = jnp.maximum(peak, jnp.max(past, 1, keepdims=True))
                past = jnp.exp(past - peak)
            near = jnp.exp(near - peak)
            total = jnp.sum(near, 1, keepdims=True)
            if i:
                total = total + jnp.sum(past, 1, keepdims=True)
            share = 1.0 / total
            out = plain_dot((near * share).astype(BF), v_ref[low:high, hs])
            if i:
                out = out + plain_dot((past * share).astype(BF), v_ref[:low, hs])
            out = out.astype(BF)
            for part in range(wide // block_rows):
                slot = slots[i * (wide // block_rows) + part]
                rows = pl.ds(pl.multiple_of(slot * block_rows, block_rows), block_rows)
                out_ref[rows, hs] = out[part * block_rows : (part + 1) * block_rows]


def attend(ring, q, k, v, time=3):
    length, cols = q.shape
    return pl.pallas_call(
        functools.partial(attend_kernel, length // ring.count, 2 * (length // ring.count)),
        out_shape=jax.ShapeDtypeStruct((length, cols), BF),
        in_specs=[SCALARS] + [ANY] * 3,
        out_specs=WHOLE,
        scratch_shapes=[pltpu.VMEM((length, cols), BF)] * 3 + [pltpu.SemaphoreType.DMA((3,))],
        compiler_params=params(40),
        cost_estimate=cost(time),
        name="attend",
    )(ring.slot_of_block, q, k, v)


def attend_back_kernel(
    block_rows, wide, slots, q_hbm, k_hbm, v_hbm, g_hbm, cos_hbm, sin_hbm, out_ref, bias_ref,
    q_ref, k_ref, v_ref, g_ref, cos, sin, k_sum, v_sum, sems,
):
    sources = (q_hbm, k_hbm, v_hbm, g_hbm, cos_hbm, sin_hbm)
    bring_all(sources, (q_ref, k_ref, v_ref, g_ref, cos, sin), sems)
    length, cols = q_ref.shape
    scale = HD ** (-0.5)
    at_key = lax.broadcasted_iota(jnp.int32, (wide, wide), 0)
    at_query = lax.broadcasted_iota(jnp.int32, (wide, wide), 1)
    allowed = at_key <= at_query
    per = wide // block_rows
    bias_ref[...] = jnp.zeros_like(bias_ref)

    def put(which, low, head, values):
        hs = slice(which * cols + head * HD, which * cols + (head + 1) * HD)
        values = values.astype(BF)
        bias_ref[:, hs] += jnp.sum(values.astype(F32), 0, keepdims=True)
        for part in range(per):
            slot = slots[low // block_rows + part]
            rows = pl.ds(pl.multiple_of(slot * block_rows, block_rows), block_rows)
            out_ref[rows, hs] = values[part * block_rows : (part + 1) * block_rows]

    def back(values, low, high):
        return values * cos[low:high] - pltpu.roll(values, HD // 2, 1) * sin[low:high]

    for head in range(cols // HD):
        hs = slice(head * HD, (head + 1) * HD)
        for i in range(length // wide):
            low, high = i * wide, (i + 1) * wide
            q = q_ref[low:high, hs]
            g = g_ref[low:high, hs]
            spans = [(low, high)] + ([(0, low)] if i else [])
            scores = [right_dot(k_ref[a:b, hs], q) * scale for a, b in spans]
            scores[0] = jnp.where(allowed, scores[0], -jnp.inf)
            peak = functools.reduce(jnp.maximum, [jnp.max(s, 0, keepdims=True) for s in scores])
            probs = [jnp.exp(s - peak) for s in scores]
            total = sum(jnp.sum(p, 0, keepdims=True) for p in probs)
            share = 1.0 / total
            probs = [p * share for p in probs]
            grads = [right_dot(v_ref[a:b, hs], g) for a, b in spans]
            mean = sum(jnp.sum(p * d, 0, keepdims=True) for p, d in zip(probs, grads))
            draws = [(p * (d - mean) * scale).astype(BF) for p, d in zip(probs, grads)]
            dq = sum(left_dot(d, k_ref[a:b, hs]) for d, (a, b) in zip(draws, spans))
            put(0, low, head, back(dq, low, high))
            for at, (a, b) in enumerate(spans):
                dv = plain_dot(probs[at].astype(BF), g)
                dk = plain_dot(draws[at], q)
                if at == 0:
                    v_sum[a:b, hs] = dv
                    k_sum[a:b, hs] = dk
                else:
                    v_sum[a:b, hs] += dv
                    k_sum[a:b, hs] += dk
        for i in range(length // wide):
            low, high = i * wide, (i + 1) * wide
            put(1, low, head, back(k_sum[low:high, hs], low, high))
            put(2, low, head, v_sum[low:high, hs])


def attend_back(ring, q, k, v, grad, tables, time=20):
    length, cols = q.shape
    return pl.pallas_call(
        functools.partial(attend_back_kernel, length // ring.count, 2 * (length // ring.count)),
        out_shape=(
            jax.ShapeDtypeStruct((length, 3 * cols), BF),
            jax.ShapeDtypeStruct((1, 3 * cols), F32),
        ),
        in_specs=[SCALARS] + [ANY] * 6,
        out_specs=(WHOLE,) * 2,
        scratch_shapes=[pltpu.VMEM((length, cols), BF)] * 4
        + [pltpu.VMEM((length, HD), F32)] * 2
        + [pltpu.VMEM((length, cols), F32)] * 2
        + [pltpu.SemaphoreType.DMA((6,))],
        compiler_params=params(48),
        cost_estimate=cost(time),
        name="attend_back",
    )(ring.slot_of_block, q, k, v, grad, *tables)


def attend_in_kernel(
    d_hbm, wq_hbm, wk_hbm, wv_hbm, h_hbm, gain_ref, out_hbm, gain_out,
    d_ref, wq_ref, wk_ref, wv_ref, h_ref, out_ref, sems,
):
    cols = wq_ref.shape[1]
    copies = Copies(sems)
    of_d = copies.start(d_hbm, d_ref)
    tiles = tiles_of(h_ref.shape[1], 512)
    weights = ((wq_hbm, wq_ref), (wk_hbm, wk_ref), (wv_hbm, wv_ref))
    of_tiles = [
        [copies.start(a.at[low:high], b.at[low:high]) for a, b in weights]
        + [copies.start(h_hbm.at[:, low:high], h_ref.at[:, low:high])]
        for low, high in tiles
    ]
    of_d.wait()
    kept = []
    for started, (low, high) in zip(of_tiles, tiles):
        for copy in started[:-1]:
            copy.wait()
        out = right_dot(d_ref[:, :cols], wq_ref[low:high])
        out = out + right_dot(d_ref[:, cols : 2 * cols], wk_ref[low:high])
        out = out + right_dot(d_ref[:, 2 * cols :], wv_ref[low:high])
        out_ref[:, low:high] = out.astype(BF)
        kept.append(copies.start(out_ref.at[:, low:high], out_hbm.at[:, low:high]))
        started[-1].wait()
        products = out * h_ref[:, low:high].astype(F32)
        gain_out[:, low:high] = jnp.sum(products, 0, keepdims=True) / gain_ref[:, low:high]
    for copy in kept:
        copy.wait()


def attend_in(grads, weights, h_all, gain, time=1):
    length, cols = grads.shape
    width = h_all.shape[1]
    return pl.pallas_call(
        attend_in_kernel,
        out_shape=(
            jax.ShapeDtypeStruct((length, width), BF),
            jax.ShapeDtypeStruct((1, width), F32),
        ),
        in_specs=[ANY] * 5 + [WHOLE],
        out_specs=(ANY, WHOLE),
        scratch_shapes=[pltpu.VMEM((length, cols), BF)]
        + [pltpu.VMEM((width, cols // 3), BF)] * 3
        + [
            pltpu.VMEM((length, width), BF),
            pltpu.VMEM((length, width), BF),
            pltpu.SemaphoreType.DMA((1 + 5 * len(tiles_of(width, 512)),)),
        ],
        compiler_params=params(48),
        cost_estimate=cost(time),
        name="attend_in",
    )(grads, *weights, h_all, gain)


def reorder_dot_kernel(pieces, splits, places, place, *refs):
    parts, refs = refs[:pieces], refs[pieces:]
    w_hbm, out_ref, refs = refs[0], refs[1], refs[2:]
    split_hbm, refs = refs[:splits], refs[splits:]
    h_ref, split_ref, w_ref = refs[0], refs[1 : 1 + splits], refs[1 + splits]
    copies = Copies(refs[-1])
    of_weight = copies.start(w_hbm, w_ref)
    brought = bring(copies, parts, h_ref)
    block_rows = h_ref.shape[0] // places.shape[0]
    of_weight.wait()
    kept = []
    for chunk, waits in chunks_of(parts, brought, 2 * block_rows):
        for copy in waits:
            copy.wait()
        put_split(place, h_ref, split_ref, chunk)
        kept += [copies.start(a.at[chunk], b.at[chunk]) for a, b in zip(split_ref, split_hbm)]
        out = plain_dot(h_ref[chunk], w_ref[...]).astype(BF)
        for part in range(2):
            start = places[chunk.start // block_rows + part] * block_rows
            rows = pl.ds(pl.multiple_of(start, block_rows), block_rows)
            out_ref[rows, :] = out[part * block_rows : (part + 1) * block_rows]
    for copy in kept:
        copy.wait()


def reorder_dot(ring, parts, weight, time=10):
    width, cols = weight.shape
    length = sum(part.shape[0] for part in parts)
    split = split_shapes(length, width)
    pieces = len(parts)
    return pl.pallas_call(
        functools.partial(reorder_dot_kernel, pieces, len(split)),
        out_shape=(jax.ShapeDtypeStruct((length, cols), BF),) + split,
        in_specs=[SCALARS] * 2 + [ANY] * (pieces + 1),
        out_specs=(WHOLE,) + (ANY,) * len(split),
        scratch_shapes=[pltpu.VMEM((length, width), BF)]
        + [pltpu.VMEM(part.shape, BF) for part in split]
        + [
            pltpu.VMEM((width, cols), BF),
            pltpu.SemaphoreType.DMA((pieces + 1 + ring.half * len(split),)),
        ],
        compiler_params=params(52),
        cost_estimate=cost(time),
        name="reorder_dot",
    )(ring.block_of_slot, ring.core, *parts, weight)


def gated(gate_pre, up_pre, back, scale):
    sigmoid = 0.5 + 0.5 * jnp.tanh(0.5 * gate_pre)
    silu = gate_pre * sigmoid
    hidden = silu * up_pre
    scaled = scale * back
    grad_gate = scaled * up_pre * (sigmoid + silu * (1.0 - sigmoid))
    return hidden, scale * hidden, grad_gate, scaled * silu


def back_kernel(pieces, which, split, place, *refs):
    parts, refs = refs[:pieces], refs[pieces:]
    wo_hbm, wd_hbm = refs[:2]
    refs = refs[-(2 * split + 6) :]
    back_e_ref, back_s_ref = refs[:2]
    kept_hbm, kept_ref = refs[2 : 2 + split], refs[2 + split : 2 + 2 * split]
    rows_ref, wo_ref, wd_ref, sems = refs[-4:]
    rows, width = rows_ref.shape
    copies = Copies(sems)
    brought = bring(copies, parts, rows_ref)
    tiles = tiles_of(wo_ref.shape[1], 512)
    of_e = [copies.start(wo_hbm.at[:, a:b], wo_ref.at[:, a:b]) for a, b in tiles]
    of_s = copies.start(wd_hbm, wd_ref)
    for copy in brought:
        copy.wait()
    put_split(place, rows_ref, kept_ref)
    chunk = slice(which * rows, (which + 1) * rows)
    kept = [copies.start(ref, hbm.at[chunk]) for ref, hbm in zip(kept_ref, kept_hbm)]
    for copy, (a, b) in zip(of_e, tiles):
        copy.wait()
        back_e_ref[:, a:b] = plain_dot(rows_ref[...], wo_ref[:, a:b]).astype(BF)
    of_s.wait()
    back_s_ref[...] = right_dot(rows_ref[...], wd_ref[...]).astype(BF)
    for copy in kept:
        copy.wait()


def back_units(ring, which, parts, weight_out, weight_down, kept, time=6):
    width, units = weight_out.shape
    shared = weight_down.shape[0]
    rows = sum(part.shape[0] for part in parts)
    pieces = len(parts)
    first = pieces + 3
    split = split_shapes(rows * ring.half, width)
    return pl.pallas_call(
        functools.partial(back_kernel, pieces, which, len(split)),
        out_shape=(
            jax.ShapeDtypeStruct((rows, units), BF),
            jax.ShapeDtypeStruct((rows, shared), BF),
        )
        + split,
        in_specs=[SCALARS] + [ANY] * (pieces + 2 + len(kept)),
        out_specs=(WHOLE, WHOLE) + (ANY,) * len(split),
        scratch_shapes=[pltpu.VMEM((rows, part.shape[1]), BF) for part in split]
        + [
            pltpu.VMEM((rows, width), BF),
            pltpu.VMEM((width, units), BF),
            pltpu.VMEM((shared, width), BF),
            pltpu.SemaphoreType.DMA((pieces + len(tiles_of(units, 512)) + 1 + len(split),)),
        ],
        input_output_aliases={first + at: 2 + at for at in range(len(kept))},
        compiler_params=params(48),
        cost_estimate=cost(time),
        name="back_units",
    )(ring.core, *parts, weight_out, weight_down, *kept)


UNIT_TILE = 512


def units_kernel(pieces, which, experts, count, me_ref, place, *refs):
    parts, refs = refs[:pieces], refs[pieces:]
    wi_hbm, wg_hbm, wu_hbm, back_e_hbm, back_s_hbm = refs[:5]
    refs = refs[-(2 * count + 9) :]
    small_ref = refs[0]
    kept_hbm, kept_ref = refs[1 : 1 + count], refs[1 + count : 1 + 2 * count]
    hid_e_ref, hid_s_ref, both_ref, both_s_ref = kept_ref[:4]
    h_ref, wi_ref, wg_ref, wu_ref, back_e_ref, back_s_ref, sum_ref, sems = refs[-8:]
    rows = h_ref.shape[0]
    width, units = wi_ref.shape[0], wi_ref.shape[1] // 2
    me = me_ref[0]
    copies = Copies(sems)
    brought = bring(copies, parts, h_ref)
    tiles = tiles_of(units, UNIT_TILE)
    of_e = []
    for a, b in tiles:
        of_e.append(
            (
                copies.start(wi_hbm.at[:, a:b], wi_ref.at[:, 2 * a : a + b]),
                copies.start(wi_hbm.at[:, units + a : units + b], wi_ref.at[:, a + b : 2 * b]),
            )
        )
        if a == 0:
            of_back_e = copies.start(back_e_hbm, back_e_ref)
    of_s = [
        copies.start(wg_hbm, wg_ref),
        copies.start(wu_hbm, wu_ref),
        copies.start(back_s_hbm, back_s_ref),
    ]
    chunk = slice(which * rows, (which + 1) * rows)
    started = []

    def keep(*places):
        for at in places:
            started.append(copies.start(kept_ref[at], kept_hbm[at].at[chunk]))

    def scale_of(low, high):
        aux = h_ref[:, width:].astype(F32)
        lane = lax.broadcasted_iota(jnp.int32, aux.shape, 1)
        return jnp.sum(jnp.where((lane == low) | (lane == high), aux, 0.0), 1, keepdims=True)

    for copy in brought:
        copy.wait()
    put_split(place, h_ref, kept_ref[4:])
    keep(*range(4, count))
    gate = scale_of(me, experts + me)
    h = h_ref[:, :width]
    sum_ref[...] = jnp.zeros_like(sum_ref)
    for which_tile, (a, b) in enumerate(tiles):
        for copy in of_e[which_tile]:
            copy.wait()
        if a == 0:
            of_back_e.wait()
        both = plain_dot(h, wi_ref[:, 2 * a : 2 * b])
        back = back_e_ref[:, a:b].astype(F32)
        hidden, scaled, da, db = gated(both[:, : b - a], both[:, b - a :], back, gate)
        products = hidden * back
        for low in range(0, b - a, 128):
            sum_ref[...] += products[:, low : low + 128]
        hid_e_ref[:, a:b] = scaled.astype(BF)
        both_ref[:, a:b] = da.astype(BF)
        both_ref[:, units + a : units + b] = db.astype(BF)
    keep(0, 2)
    for copy in of_s:
        copy.wait()
    switch = scale_of(2 * experts, 3 * experts)
    back = back_s_ref[...].astype(F32)
    hidden, scaled, dg, du = gated(
        right_dot(h, wg_ref[...]), right_dot(h, wu_ref[...]), back, switch
    )
    hid_s_ref[...] = jnp.zeros_like(hid_s_ref)
    hid_s_ref[:, : scaled.shape[1]] = scaled.astype(BF)
    shared = dg.shape[1]
    both_s_ref[:, :shared] = dg.astype(BF)
    both_s_ref[:, shared:] = du.astype(BF)
    keep(1, 3)
    of_switch = jnp.sum(hidden * back, 1, keepdims=True)
    of_gate = jnp.sum(sum_ref[...], 1, keepdims=True)
    lane = lax.broadcasted_iota(jnp.int32, small_ref.shape, 1)
    small = jnp.zeros(small_ref.shape, F32)
    for value, first in ((of_gate, 0), (of_switch, 2 * experts)):
        high = value.astype(BF).astype(F32)
        small = small + jnp.where(lane == first + me, high, 0.0)
        small = small + jnp.where(lane == first + experts + me, value - high, 0.0)
    small_ref[...] = small.astype(BF)
    for copy in started:
        copy.wait()


def hidden_units(
    ring, which, me, experts, parts, weight_in, weight_gate, weight_up, back_e, back_s, kept,
    time=6,
):
    rows, units = back_e.shape
    shared = back_s.shape[1]
    width = weight_in.shape[0]
    pieces = len(parts)
    first = pieces + 7
    columns = [units, -(-shared // 128) * 128, 2 * units, 2 * shared]
    columns += [part.shape[1] for part in split_shapes(rows, width)]
    copies = pieces + 2 * len(tiles_of(units, UNIT_TILE)) + 4 + len(columns)
    return pl.pallas_call(
        functools.partial(units_kernel, pieces, which, experts, len(columns)),
        out_shape=(jax.ShapeDtypeStruct((rows, 128), BF),)
        + tuple(jax.ShapeDtypeStruct((rows * ring.half, c), BF) for c in columns),
        in_specs=[SCALARS] * 2 + [ANY] * (pieces + 5 + len(kept)),
        out_specs=(WHOLE,) + (ANY,) * len(columns),
        scratch_shapes=[pltpu.VMEM((rows, c), BF) for c in columns]
        + [
            pltpu.VMEM((rows, width + 128), BF),
            pltpu.VMEM((width, 2 * units), BF),
            pltpu.VMEM((shared, width), BF),
            pltpu.VMEM((shared, width), BF),
            pltpu.VMEM((rows, units), BF),
            pltpu.VMEM((rows, shared), BF),
            pltpu.VMEM((rows, 128), F32),
            pltpu.SemaphoreType.DMA((copies,)),
        ],
        input_output_aliases={first + at: 1 + at for at in range(len(kept))},
        compiler_params=params(52),
        cost_estimate=cost(time),
        name="hidden_units",
    )(
        me,
        ring.core,
        *parts,
        weight_in,
        weight_gate,
        weight_up,
        back_e,
        back_s,
        *kept,
    )


IN_TILE = 512


def units_in_kernel(
    which, both_hbm, both_s_hbm, small_ref, wi_hbm, wg_hbm, wu_hbm, out_ref,
    both_ref, both_s_ref, wi_ref, ws_ref, sems,
):
    rows = both_ref.shape[0]
    width, shared = wi_ref.shape[0], ws_ref.shape[0] // 2
    copies = Copies(sems)
    chunk = slice(which * rows, (which + 1) * rows)
    brought = [
        copies.start(both_hbm.at[chunk], both_ref),
        copies.start(both_s_hbm.at[chunk], both_s_ref),
    ]
    tiles = tiles_of(width, IN_TILE)
    weights = [
        [
            copies.start(wi_hbm.at[a:b], wi_ref.at[a:b]),
            copies.start(wg_hbm.at[:, a:b], ws_ref.at[:shared, a:b]),
            copies.start(wu_hbm.at[:, a:b], ws_ref.at[shared:, a:b]),
        ]
        for a, b in tiles
    ]
    out_ref[:, width:] = small_ref[...]
    for copy in brought:
        copy.wait()
    for started, (a, b) in zip(weights, tiles):
        for copy in started:
            copy.wait()
        out = right_dot(both_ref[...], wi_ref[a:b])
        out = out + plain_dot(both_s_ref[...], ws_ref[:, a:b])
        out_ref[:, a:b] = out.astype(BF)


def units_in(which, both, both_s, small, weight_in, weight_gate, weight_up, time):
    joined, joined_s = both.shape[1], both_s.shape[1]
    rows = small.shape[0]
    width = weight_in.shape[0]
    return pl.pallas_call(
        functools.partial(units_in_kernel, which),
        out_shape=jax.ShapeDtypeStruct((rows, width + 128), BF),
        in_specs=[ANY] * 2 + [WHOLE] + [ANY] * 3,
        out_specs=WHOLE,
        scratch_shapes=[
            pltpu.VMEM((rows, joined), BF),
            pltpu.VMEM((rows, joined_s), BF),
            pltpu.VMEM((width, joined), BF),
            pltpu.VMEM((joined_s, width), BF),
            pltpu.SemaphoreType.DMA((2 + 3 * len(tiles_of(width, IN_TILE)),)),
        ],
        compiler_params=params(48),
        cost_estimate=cost(time),
        name="units_in",
    )(both, both_s, small, weight_in, weight_gate, weight_up)


def pair_kernel(pairs, first_rows, outs, turned_rows, *refs):
    adds = len(first_rows)
    lefts_hbm, rights_hbm = refs[:pairs], refs[pairs : 2 * pairs]
    refs = refs[2 * pairs :]
    adds_hbm, outs_hbm = refs[:adds], refs[adds : adds + outs]
    refs = refs[adds + outs :]
    lefts_ref, rights_ref = refs[:pairs], refs[pairs : 2 * pairs]
    refs = refs[2 * pairs :]
    adds_ref, outs_ref = refs[:adds], refs[adds : adds + outs]
    copies = Copies(refs[-1])
    rows = lefts_ref[0].shape[1]
    tiles = pair_tiles([ref.shape[1] for ref in rights_ref], 1 if turned_rows else outs)
    of_lefts = [None] * pairs
    of_tiles = []
    for pair, low, a, b in tiles:
        if of_lefts[pair] is None:
            of_lefts[pair] = copies.start(lefts_hbm[pair], lefts_ref[pair])
        near = slice(a - low, b - low)
        started = [copies.start(rights_hbm[pair].at[:, near], rights_ref[pair].at[:, near])]
        for first, hbm, ref in zip(first_rows, adds_hbm, adds_ref):
            started.append(copies.start(hbm.at[first : first + rows, a:b], ref.at[:, a:b]))
        of_tiles.append(started)
    started = []
    for at, (pair, low, a, b) in enumerate(tiles):
        if of_lefts[pair] is not None:
            of_lefts[pair].wait()
            of_lefts[pair] = None
        for copy in of_tiles[at]:
            copy.wait()
        out = left_dot(lefts_ref[pair][...], rights_ref[pair][:, a - low : b - low])
        for ref in adds_ref:
            out = out + ref[:, a:b].astype(F32)
        if turned_rows:
            out = out.T
            for which, target in enumerate(outs_ref):
                low = which * turned_rows
                first, last = max(a, low), min(b, low + turned_rows)
                if first < last:
                    target[first - low : last - low] = out[first - a : last - a]
            continue
        wide = outs_ref[0].shape[1]
        target, hbm = outs_ref[a // wide], outs_hbm[a // wide]
        near = slice(a % wide, a % wide + b - a)
        target[:, near] = out.astype(target.dtype)
        started.append(copies.start(target.at[:, near], hbm.at[:, near]))
    if turned_rows:
        started = [copies.start(target, hbm) for target, hbm in zip(outs_ref, outs_hbm)]
    for copy in started:
        copy.wait()


def pair_tiles(widths, outs):
    wide = sum(widths) // outs
    tiles, low = [], 0
    for pair, width in enumerate(widths):
        a = low
        while a < low + width:
            b = min(a + 512, low + width, (a // wide + 1) * wide)
            tiles.append((pair, low, a, b))
            a = b
        low += width
    return tiles


def pair_dot(lefts, rights, adds, held, outs=1, time=0, turned_rows=0):
    length, rows = lefts[0].shape
    widths = [right.shape[1] for right in rights]
    columns = sum(widths)
    tiles = len(pair_tiles(widths, 1 if turned_rows else outs))
    pairs = len(lefts)
    shape = (turned_rows, rows) if turned_rows else (rows, columns // outs)
    return pl.pallas_call(
        functools.partial(
            pair_kernel, pairs, [first for _, first in adds], outs, turned_rows
        ),
        out_shape=(jax.ShapeDtypeStruct(shape, held),) * outs,
        in_specs=[ANY] * (2 * pairs + len(adds)),
        out_specs=(ANY,) * outs,
        scratch_shapes=[pltpu.VMEM((length, rows), BF)] * pairs
        + [pltpu.VMEM((length, width), BF) for width in widths]
        + [pltpu.VMEM((rows, columns), BF)] * len(adds)
        + [pltpu.VMEM(shape, held)] * outs
        + [pltpu.SemaphoreType.DMA((pairs + outs + tiles * (2 + len(adds)),))],
        compiler_params=params(52),
        cost_estimate=cost(time),
        name="pair_dot",
    )(*lefts, *rights, *[values for values, _ in adds])


def layer_kernel(low, he_hbm, hs_hbm, wo_hbm, wd_hbm, out_ref, he_ref, hs_ref, wo_ref, wd_ref, sems):
    rows = slice(low, low + he_ref.shape[0])
    copies = Copies(sems)
    brought = [
        copies.start(he_hbm.at[rows], he_ref),
        copies.start(hs_hbm.at[rows], hs_ref),
    ]
    tiles = tiles_of(wo_ref.shape[0], IN_TILE)
    weights = [
        (
            copies.start(wo_hbm.at[a:b], wo_ref.at[a:b]),
            copies.start(wd_hbm.at[:, a:b], wd_ref.at[:, a:b]),
        )
        for a, b in tiles
    ]
    for copy in brought:
        copy.wait()
    for started, (a, b) in zip(weights, tiles):
        for copy in started:
            copy.wait()
        out = right_dot(he_ref[...], wo_ref[a:b]) + plain_dot(hs_ref[:, : wd_ref.shape[0]], wd_ref[:, a:b])
        out_ref[:, a:b] = out.astype(BF)


def layer_part(low, high, hid_e, hid_s, weight_out, weight_down, time):
    width, units = weight_out.shape
    shared = weight_down.shape[0]
    rows = high - low
    return pl.pallas_call(
        functools.partial(layer_kernel, low),
        out_shape=jax.ShapeDtypeStruct((rows, width), BF),
        in_specs=[ANY] * 4,
        out_specs=WHOLE,
        scratch_shapes=[
            pltpu.VMEM((rows, units), BF),
            pltpu.VMEM((rows, hid_s.shape[1]), BF),
            pltpu.VMEM((width, units), BF),
            pltpu.VMEM((shared, width), BF),
            pltpu.SemaphoreType.DMA((2 + 2 * len(tiles_of(width, IN_TILE)),)),
        ],
        compiler_params=params(48),
        cost_estimate=cost(time),
        name="layer_part",
    )(hid_e, hid_s, weight_out, weight_down)


def past_units_kernel(
    experts, residual_ref, own_ref, ahead_ref, behind_ref, grad_ref, gain_ref, head_ref,
    routed_ref, picked_ref, sent_ref, out_ref, low_ref, rows_ref, gain_out,
):
    width = residual_ref.shape[1]
    total = own_ref[...].astype(F32) + ahead_ref[...].astype(F32) + behind_ref[...].astype(F32)
    small = total[:, width:]
    routed = routed_ref[...]
    lane = lax.broadcasted_iota(jnp.int32, small.shape, 1)
    probs = jnp.where(lane < experts, routed, 0.0)
    grads = picked_ref[...] * (small + pltpu.roll(small, 128 - experts, 1))
    grads = jnp.where(lane < experts, grads, 0.0)
    logits = probs * (grads - jnp.sum(probs * grads, 1, keepdims=True))
    switch = jnp.where(lane == 2 * experts, routed, 0.0)
    of_switch = jnp.where((lane >= 2 * experts) & (lane < 4 * experts), small, 0.0)
    of_switch = jnp.sum(of_switch, 1, keepdims=True) * switch * (1.0 - switch)
    scores = logits + of_switch
    high = scores.astype(BF)
    rest = (scores - high.astype(F32)).astype(BF)
    grad = total[:, :width] + plain_dot(high, head_ref[...]) + plain_dot(rest, head_ref[...])
    h = sent_ref[:, :width]
    rows_ref[...] = left_dot(high, h) + left_dot(rest, h)
    residual = residual_ref[...]
    scale = rms_scale(residual)
    unit = residual * scale
    gain_out[...] = jnp.sum(grad * unit, 0, keepdims=True)
    grad = grad * gain_ref[...].astype(F32)
    mean = jnp.mean(grad * unit, -1, keepdims=True)
    out = grad_ref[...].astype(F32) + scale * (grad - unit * mean)
    out_ref[...] = out
    low_ref[...] = out.astype(BF)


def past_units(experts, residual, own, ahead, behind, grad, gain, head, routed, picked, sent):
    rows, width = residual.shape
    return pl.pallas_call(
        functools.partial(past_units_kernel, experts),
        out_shape=(
            jax.ShapeDtypeStruct((rows, width), F32),
            jax.ShapeDtypeStruct((rows, width), BF),
            jax.ShapeDtypeStruct((128, width), F32),
            jax.ShapeDtypeStruct((1, width), F32),
        ),
        in_specs=[WHOLE] * 10,
        out_specs=(WHOLE,) * 4,
        compiler_params=params(40),
        cost_estimate=cost(0),
        name="past_units",
    )(residual, own, ahead, behind, grad, gain, head, routed, picked, sent)


def routing_kernel(
    experts, x_ref, own_ref, ahead_ref, behind_ref, gain_ref, head_ref, picked_ref,
    residual_ref, sent_ref, routing_ref,
):
    width = x_ref.shape[1]
    residual = x_ref[...].astype(F32) + own_ref[...].astype(F32)
    residual = residual + ahead_ref[...].astype(F32) + behind_ref[...].astype(F32)
    h = (residual * rms_scale(residual) * gain_ref[...].astype(F32)).astype(BF)
    scores = right_dot(h, head_ref[...])
    lane = lax.broadcasted_iota(jnp.int32, scores.shape, 1)
    is_expert = lane < experts
    raised = jnp.where(is_expert, scores, -jnp.inf)
    raised = jnp.exp(raised - jnp.max(raised, 1, keepdims=True))
    probs = raised / jnp.sum(raised, 1, keepdims=True)
    switch = jnp.where(lane == 2 * experts, 1.0 / (1.0 + jnp.exp(-scores)), 0.0)
    values = probs * picked_ref[...] + switch
    high = values.astype(BF).astype(F32)
    rest = pltpu.roll(values - high, experts, 1)
    residual_ref[...] = residual
    routing_ref[...] = probs + switch
    sent_ref[:, :width] = h
    sent_ref[:, width:] = (high + rest).astype(BF)


def routing(experts, x, own, ahead, behind, gain, head, picked, time=0):
    rows, width = x.shape
    return pl.pallas_call(
        functools.partial(routing_kernel, experts),
        out_shape=(
            jax.ShapeDtypeStruct((rows, width), F32),
            jax.ShapeDtypeStruct((rows, width + 128), BF),
            jax.ShapeDtypeStruct((rows, 128), F32),
        ),
        in_specs=[WHOLE] * 7,
        out_specs=(WHOLE,) * 3,
        compiler_params=params(40),
        cost_estimate=cost(time),
        name="routing",
    )(x, own, ahead, behind, gain, head, picked)


def shards(
    tokens,
    attention_gain,
    query_weight,
    query_bias,
    key_weight,
    key_bias,
    value_weight,
    value_bias,
    output_weight,
    feedforward_gain,
    shared_gate_weight,
    shared_up_weight,
    shared_down_weight,
    shared_switch,
    router_weight,
    expert_in,
    expert_out,
    routes,
    cotangent,
):
    tok_rows, model_width = tokens.shape
    groups = lax.axis_size("expert")
    me = lax.axis_index("expert").astype(jnp.int32)[None]
    ring = Ring(groups)
    length = tok_rows * groups
    experts = router_weight.shape[1]
    weight_in = expert_in[0]
    weight_out = expert_out[0]
    weight_gate = shared_gate_weight.T
    weight_up = shared_up_weight.T
    weight_down = shared_down_weight.T
    x_float = tokens.astype(F32)
    rms_attn = rms_scale(x_float)
    unit_attn = x_float * rms_attn
    gain_attn = attention_gain.astype(F32)
    h_attn = (unit_attn * gain_attn).astype(BF)

    lanes = jnp.arange(128, dtype=jnp.int32)
    picked = jnp.sum((routes[:, :, None] == lanes).astype(F32), 1)
    head = jnp.concatenate(
        [
            router_weight.T,
            jnp.zeros((experts, model_width), BF),
            shared_switch[None],
            jnp.zeros((127 - 2 * experts, model_width), BF),
        ],
        0,
    )

    gather_attn = Gather(ring, h_attn)
    last = gather_attn.step()
    tables = rope_tables(length)
    last = gather_attn.step(tables, head, picked)
    h_attn_parts = gather_attn.rest()
    gather_cot = Gather(ring, after(cotangent, *gather_attn.pieces[-2:]))
    of_cot = gather_cot.step()

    q_rot, k_rot, v_low, *h_attn_split, h_attn_all = project(
        ring,
        h_attn_parts,
        (query_weight, key_weight, value_weight),
        (query_bias, key_bias, value_bias),
        tables,
    )
    att_low = attend(ring, q_rot, k_rot, v_low)
    sum_att = Scatter(
        ring, [right_dot(after(att_low, of_cot), output_weight).astype(BF)], tok_rows
    )
    backs = []
    cotangent_split = []

    def next_back(*others):
        which = len(backs)
        parts = after(gather_cot.chunk(which), *others)
        new = back_units(ring, which, parts, weight_out, weight_down, cotangent_split)
        cotangent_split[:] = new[2:]
        backs.append(new[:2])
        return new[:2]

    befores = [sum_att.chunks, move(ring, [sum_att, gather_cot])]
    while sum_att.at:
        busy = next_back(befores[-2])
        rounds = [sum_att] + [gather_cot] * (gather_cot.at < ring.half)
        befores.append(move(ring, rounds, busy))
    busy = next_back(befores[-2])

    residual, h_sent, routed = routing(
        experts,
        tokens,
        sum_att.own(0),
        sum_att.ahead,
        after(sum_att.behind, busy),
        feedforward_gain[None],
        head,
        picked,
    )

    gather_ffn = Gather(ring, h_sent)
    last = gather_ffn.step()
    busy = ()
    smalls = []
    kept = []

    def next_units(*others):
        which = len(smalls)
        parts = after(gather_ffn.chunk(which), *others)
        small, *new = hidden_units(
            ring,
            which,
            me,
            experts,
            parts,
            weight_in,
            weight_gate,
            weight_up,
            *backs[which],
            kept,
        )
        kept[:] = new
        smalls.append(small)
        return small

    while gather_ffn.at < ring.half:
        last = gather_ffn.step(busy)
        busy = next_units()
    next_units()
    hid_e, hid_s, grad_joined, grad_shared, *h_ffn_split = kept

    def chunk_in(which, time, *others):
        return units_in(
            which,
            *after((grad_joined, grad_shared), *others),
            smalls[which],
            weight_in,
            weight_gate,
            weight_up,
            time,
        )

    out_e = PairSum([cotangent_split], [hid_e])
    out_s = PairSum([cotangent_split], [hid_s])
    in_e = PairSum([h_ffn_split], [grad_joined])
    in_s = PairSum([h_ffn_split], [grad_shared])
    half_rows = length // 2

    def layer_rows(low, time, *others):
        return layer_part(
            low, low + half_rows, *after((hid_e, hid_s), *others), weight_out, weight_down, time
        )

    chunks = [None] * ring.half
    layer_parts = [None, None]
    busy = in_e.cores()
    chunks[-1] = chunk_in(ring.half - 1, 70, busy)
    sum_ffn = Scatter(ring, chunks, tok_rows)
    befores = [chunks[-1], sum_ffn.step()]
    busy = chunks[-1]
    works = [(6, in_e.chips), (6, out_e.cores), (12, out_s.cores)]
    for at, which in enumerate(range(ring.half - 2, -1, -1)):
        time, work = works[at] if at < len(works) else (6, None)
        chunks[which] = chunk_in(which, time, busy, befores[-2])
        busy = chunks[which]
        if work is not None:
            busy = (busy, work(busy))
        befores.append(sum_ffn.step(busy))
    layer_parts[1] = layer_rows(half_rows, 12, befores[-2], busy)

    grad_residual, attention_grad, score_rows, grad_ffn_gain_part = past_units(
        experts,
        residual,
        after(sum_ffn.own(0), layer_parts[1]),
        sum_ffn.ahead,
        sum_ffn.behind,
        cotangent,
        feedforward_gain[None],
        head,
        routed,
        picked,
        h_sent,
    )

    gather_grad = Gather(ring, attention_grad)
    first = gather_grad.step()
    layer_parts[0] = layer_rows(0, 12, attention_grad)
    busy = out_e.chips(layer_parts[0])
    second = gather_grad.step(busy)
    totals = in_e.total(first, busy, time=7.5)
    busy = out_s.chips(totals)
    third = gather_grad.step(busy)
    busy = in_s.cores(second, busy, time=7.5)
    last = gather_grad.step(busy)
    while gather_grad.at < ring.half:
        last = gather_grad.step()
    attention_grad_parts = gather_grad.rest()
    sum_layer = Scatter(ring, layer_parts, tok_rows)
    of_layer = sum_layer.step(last)
    grad_att, *grad_split = reorder_dot(
        ring, after(attention_grad_parts, totals), output_weight
    )
    grads, biases = attend_back(ring, q_rot, k_rot, v_low, grad_att, tables)
    attn_part, gain_part = attend_in(
        after(grads, of_layer),
        (query_weight, key_weight, value_weight),
        h_attn_all,
        gain_attn[None],
    )
    sum_attn = Scatter(ring, [attn_part], tok_rows)
    first = move(ring, [sum_attn, sum_layer])

    sums = jnp.concatenate(
        [
            gain_part,
            score_rows[2 * experts : 2 * experts + 1],
            grad_ffn_gain_part,
            score_rows[:experts],
        ],
        0,
    )
    in_qkvo = PairSum([h_attn_split, grad_split], [grads, att_low])
    packed = jnp.concatenate([sums.reshape(-1), biases[0]]).reshape(-1, 128)
    for axis, moves in cube_steps("dp"):
        packed = packed + lax.ppermute(packed, axis, moves)
    totals += out_e.total(attn_part, time=6)
    busy = in_qkvo.cores(totals)
    sums = packed.reshape(-1)[: sums.size].reshape(sums.shape)
    rounds = [sum_attn, sum_layer]
    befores = [attn_part, first]
    shared_cols = shared_gate_weight.shape[1]
    while sum_layer.at:
        befores.append(move(ring, rounds, busy))
        if len(befores) == 3:
            busy = in_s.chips(befores[-2], busy, time=6)
            totals += out_s.total(busy, turned_rows=shared_cols)
            busy = totals
        elif len(befores) == 4:
            busy = in_qkvo.chips(befores[-2], totals, time=6)
    last = sum_attn.step()
    totals += in_s.total(befores[-1], busy, time=3, outs=2, turned_rows=shared_cols)
    while sum_attn.at:
        last = sum_attn.step()
    for axis, moves in cube_steps("expert"):
        sums = sums + lax.ppermute(after(sums, last), axis, moves)
    biases = packed.reshape(-1)[sums.size :].reshape(3, -1)

    layer_out = (residual + sum_layer.rest()).astype(BF)
    grad_attn_in = sum_attn.rest()
    grad_unit_attn = grad_attn_in * gain_attn
    grad_tokens = grad_residual + rms_attn * (
        grad_unit_attn - unit_attn * jnp.mean(grad_unit_attn * unit_attn, -1, keepdims=True)
    )
    qkv = in_qkvo.total(last, outs=4)
    return (
        layer_out,
        grad_tokens,
        sums[0],
        qkv[0],
        biases[0],
        qkv[1],
        biases[1],
        qkv[2],
        biases[2],
        qkv[3],
        sums[2],
        totals[3].T,
        totals[4].T,
        totals[2].T,
        sums[1],
        sums[3:].T,
        totals[0][None],
        totals[1][None],
    )


def solution(mesh):
    return jax.shard_map(
        shards,
        mesh=mesh,
        in_specs=(
            P(("dp", "expert"), None),
            P(),
            P(None, "expert"),
            P("expert"),
            P(None, "expert"),
            P("expert"),
            P(None, "expert"),
            P("expert"),
            P(None, "expert"),
            P(),
            P(None, "expert"),
            P(None, "expert"),
            P(None, "expert"),
            P(),
            P(),
            P("expert", None, None),
            P("expert", None, None),
            P(("dp", "expert"), None),
            P(("dp", "expert"), None),
        ),
        out_specs=(
            P(("dp", "expert"), None),
            P(("dp", "expert"), None),
            P(),
            P("dp", "expert"),
            P("expert"),
            P("dp", "expert"),
            P("expert"),
            P("dp", "expert"),
            P("expert"),
            P("dp", "expert"),
            P(),
            P("dp", "expert"),
            P("dp", "expert"),
            P("dp", "expert"),
            P(),
            P(),
            P("expert", "dp", None),
            P("expert", "dp", None),
        ),
        check_vma=False,
    )
```

```python
import functools

import jax
import jax.numpy as jnp
from jax import lax
from jax.experimental import pallas as pl
from jax.experimental.pallas import tpu as pltpu
from jax.sharding import PartitionSpec as P

HD = 128
EPSILON = 1e-06
THETA = 1000000.0
BF = jnp.bfloat16
F32 = jnp.float32


def rope_tables(length):
    middle = HD // 2
    inverse = THETA ** (-(jnp.arange(middle, dtype=F32) * 2.0 / HD))
    angles = jnp.arange(length, dtype=F32)[:, None] * inverse[None, :]
    sine = jnp.sin(angles)
    return (jnp.concatenate([jnp.cos(angles)] * 2, -1), jnp.concatenate([-sine, sine], -1))


def rms_scale(values):
    return lax.rsqrt(jnp.mean(values * values, -1, keepdims=True) + EPSILON)


def plain_dot(left_side, right_side):
    return jnp.dot(left_side, right_side, preferred_element_type=F32)


def right_dot(left_side, right_side):
    return lax.dot_general(
        left_side, right_side, (((1,), (1,)), ((), ())), preferred_element_type=F32
    )


def left_dot(left_side, right_side):
    return lax.dot_general(
        left_side, right_side, (((0,), (0,)), ((), ())), preferred_element_type=F32
    )


def ring_order(count):
    wide = 2 if count <= 8 else 4
    tall = count // wide
    order = [z * wide for z in range(tall)]
    for z in range(tall - 1, -1, -1):
        row = list(range(1, wide))
        if (tall - 1 - z) % 2:
            row = row[::-1]
        order += [z * wide + x for x in row]
    return order


class Ring:
    def __init__(self, count):
        self.count = count
        self.half = count // 2
        place = lax.axis_index("dp").astype(jnp.int32)
        self.core = jnp.stack([place % 2, place // 2])
        order = ring_order(count)
        self.forward = [(order[i], order[(i + 1) % count]) for i in range(count)]
        self.backward = [(order[i], order[(i - 1) % count]) for i in range(count)]
        place = [0] * count
        for at, device in enumerate(order):
            place[device] = at
        distances = []
        for step in range(1, self.half):
            distances += [-step, step]
        distances += [0, self.half]
        here = jnp.array(place, jnp.int32)[lax.axis_index("expert")]
        around = (here + jnp.array(distances, jnp.int32) + count) % count
        self.block_of_slot = jnp.array(order, jnp.int32)[around]
        hits = self.block_of_slot[None, :] == jnp.arange(count, dtype=jnp.int32)[:, None]
        self.slot_of_block = jnp.sum(hits * jnp.arange(count, dtype=jnp.int32)[None, :], 1)

    def slot(self, distance):
        if distance in (0, self.half):
            return self.count - 2 + (distance > 0)
        return 2 * abs(distance) - 2 + (distance > 0)


def after(values, *others):
    return lax.optimization_barrier((values, others))[0]


def move(ring, rounds, *others):
    up, down = zip(*[each.outgoing() for each in rounds])
    rows = [piece.shape[0] for piece in up]
    if len(rounds) > 1:
        up, down = jnp.concatenate(up, 0), jnp.concatenate(down, 0)
    else:
        up, down = up[0], down[0]
    up, down = after((up, down), *others)
    ahead = lax.ppermute(up, "expert", ring.forward)
    behind = lax.ppermute(down, "expert", ring.backward)
    at = 0
    for each, count in zip(rounds, rows):
        if len(rounds) > 1:
            each.arrive(ahead[at : at + count], behind[at : at + count])
        else:
            each.arrive(ahead, behind)
        at += count
    return (ahead, behind)


class Gather:
    def __init__(self, ring, block):
        self.ring = ring
        self.pieces = [block]
        self.ahead = self.behind = block
        self.at = 0

    def outgoing(self):
        self.at += 1
        if self.at < self.ring.half:
            return self.ahead, self.behind
        middle = self.pieces[0].shape[0] // 2
        return self.ahead[:middle], self.behind[middle:]

    def arrive(self, ahead, behind):
        self.ahead, self.behind = ahead, behind
        self.pieces += [ahead, behind]

    def step(self, *others):
        return move(self.ring, [self], *others)

    def chunk(self, which):
        if which < self.ring.half - 1:
            return self.pieces[2 * which + 1 : 2 * which + 3]
        return [self.pieces[0]] + self.pieces[-2:]

    def rest(self):
        while self.at < self.ring.half:
            self.step()
        return self.pieces[1:-2] + [self.pieces[0]] + self.pieces[-2:]


class Scatter:
    def __init__(self, ring, chunks, rows):
        self.ring = ring
        self.chunks = chunks
        self.rows = rows
        self.at = ring.half

    def own(self, distance):
        slot = self.ring.slot(distance)
        slots = self.ring.count // len(self.chunks)
        start = slot % slots * self.rows
        return self.chunks[slot // slots][start : start + self.rows]

    def outgoing(self):
        middle = self.rows // 2
        at = self.at
        self.at -= 1
        if at == self.ring.half:
            far = self.own(at)
            return far[:middle], far[middle:]
        up = self.own(at).astype(F32)
        down = self.own(-at).astype(F32)
        if at == self.ring.half - 1:
            up = jnp.concatenate([up[:middle] + self.ahead.astype(F32), up[middle:]], 0)
            down = jnp.concatenate([down[:middle], down[middle:] + self.behind.astype(F32)], 0)
        else:
            up = up + self.ahead.astype(F32)
            down = down + self.behind.astype(F32)
        return up.astype(BF), down.astype(BF)

    def arrive(self, ahead, behind):
        self.ahead, self.behind = ahead, behind

    def step(self, *others):
        return move(self.ring, [self], *others)

    def rest(self, *others):
        while self.at:
            self.step()
        return after(self.own(0), *others).astype(F32) + self.ahead.astype(F32) + self.behind.astype(F32)


def cube_steps(axis):
    count = lax.axis_size(axis)
    step, moves = 1, []
    while step < count:
        moves.append((axis, [(i, i ^ step) for i in range(count)]))
        step *= 2
    return moves


class PairSum:
    def __init__(self, splits, rights):
        self.splits = splits
        self.rights = rights
        self.tall = len(splits[0]) - 1

    def lefts(self, which, *others):
        return after([split[which] for split in self.splits], *others)

    def cores(self, *others, time=0):
        count = lax.axis_size("dp")
        (sent,) = pair_dot(self.lefts(0, *others), self.rights, [], BF, 1, time)
        self.arrived = lax.ppermute(sent, "dp", [(i, i ^ 1) for i in range(count)])
        return sent

    def chips(self, *others, time=0):
        count = lax.axis_size("dp")
        size = self.splits[0][1].shape[1]
        self.parts = []
        out = others
        for step in range(1, self.tall):
            adds = [(self.arrived, step * size)]
            (out,) = pair_dot(self.lefts(1 + step, *others), self.rights, adds, BF, 1, time)
            moves = [(i, (i // 2 + step) % self.tall * 2 + i % 2) for i in range(count)]
            self.parts.append(lax.ppermute(out, "dp", moves))
        return out

    def total(self, *others, time=0, outs=1, turned_rows=0):
        adds = [(self.arrived, 0)] + [(part, 0) for part in self.parts]
        lefts = self.lefts(1, *others)
        return pair_dot(lefts, self.rights, adds, F32, outs, time, turned_rows)


WHOLE = pl.BlockSpec(memory_space=pltpu.VMEM)
ANY = pl.BlockSpec(memory_space=pl.ANY)
SCALARS = pl.BlockSpec(memory_space=pltpu.SMEM)


class Copies:
    def __init__(self, sems):
        self.sems = sems
        self.count = 0

    def start(self, source, target):
        copy = pltpu.make_async_copy(source, target, self.sems.at[self.count])
        self.count += 1
        copy.start()
        return copy


def tiles_of(columns, wide):
    return [(low, min(low + wide, columns)) for low in range(0, columns, wide)]


def bring(copies, pieces, rows_ref):
    at, started = 0, []
    for piece in pieces:
        rows = slice(at, at + piece.shape[0])
        started.append(copies.start(piece, rows_ref.at[rows]))
        at += piece.shape[0]
    return started


def chunks_of(pieces, brought, wide):
    at, left = 0, list(zip(pieces, brought))
    for low in range(0, sum(piece.shape[0] for piece in pieces), wide):
        waits = []
        while left and at < low + wide:
            piece, copy = left.pop(0)
            at += piece.shape[0]
            waits.append(copy)
        yield slice(low, low + wide), waits


def params(mebibytes):
    return pltpu.CompilerParams(vmem_limit_bytes=mebibytes * 1024 * 1024)


def cost(time):
    return pl.CostEstimate(flops=int(1e9 * time) + 1, bytes_accessed=1, transcendentals=0)


def split_shapes(rows, width):
    count = lax.axis_size("dp")
    widths = [width // 2] + [width // count] * (count // 2)
    return tuple(jax.ShapeDtypeStruct((rows, w), BF) for w in widths)


def put_split(place, row_ref, refs, rows=slice(None)):
    core, far = place[0], place[1]
    other_ref, own_refs = refs[0], refs[1:]
    columns, tall = own_refs[0].shape[1], len(own_refs)
    for part in range(tall):
        chip = lax.rem(far + part, tall)
        at = pl.multiple_of((2 * chip + 1 - core) * columns, columns)
        there = slice(part * columns, (part + 1) * columns)
        other_ref[rows, there] = row_ref[rows, pl.ds(at, columns)]
        at = pl.multiple_of((2 * chip + core) * columns, columns)
        own_refs[part][rows, :] = row_ref[rows, pl.ds(at, columns)]


def turned(values, cosine, sine):
    return values * cosine + pltpu.roll(values, HD // 2, 1) * sine


def project_kernel(pieces, splits, places, place, *refs):
    parts, refs = refs[:pieces], refs[pieces:]
    hbm, refs = refs[:8], refs[8:]
    outs, refs = refs[:3], refs[3:]
    split_hbm, refs = refs[: splits + 1], refs[splits + 1 :]
    q_ref, k_ref, v_ref = outs
    h_ref, refs = refs[0], refs[1:]
    split_ref, refs = refs[:splits], refs[splits:]
    w_ref, bq, bk, bv, cos, sin, sems = refs
    cols = bq.shape[1]
    copies = Copies(sems)
    targets = [w_ref.at[:, at * cols : (at + 1) * cols] for at in range(3)]
    of_weights = [copies.start(a, b) for a, b in zip(hbm, targets + [bq, bk, bv, cos, sin])]
    brought = bring(copies, parts, h_ref)
    block_rows = h_ref.shape[0] // places.shape[0]
    for copy in of_weights:
        copy.wait()
    kept = []
    sources = [h_ref] + list(split_ref)
    targets = [split_hbm[-1]] + list(split_hbm[:-1])
    for chunk, waits in chunks_of(parts, brought, 2 * block_rows):
        for copy in waits:
            copy.wait()
        put_split(place, h_ref, split_ref, chunk)
        kept += [copies.start(a.at[chunk], b.at[chunk]) for a, b in zip(sources, targets)]
        qkv = plain_dot(h_ref[chunk], w_ref[...])
        q = qkv[:, :cols] + bq[...].astype(F32)
        k = qkv[:, cols : 2 * cols] + bk[...].astype(F32)
        v = qkv[:, 2 * cols :] + bv[...].astype(F32)
        for part in range(2):
            start = places[chunk.start // block_rows + part] * block_rows
            rows = pl.ds(pl.multiple_of(start, block_rows), block_rows)
            near = slice(part * block_rows, (part + 1) * block_rows)
            cosine, sine = cos[rows, :], sin[rows, :]
            for head in range(cols // HD):
                hs = slice(head * HD, (head + 1) * HD)
                q_ref[rows, hs] = turned(q[near, hs], cosine, sine).astype(BF)
                k_ref[rows, hs] = turned(k[near, hs], cosine, sine).astype(BF)
            v_ref[rows, :] = v[near].astype(BF)
    for copy in kept:
        copy.wait()


def project(ring, parts, weights, biases, tables, time=3):
    width, cols = weights[0].shape
    length = sum(part.shape[0] for part in parts)
    shape = jax.ShapeDtypeStruct((length, cols), BF)
    split = split_shapes(length, width)
    pieces = len(parts)
    return pl.pallas_call(
        functools.partial(project_kernel, pieces, len(split)),
        out_shape=(shape,) * 3 + split + (jax.ShapeDtypeStruct((length, width), BF),),
        in_specs=[SCALARS] * 2 + [ANY] * (pieces + 8),
        out_specs=(WHOLE,) * 3 + (ANY,) * (len(split) + 1),
        scratch_shapes=[pltpu.VMEM((length, width), BF)]
        + [pltpu.VMEM(part.shape, BF) for part in split]
        + [pltpu.VMEM((width, 3 * cols), BF)]
        + [pltpu.VMEM((1, cols), BF)] * 3
        + [pltpu.VMEM((length, HD), F32)] * 2
        + [pltpu.SemaphoreType.DMA((pieces + 8 + ring.half * (len(split) + 1),))],
        compiler_params=params(52),
        cost_estimate=cost(time),
        name="project",
    )(ring.block_of_slot, ring.core, *parts, *weights, *[b[None] for b in biases], *tables)


def bring_all(sources, targets, sems):
    copies = Copies(sems)
    for copy in [copies.start(source, target) for source, target in zip(sources, targets)]:
        copy.wait()


def attend_kernel(
    block_rows, wide, slots, q_hbm, k_hbm, v_hbm, out_ref, q_ref, k_ref, v_ref, sems
):
    bring_all((q_hbm, k_hbm, v_hbm), (q_ref, k_ref, v_ref), sems)
    length, cols = q_ref.shape
    scale = HD ** (-0.5)
    at_row = lax.broadcasted_iota(jnp.int32, (wide, wide), 0)
    at_col = lax.broadcasted_iota(jnp.int32, (wide, wide), 1)
    allowed = at_col <= at_row
    for head in range(cols // HD):
        hs = slice(head * HD, (head + 1) * HD)
        for i in range(length // wide):
            low, high = i * wide, (i + 1) * wide
            q = q_ref[low:high, hs]
            near = right_dot(q, k_ref[low:high, hs]) * scale
            near = jnp.where(allowed, near, -jnp.inf)
            peak = jnp.max(near, 1, keepdims=True)
            if i:
                past = right_dot(q, k_ref[:low, hs]) * scale
                peak = jnp.maximum(peak, jnp.max(past, 1, keepdims=True))
                past = jnp.exp(past - peak)
            near = jnp.exp(near - peak)
            total = jnp.sum(near, 1, keepdims=True)
            if i:
                total = total + jnp.sum(past, 1, keepdims=True)
            share = 1.0 / total
            out = plain_dot((near * share).astype(BF), v_ref[low:high, hs])
            if i:
                out = out + plain_dot((past * share).astype(BF), v_ref[:low, hs])
            out = out.astype(BF)
            for part in range(wide // block_rows):
                slot = slots[i * (wide // block_rows) + part]
                rows = pl.ds(pl.multiple_of(slot * block_rows, block_rows), block_rows)
                out_ref[rows, hs] = out[part * block_rows : (part + 1) * block_rows]


def attend(ring, q, k, v, time=3):
    length, cols = q.shape
    return pl.pallas_call(
        functools.partial(attend_kernel, length // ring.count, 2 * (length // ring.count)),
        out_shape=jax.ShapeDtypeStruct((length, cols), BF),
        in_specs=[SCALARS] + [ANY] * 3,
        out_specs=WHOLE,
        scratch_shapes=[pltpu.VMEM((length, cols), BF)] * 3 + [pltpu.SemaphoreType.DMA((3,))],
        compiler_params=params(40),
        cost_estimate=cost(time),
        name="attend",
    )(ring.slot_of_block, q, k, v)


def attend_back_kernel(
    block_rows, wide, slots, q_hbm, k_hbm, v_hbm, g_hbm, cos_hbm, sin_hbm, out_ref, bias_ref,
    q_ref, k_ref, v_ref, g_ref, cos, sin, k_sum, v_sum, sems,
):
    sources = (q_hbm, k_hbm, v_hbm, g_hbm, cos_hbm, sin_hbm)
    bring_all(sources, (q_ref, k_ref, v_ref, g_ref, cos, sin), sems)
    length, cols = q_ref.shape
    scale = HD ** (-0.5)
    at_key = lax.broadcasted_iota(jnp.int32, (wide, wide), 0)
    at_query = lax.broadcasted_iota(jnp.int32, (wide, wide), 1)
    allowed = at_key <= at_query
    per = wide // block_rows
    bias_ref[...] = jnp.zeros_like(bias_ref)

    def put(which, low, head, values):
        hs = slice(which * cols + head * HD, which * cols + (head + 1) * HD)
        values = values.astype(BF)
        bias_ref[:, hs] += jnp.sum(values.astype(F32), 0, keepdims=True)
        for part in range(per):
            slot = slots[low // block_rows + part]
            rows = pl.ds(pl.multiple_of(slot * block_rows, block_rows), block_rows)
            out_ref[rows, hs] = values[part * block_rows : (part + 1) * block_rows]

    def back(values, low, high):
        return values * cos[low:high] - pltpu.roll(values, HD // 2, 1) * sin[low:high]

    for head in range(cols // HD):
        hs = slice(head * HD, (head + 1) * HD)
        for i in range(length // wide):
            low, high = i * wide, (i + 1) * wide
            q = q_ref[low:high, hs]
            g = g_ref[low:high, hs]
            spans = [(low, high)] + ([(0, low)] if i else [])
            scores = [right_dot(k_ref[a:b, hs], q) * scale for a, b in spans]
            scores[0] = jnp.where(allowed, scores[0], -jnp.inf)
            peak = functools.reduce(jnp.maximum, [jnp.max(s, 0, keepdims=True) for s in scores])
            probs = [jnp.exp(s - peak) for s in scores]
            total = sum(jnp.sum(p, 0, keepdims=True) for p in probs)
            share = 1.0 / total
            probs = [p * share for p in probs]
            grads = [right_dot(v_ref[a:b, hs], g) for a, b in spans]
            mean = sum(jnp.sum(p * d, 0, keepdims=True) for p, d in zip(probs, grads))
            draws = [(p * (d - mean) * scale).astype(BF) for p, d in zip(probs, grads)]
            dq = sum(left_dot(d, k_ref[a:b, hs]) for d, (a, b) in zip(draws, spans))
            put(0, low, head, back(dq, low, high))
            for at, (a, b) in enumerate(spans):
                dv = plain_dot(probs[at].astype(BF), g)
                dk = plain_dot(draws[at], q)
                if at == 0:
                    v_sum[a:b, hs] = dv
                    k_sum[a:b, hs] = dk
                else:
                    v_sum[a:b, hs] += dv
                    k_sum[a:b, hs] += dk
        for i in range(length // wide):
            low, high = i * wide, (i + 1) * wide
            put(1, low, head, back(k_sum[low:high, hs], low, high))
            put(2, low, head, v_sum[low:high, hs])


def attend_back(ring, q, k, v, grad, tables, time=20):
    length, cols = q.shape
    return pl.pallas_call(
        functools.partial(attend_back_kernel, length // ring.count, 2 * (length // ring.count)),
        out_shape=(
            jax.ShapeDtypeStruct((length, 3 * cols), BF),
            jax.ShapeDtypeStruct((1, 3 * cols), F32),
        ),
        in_specs=[SCALARS] + [ANY] * 6,
        out_specs=(WHOLE,) * 2,
        scratch_shapes=[pltpu.VMEM((length, cols), BF)] * 4
        + [pltpu.VMEM((length, HD), F32)] * 2
        + [pltpu.VMEM((length, cols), F32)] * 2
        + [pltpu.SemaphoreType.DMA((6,))],
        compiler_params=params(48),
        cost_estimate=cost(time),
        name="attend_back",
    )(ring.slot_of_block, q, k, v, grad, *tables)


def attend_in_kernel(
    d_hbm, wq_hbm, wk_hbm, wv_hbm, h_hbm, gain_ref, out_hbm, gain_out,
    d_ref, wq_ref, wk_ref, wv_ref, h_ref, out_ref, sems,
):
    cols = wq_ref.shape[1]
    copies = Copies(sems)
    of_d = copies.start(d_hbm, d_ref)
    tiles = tiles_of(h_ref.shape[1], 512)
    weights = ((wq_hbm, wq_ref), (wk_hbm, wk_ref), (wv_hbm, wv_ref))
    of_tiles = [
        [copies.start(a.at[low:high], b.at[low:high]) for a, b in weights]
        + [copies.start(h_hbm.at[:, low:high], h_ref.at[:, low:high])]
        for low, high in tiles
    ]
    of_d.wait()
    kept = []
    for started, (low, high) in zip(of_tiles, tiles):
        for copy in started[:-1]:
            copy.wait()
        out = right_dot(d_ref[:, :cols], wq_ref[low:high])
        out = out + right_dot(d_ref[:, cols : 2 * cols], wk_ref[low:high])
        out = out + right_dot(d_ref[:, 2 * cols :], wv_ref[low:high])
        out_ref[:, low:high] = out.astype(BF)
        kept.append(copies.start(out_ref.at[:, low:high], out_hbm.at[:, low:high]))
        started[-1].wait()
        products = out * h_ref[:, low:high].astype(F32)
        gain_out[:, low:high] = jnp.sum(products, 0, keepdims=True) / gain_ref[:, low:high]
    for copy in kept:
        copy.wait()


def attend_in(grads, weights, h_all, gain, time=1):
    length, cols = grads.shape
    width = h_all.shape[1]
    return pl.pallas_call(
        attend_in_kernel,
        out_shape=(
            jax.ShapeDtypeStruct((length, width), BF),
            jax.ShapeDtypeStruct((1, width), F32),
        ),
        in_specs=[ANY] * 5 + [WHOLE],
        out_specs=(ANY, WHOLE),
        scratch_shapes=[pltpu.VMEM((length, cols), BF)]
        + [pltpu.VMEM((width, cols // 3), BF)] * 3
        + [
            pltpu.VMEM((length, width), BF),
            pltpu.VMEM((length, width), BF),
            pltpu.SemaphoreType.DMA((1 + 5 * len(tiles_of(width, 512)),)),
        ],
        compiler_params=params(48),
        cost_estimate=cost(time),
        name="attend_in",
    )(grads, *weights, h_all, gain)


def reorder_dot_kernel(pieces, splits, places, place, *refs):
    parts, refs = refs[:pieces], refs[pieces:]
    w_hbm, out_ref, refs = refs[0], refs[1], refs[2:]
    split_hbm, refs = refs[:splits], refs[splits:]
    h_ref, split_ref, w_ref = refs[0], refs[1 : 1 + splits], refs[1 + splits]
    copies = Copies(refs[-1])
    of_weight = copies.start(w_hbm, w_ref)
    brought = bring(copies, parts, h_ref)
    block_rows = h_ref.shape[0] // places.shape[0]
    of_weight.wait()
    kept = []
    for chunk, waits in chunks_of(parts, brought, 2 * block_rows):
        for copy in waits:
            copy.wait()
        put_split(place, h_ref, split_ref, chunk)
        kept += [copies.start(a.at[chunk], b.at[chunk]) for a, b in zip(split_ref, split_hbm)]
        out = plain_dot(h_ref[chunk], w_ref[...]).astype(BF)
        for part in range(2):
            start = places[chunk.start // block_rows + part] * block_rows
            rows = pl.ds(pl.multiple_of(start, block_rows), block_rows)
            out_ref[rows, :] = out[part * block_rows : (part + 1) * block_rows]
    for copy in kept:
        copy.wait()


def reorder_dot(ring, parts, weight, time=10):
    width, cols = weight.shape
    length = sum(part.shape[0] for part in parts)
    split = split_shapes(length, width)
    pieces = len(parts)
    return pl.pallas_call(
        functools.partial(reorder_dot_kernel, pieces, len(split)),
        out_shape=(jax.ShapeDtypeStruct((length, cols), BF),) + split,
        in_specs=[SCALARS] * 2 + [ANY] * (pieces + 1),
        out_specs=(WHOLE,) + (ANY,) * len(split),
        scratch_shapes=[pltpu.VMEM((length, width), BF)]
        + [pltpu.VMEM(part.shape, BF) for part in split]
        + [
            pltpu.VMEM((width, cols), BF),
            pltpu.SemaphoreType.DMA((pieces + 1 + ring.half * len(split),)),
        ],
        compiler_params=params(52),
        cost_estimate=cost(time),
        name="reorder_dot",
    )(ring.block_of_slot, ring.core, *parts, weight)


def gated(gate_pre, up_pre, back, scale):
    sigmoid = 0.5 + 0.5 * jnp.tanh(0.5 * gate_pre)
    silu = gate_pre * sigmoid
    hidden = silu * up_pre
    scaled = scale * back
    grad_gate = scaled * up_pre * (sigmoid + silu * (1.0 - sigmoid))
    return hidden, scale * hidden, grad_gate, scaled * silu


def back_kernel(pieces, which, split, place, *refs):
    parts, refs = refs[:pieces], refs[pieces:]
    wo_hbm, wd_hbm = refs[:2]
    refs = refs[-(2 * split + 6) :]
    back_e_ref, back_s_ref = refs[:2]
    kept_hbm, kept_ref = refs[2 : 2 + split], refs[2 + split : 2 + 2 * split]
    rows_ref, wo_ref, wd_ref, sems = refs[-4:]
    rows, width = rows_ref.shape
    copies = Copies(sems)
    brought = bring(copies, parts, rows_ref)
    tiles = tiles_of(wo_ref.shape[1], 512)
    of_e = [copies.start(wo_hbm.at[:, a:b], wo_ref.at[:, a:b]) for a, b in tiles]
    of_s = copies.start(wd_hbm, wd_ref)
    for copy in brought:
        copy.wait()
    put_split(place, rows_ref, kept_ref)
    chunk = slice(which * rows, (which + 1) * rows)
    kept = [copies.start(ref, hbm.at[chunk]) for ref, hbm in zip(kept_ref, kept_hbm)]
    for copy, (a, b) in zip(of_e, tiles):
        copy.wait()
        back_e_ref[:, a:b] = plain_dot(rows_ref[...], wo_ref[:, a:b]).astype(BF)
    of_s.wait()
    back_s_ref[...] = right_dot(rows_ref[...], wd_ref[...]).astype(BF)
    for copy in kept:
        copy.wait()


def back_units(ring, which, parts, weight_out, weight_down, kept, time=6):
    width, units = weight_out.shape
    shared = weight_down.shape[0]
    rows = sum(part.shape[0] for part in parts)
    pieces = len(parts)
    first = pieces + 3
    split = split_shapes(rows * ring.half, width)
    return pl.pallas_call(
        functools.partial(back_kernel, pieces, which, len(split)),
        out_shape=(
            jax.ShapeDtypeStruct((rows, units), BF),
            jax.ShapeDtypeStruct((rows, shared), BF),
        )
        + split,
        in_specs=[SCALARS] + [ANY] * (pieces + 2 + len(kept)),
        out_specs=(WHOLE, WHOLE) + (ANY,) * len(split),
        scratch_shapes=[pltpu.VMEM((rows, part.shape[1]), BF) for part in split]
        + [
            pltpu.VMEM((rows, width), BF),
            pltpu.VMEM((width, units), BF),
            pltpu.VMEM((shared, width), BF),
            pltpu.SemaphoreType.DMA((pieces + len(tiles_of(units, 512)) + 1 + len(split),)),
        ],
        input_output_aliases={first + at: 2 + at for at in range(len(kept))},
        compiler_params=params(48),
        cost_estimate=cost(time),
        name="back_units",
    )(ring.core, *parts, weight_out, weight_down, *kept)


UNIT_TILE = 512


def units_kernel(pieces, which, experts, count, me_ref, place, *refs):
    parts, refs = refs[:pieces], refs[pieces:]
    wi_hbm, wg_hbm, wu_hbm, back_e_hbm, back_s_hbm = refs[:5]
    refs = refs[-(2 * count + 9) :]
    small_ref = refs[0]
    kept_hbm, kept_ref = refs[1 : 1 + count], refs[1 + count : 1 + 2 * count]
    hid_e_ref, hid_s_ref, both_ref, both_s_ref = kept_ref[:4]
    h_ref, wi_ref, wg_ref, wu_ref, back_e_ref, back_s_ref, sum_ref, sems = refs[-8:]
    rows = h_ref.shape[0]
    width, units = wi_ref.shape[0], wi_ref.shape[1] // 2
    me = me_ref[0]
    copies = Copies(sems)
    brought = bring(copies, parts, h_ref)
    tiles = tiles_of(units, UNIT_TILE)
    of_e = []
    for a, b in tiles:
        of_e.append(
            (
                copies.start(wi_hbm.at[:, a:b], wi_ref.at[:, 2 * a : a + b]),
                copies.start(wi_hbm.at[:, units + a : units + b], wi_ref.at[:, a + b : 2 * b]),
            )
        )
        if a == 0:
            of_back_e = copies.start(back_e_hbm, back_e_ref)
    of_s = [
        copies.start(wg_hbm, wg_ref),
        copies.start(wu_hbm, wu_ref),
        copies.start(back_s_hbm, back_s_ref),
    ]
    chunk = slice(which * rows, (which + 1) * rows)
    started = []

    def keep(*places):
        for at in places:
            started.append(copies.start(kept_ref[at], kept_hbm[at].at[chunk]))

    def scale_of(low, high):
        aux = h_ref[:, width:].astype(F32)
        lane = lax.broadcasted_iota(jnp.int32, aux.shape, 1)
        return jnp.sum(jnp.where((lane == low) | (lane == high), aux, 0.0), 1, keepdims=True)

    for copy in brought:
        copy.wait()
    put_split(place, h_ref, kept_ref[4:])
    keep(*range(4, count))
    gate = scale_of(me, experts + me)
    h = h_ref[:, :width]
    sum_ref[...] = jnp.zeros_like(sum_ref)
    for which_tile, (a, b) in enumerate(tiles):
        for copy in of_e[which_tile]:
            copy.wait()
        if a == 0:
            of_back_e.wait()
        both = plain_dot(h, wi_ref[:, 2 * a : 2 * b])
        back = back_e_ref[:, a:b].astype(F32)
        hidden, scaled, da, db = gated(both[:, : b - a], both[:, b - a :], back, gate)
        products = hidden * back
        for low in range(0, b - a, 128):
            sum_ref[...] += products[:, low : low + 128]
        hid_e_ref[:, a:b] = scaled.astype(BF)
        both_ref[:, a:b] = da.astype(BF)
        both_ref[:, units + a : units + b] = db.astype(BF)
    keep(0, 2)
    for copy in of_s:
        copy.wait()
    switch = scale_of(2 * experts, 3 * experts)
    back = back_s_ref[...].astype(F32)
    hidden, scaled, dg, du = gated(
        right_dot(h, wg_ref[...]), right_dot(h, wu_ref[...]), back, switch
    )
    hid_s_ref[...] = jnp.zeros_like(hid_s_ref)
    hid_s_ref[:, : scaled.shape[1]] = scaled.astype(BF)
    shared = dg.shape[1]
    both_s_ref[:, :shared] = dg.astype(BF)
    both_s_ref[:, shared:] = du.astype(BF)
    keep(1, 3)
    of_switch = jnp.sum(hidden * back, 1, keepdims=True)
    of_gate = jnp.sum(sum_ref[...], 1, keepdims=True)
    lane = lax.broadcasted_iota(jnp.int32, small_ref.shape, 1)
    small = jnp.zeros(small_ref.shape, F32)
    for value, first in ((of_gate, 0), (of_switch, 2 * experts)):
        high = value.astype(BF).astype(F32)
        small = small + jnp.where(lane == first + me, high, 0.0)
        small = small + jnp.where(lane == first + experts + me, value - high, 0.0)
    small_ref[...] = small.astype(BF)
    for copy in started:
        copy.wait()


def hidden_units(
    ring, which, me, experts, parts, weight_in, weight_gate, weight_up, back_e, back_s, kept,
    time=6,
):
    rows, units = back_e.shape
    shared = back_s.shape[1]
    width = weight_in.shape[0]
    pieces = len(parts)
    first = pieces + 7
    columns = [units, -(-shared // 128) * 128, 2 * units, 2 * shared]
    columns += [part.shape[1] for part in split_shapes(rows, width)]
    copies = pieces + 2 * len(tiles_of(units, UNIT_TILE)) + 4 + len(columns)
    return pl.pallas_call(
        functools.partial(units_kernel, pieces, which, experts, len(columns)),
        out_shape=(jax.ShapeDtypeStruct((rows, 128), BF),)
        + tuple(jax.ShapeDtypeStruct((rows * ring.half, c), BF) for c in columns),
        in_specs=[SCALARS] * 2 + [ANY] * (pieces + 5 + len(kept)),
        out_specs=(WHOLE,) + (ANY,) * len(columns),
        scratch_shapes=[pltpu.VMEM((rows, c), BF) for c in columns]
        + [
            pltpu.VMEM((rows, width + 128), BF),
            pltpu.VMEM((width, 2 * units), BF),
            pltpu.VMEM((shared, width), BF),
            pltpu.VMEM((shared, width), BF),
            pltpu.VMEM((rows, units), BF),
            pltpu.VMEM((rows, shared), BF),
            pltpu.VMEM((rows, 128), F32),
            pltpu.SemaphoreType.DMA((copies,)),
        ],
        input_output_aliases={first + at: 1 + at for at in range(len(kept))},
        compiler_params=params(52),
        cost_estimate=cost(time),
        name="hidden_units",
    )(
        me,
        ring.core,
        *parts,
        weight_in,
        weight_gate,
        weight_up,
        back_e,
        back_s,
        *kept,
    )


IN_TILE = 512


def units_in_kernel(
    which, both_hbm, both_s_hbm, small_ref, wi_hbm, wg_hbm, wu_hbm, out_ref,
    both_ref, both_s_ref, wi_ref, ws_ref, sems,
):
    rows = both_ref.shape[0]
    width, shared = wi_ref.shape[0], ws_ref.shape[0] // 2
    copies = Copies(sems)
    chunk = slice(which * rows, (which + 1) * rows)
    brought = [
        copies.start(both_hbm.at[chunk], both_ref),
        copies.start(both_s_hbm.at[chunk], both_s_ref),
    ]
    tiles = tiles_of(width, IN_TILE)
    weights = [
        [
            copies.start(wi_hbm.at[a:b], wi_ref.at[a:b]),
            copies.start(wg_hbm.at[:, a:b], ws_ref.at[:shared, a:b]),
            copies.start(wu_hbm.at[:, a:b], ws_ref.at[shared:, a:b]),
        ]
        for a, b in tiles
    ]
    out_ref[:, width:] = small_ref[...]
    for copy in brought:
        copy.wait()
    for started, (a, b) in zip(weights, tiles):
        for copy in started:
            copy.wait()
        out = right_dot(both_ref[...], wi_ref[a:b])
        out = out + plain_dot(both_s_ref[...], ws_ref[:, a:b])
        out_ref[:, a:b] = out.astype(BF)


def units_in(which, both, both_s, small, weight_in, weight_gate, weight_up, time):
    joined, joined_s = both.shape[1], both_s.shape[1]
    rows = small.shape[0]
    width = weight_in.shape[0]
    return pl.pallas_call(
        functools.partial(units_in_kernel, which),
        out_shape=jax.ShapeDtypeStruct((rows, width + 128), BF),
        in_specs=[ANY] * 2 + [WHOLE] + [ANY] * 3,
        out_specs=WHOLE,
        scratch_shapes=[
            pltpu.VMEM((rows, joined), BF),
            pltpu.VMEM((rows, joined_s), BF),
            pltpu.VMEM((width, joined), BF),
            pltpu.VMEM((joined_s, width), BF),
            pltpu.SemaphoreType.DMA((2 + 3 * len(tiles_of(width, IN_TILE)),)),
        ],
        compiler_params=params(48),
        cost_estimate=cost(time),
        name="units_in",
    )(both, both_s, small, weight_in, weight_gate, weight_up)


def pair_kernel(pairs, first_rows, outs, turned_rows, *refs):
    adds = len(first_rows)
    lefts_hbm, rights_hbm = refs[:pairs], refs[pairs : 2 * pairs]
    refs = refs[2 * pairs :]
    adds_hbm, outs_hbm = refs[:adds], refs[adds : adds + outs]
    refs = refs[adds + outs :]
    lefts_ref, rights_ref = refs[:pairs], refs[pairs : 2 * pairs]
    refs = refs[2 * pairs :]
    adds_ref, outs_ref = refs[:adds], refs[adds : adds + outs]
    copies = Copies(refs[-1])
    rows = lefts_ref[0].shape[1]
    tiles = pair_tiles([ref.shape[1] for ref in rights_ref], 1 if turned_rows else outs)
    of_lefts = [None] * pairs
    of_tiles = []
    for pair, low, a, b in tiles:
        if of_lefts[pair] is None:
            of_lefts[pair] = copies.start(lefts_hbm[pair], lefts_ref[pair])
        near = slice(a - low, b - low)
        started = [copies.start(rights_hbm[pair].at[:, near], rights_ref[pair].at[:, near])]
        for first, hbm, ref in zip(first_rows, adds_hbm, adds_ref):
            started.append(copies.start(hbm.at[first : first + rows, a:b], ref.at[:, a:b]))
        of_tiles.append(started)
    started = []
    for at, (pair, low, a, b) in enumerate(tiles):
        if of_lefts[pair] is not None:
            of_lefts[pair].wait()
            of_lefts[pair] = None
        for copy in of_tiles[at]:
            copy.wait()
        out = left_dot(lefts_ref[pair][...], rights_ref[pair][:, a - low : b - low])
        for ref in adds_ref:
            out = out + ref[:, a:b].astype(F32)
        if turned_rows:
            out = out.T
            for which, target in enumerate(outs_ref):
                low = which * turned_rows
                first, last = max(a, low), min(b, low + turned_rows)
                if first < last:
                    target[first - low : last - low] = out[first - a : last - a]
            continue
        wide = outs_ref[0].shape[1]
        target, hbm = outs_ref[a // wide], outs_hbm[a // wide]
        near = slice(a % wide, a % wide + b - a)
        target[:, near] = out.astype(target.dtype)
        started.append(copies.start(target.at[:, near], hbm.at[:, near]))
    if turned_rows:
        started = [copies.start(target, hbm) for target, hbm in zip(outs_ref, outs_hbm)]
    for copy in started:
        copy.wait()


def pair_tiles(widths, outs):
    wide = sum(widths) // outs
    tiles, low = [], 0
    for pair, width in enumerate(widths):
        a = low
        while a < low + width:
            b = min(a + 512, low + width, (a // wide + 1) * wide)
            tiles.append((pair, low, a, b))
            a = b
        low += width
    return tiles


def pair_dot(lefts, rights, adds, held, outs=1, time=0, turned_rows=0):
    length, rows = lefts[0].shape
    widths = [right.shape[1] for right in rights]
    columns = sum(widths)
    tiles = len(pair_tiles(widths, 1 if turned_rows else outs))
    pairs = len(lefts)
    shape = (turned_rows, rows) if turned_rows else (rows, columns // outs)
    return pl.pallas_call(
        functools.partial(
            pair_kernel, pairs, [first for _, first in adds], outs, turned_rows
        ),
        out_shape=(jax.ShapeDtypeStruct(shape, held),) * outs,
        in_specs=[ANY] * (2 * pairs + len(adds)),
        out_specs=(ANY,) * outs,
        scratch_shapes=[pltpu.VMEM((length, rows), BF)] * pairs
        + [pltpu.VMEM((length, width), BF) for width in widths]
        + [pltpu.VMEM((rows, columns), BF)] * len(adds)
        + [pltpu.VMEM(shape, held)] * outs
        + [pltpu.SemaphoreType.DMA((pairs + outs + tiles * (2 + len(adds)),))],
        compiler_params=params(52),
        cost_estimate=cost(time),
        name="pair_dot",
    )(*lefts, *rights, *[values for values, _ in adds])


def layer_kernel(low, he_hbm, hs_hbm, wo_hbm, wd_hbm, out_ref, he_ref, hs_ref, wo_ref, wd_ref, sems):
    rows = slice(low, low + he_ref.shape[0])
    copies = Copies(sems)
    brought = [
        copies.start(he_hbm.at[rows], he_ref),
        copies.start(hs_hbm.at[rows], hs_ref),
    ]
    tiles = tiles_of(wo_ref.shape[0], IN_TILE)
    weights = [
        (
            copies.start(wo_hbm.at[a:b], wo_ref.at[a:b]),
            copies.start(wd_hbm.at[:, a:b], wd_ref.at[:, a:b]),
        )
        for a, b in tiles
    ]
    for copy in brought:
        copy.wait()
    for started, (a, b) in zip(weights, tiles):
        for copy in started:
            copy.wait()
        out = right_dot(he_ref[...], wo_ref[a:b]) + plain_dot(hs_ref[:, : wd_ref.shape[0]], wd_ref[:, a:b])
        out_ref[:, a:b] = out.astype(BF)


def layer_part(low, high, hid_e, hid_s, weight_out, weight_down, time):
    width, units = weight_out.shape
    shared = weight_down.shape[0]
    rows = high - low
    return pl.pallas_call(
        functools.partial(layer_kernel, low),
        out_shape=jax.ShapeDtypeStruct((rows, width), BF),
        in_specs=[ANY] * 4,
        out_specs=WHOLE,
        scratch_shapes=[
            pltpu.VMEM((rows, units), BF),
            pltpu.VMEM((rows, hid_s.shape[1]), BF),
            pltpu.VMEM((width, units), BF),
            pltpu.VMEM((shared, width), BF),
            pltpu.SemaphoreType.DMA((2 + 2 * len(tiles_of(width, IN_TILE)),)),
        ],
        compiler_params=params(48),
        cost_estimate=cost(time),
        name="layer_part",
    )(hid_e, hid_s, weight_out, weight_down)


def past_units_kernel(
    experts, residual_ref, own_ref, ahead_ref, behind_ref, grad_ref, gain_ref, head_ref,
    routed_ref, picked_ref, sent_ref, out_ref, low_ref, rows_ref, gain_out,
):
    width = residual_ref.shape[1]
    total = own_ref[...].astype(F32) + ahead_ref[...].astype(F32) + behind_ref[...].astype(F32)
    small = total[:, width:]
    routed = routed_ref[...]
    lane = lax.broadcasted_iota(jnp.int32, small.shape, 1)
    probs = jnp.where(lane < experts, routed, 0.0)
    grads = picked_ref[...] * (small + pltpu.roll(small, 128 - experts, 1))
    grads = jnp.where(lane < experts, grads, 0.0)
    logits = probs * (grads - jnp.sum(probs * grads, 1, keepdims=True))
    switch = jnp.where(lane == 2 * experts, routed, 0.0)
    of_switch = jnp.where((lane >= 2 * experts) & (lane < 4 * experts), small, 0.0)
    of_switch = jnp.sum(of_switch, 1, keepdims=True) * switch * (1.0 - switch)
    scores = logits + of_switch
    high = scores.astype(BF)
    rest = (scores - high.astype(F32)).astype(BF)
    grad = total[:, :width] + plain_dot(high, head_ref[...]) + plain_dot(rest, head_ref[...])
    h = sent_ref[:, :width]
    rows_ref[...] = left_dot(high, h) + left_dot(rest, h)
    residual = residual_ref[...]
    scale = rms_scale(residual)
    unit = residual * scale
    gain_out[...] = jnp.sum(grad * unit, 0, keepdims=True)
    grad = grad * gain_ref[...].astype(F32)
    mean = jnp.mean(grad * unit, -1, keepdims=True)
    out = grad_ref[...].astype(F32) + scale * (grad - unit * mean)
    out_ref[...] = out
    low_ref[...] = out.astype(BF)


def past_units(experts, residual, own, ahead, behind, grad, gain, head, routed, picked, sent):
    rows, width = residual.shape
    return pl.pallas_call(
        functools.partial(past_units_kernel, experts),
        out_shape=(
            jax.ShapeDtypeStruct((rows, width), F32),
            jax.ShapeDtypeStruct((rows, width), BF),
            jax.ShapeDtypeStruct((128, width), F32),
            jax.ShapeDtypeStruct((1, width), F32),
        ),
        in_specs=[WHOLE] * 10,
        out_specs=(WHOLE,) * 4,
        compiler_params=params(40),
        cost_estimate=cost(0),
        name="past_units",
    )(residual, own, ahead, behind, grad, gain, head, routed, picked, sent)


def routing_kernel(
    experts, x_ref, own_ref, ahead_ref, behind_ref, gain_ref, head_ref, picked_ref,
    residual_ref, sent_ref, routing_ref,
):
    width = x_ref.shape[1]
    residual = x_ref[...].astype(F32) + own_ref[...].astype(F32)
    residual = residual + ahead_ref[...].astype(F32) + behind_ref[...].astype(F32)
    h = (residual * rms_scale(residual) * gain_ref[...].astype(F32)).astype(BF)
    scores = right_dot(h, head_ref[...])
    lane = lax.broadcasted_iota(jnp.int32, scores.shape, 1)
    is_expert = lane < experts
    raised = jnp.where(is_expert, scores, -jnp.inf)
    raised = jnp.exp(raised - jnp.max(raised, 1, keepdims=True))
    probs = raised / jnp.sum(raised, 1, keepdims=True)
    switch = jnp.where(lane == 2 * experts, 1.0 / (1.0 + jnp.exp(-scores)), 0.0)
    values = probs * picked_ref[...] + switch
    high = values.astype(BF).astype(F32)
    rest = pltpu.roll(values - high, experts, 1)
    residual_ref[...] = residual
    routing_ref[...] = probs + switch
    sent_ref[:, :width] = h
    sent_ref[:, width:] = (high + rest).astype(BF)


def routing(experts, x, own, ahead, behind, gain, head, picked, time=0):
    rows, width = x.shape
    return pl.pallas_call(
        functools.partial(routing_kernel, experts),
        out_shape=(
            jax.ShapeDtypeStruct((rows, width), F32),
            jax.ShapeDtypeStruct((rows, width + 128), BF),
            jax.ShapeDtypeStruct((rows, 128), F32),
        ),
        in_specs=[WHOLE] * 7,
        out_specs=(WHOLE,) * 3,
        compiler_params=params(40),
        cost_estimate=cost(time),
        name="routing",
    )(x, own, ahead, behind, gain, head, picked)


def shards(
    tokens,
    attention_gain,
    query_weight,
    query_bias,
    key_weight,
    key_bias,
    value_weight,
    value_bias,
    output_weight,
    feedforward_gain,
    shared_gate_weight,
    shared_up_weight,
    shared_down_weight,
    shared_switch,
    router_weight,
    expert_in,
    expert_out,
    routes,
    cotangent,
):
    tok_rows, model_width = tokens.shape
    groups = lax.axis_size("expert")
    me = lax.axis_index("expert").astype(jnp.int32)[None]
    ring = Ring(groups)
    length = tok_rows * groups
    experts = router_weight.shape[1]
    weight_in = expert_in[0]
    weight_out = expert_out[0]
    weight_gate = shared_gate_weight.T
    weight_up = shared_up_weight.T
    weight_down = shared_down_weight.T
    x_float = tokens.astype(F32)
    rms_attn = rms_scale(x_float)
    unit_attn = x_float * rms_attn
    gain_attn = attention_gain.astype(F32)
    h_attn = (unit_attn * gain_attn).astype(BF)

    lanes = jnp.arange(128, dtype=jnp.int32)
    picked = jnp.sum((routes[:, :, None] == lanes).astype(F32), 1)
    head = jnp.concatenate(
        [
            router_weight.T,
            jnp.zeros((experts, model_width), BF),
            shared_switch[None],
            jnp.zeros((127 - 2 * experts, model_width), BF),
        ],
        0,
    )

    gather_attn = Gather(ring, h_attn)
    last = gather_attn.step()
    tables = rope_tables(length)
    last = gather_attn.step(tables, head, picked)
    h_attn_parts = gather_attn.rest()
    gather_cot = Gather(ring, after(cotangent, *gather_attn.pieces[-2:]))
    of_cot = gather_cot.step()

    q_rot, k_rot, v_low, *h_attn_split, h_attn_all = project(
        ring,
        h_attn_parts,
        (query_weight, key_weight, value_weight),
        (query_bias, key_bias, value_bias),
        tables,
    )
    att_low = attend(ring, q_rot, k_rot, v_low)
    sum_att = Scatter(
        ring, [right_dot(after(att_low, of_cot), output_weight).astype(BF)], tok_rows
    )
    backs = []
    cotangent_split = []

    def next_back(*others):
        which = len(backs)
        parts = after(gather_cot.chunk(which), *others)
        new = back_units(ring, which, parts, weight_out, weight_down, cotangent_split)
        cotangent_split[:] = new[2:]
        backs.append(new[:2])
        return new[:2]

    befores = [sum_att.chunks, move(ring, [sum_att, gather_cot])]
    while sum_att.at:
        busy = next_back(befores[-2])
        rounds = [sum_att] + [gather_cot] * (gather_cot.at < ring.half)
        befores.append(move(ring, rounds, busy))
    busy = next_back(befores[-2])

    residual, h_sent, routed = routing(
        experts,
        tokens,
        sum_att.own(0),
        sum_att.ahead,
        after(sum_att.behind, busy),
        feedforward_gain[None],
        head,
        picked,
    )

    gather_ffn = Gather(ring, h_sent)
    last = gather_ffn.step()
    busy = ()
    smalls = []
    kept = []

    def next_units(*others):
        which = len(smalls)
        parts = after(gather_ffn.chunk(which), *others)
        small, *new = hidden_units(
            ring,
            which,
            me,
            experts,
            parts,
            weight_in,
            weight_gate,
            weight_up,
            *backs[which],
            kept,
        )
        kept[:] = new
        smalls.append(small)
        return small

    while gather_ffn.at < ring.half:
        last = gather_ffn.step(busy)
        busy = next_units()
    next_units()
    hid_e, hid_s, grad_joined, grad_shared, *h_ffn_split = kept

    def chunk_in(which, time, *others):
        return units_in(
            which,
            *after((grad_joined, grad_shared), *others),
            smalls[which],
            weight_in,
            weight_gate,
            weight_up,
            time,
        )

    out_e = PairSum([cotangent_split], [hid_e])
    out_s = PairSum([cotangent_split], [hid_s])
    in_e = PairSum([h_ffn_split], [grad_joined])
    in_s = PairSum([h_ffn_split], [grad_shared])
    half_rows = length // 2

    def layer_rows(low, time, *others):
        return layer_part(
            low, low + half_rows, *after((hid_e, hid_s), *others), weight_out, weight_down, time
        )

    chunks = [None] * ring.half
    layer_parts = [None, None]
    busy = in_e.cores()
    chunks[-1] = chunk_in(ring.half - 1, 70, busy)
    sum_ffn = Scatter(ring, chunks, tok_rows)
    befores = [chunks[-1], sum_ffn.step()]
    busy = chunks[-1]
    works = [(6, None), (6, in_e.chips), (12, out_s.cores)]
    for at, which in enumerate(range(ring.half - 2, -1, -1)):
        time, work = works[at] if at < len(works) else (6, None)
        if at == 1:
            busy = in_e.chips(busy, befores[-2], time=6)
            time, work = 0, None
        chunks[which] = chunk_in(which, time, busy, befores[-2])
        busy = chunks[which]
        if work is not None:
            busy = (busy, work(busy))
        befores.append(sum_ffn.step(busy))
    layer_parts[1] = layer_rows(half_rows, 12, befores[-2], busy)
    busy = out_e.cores(layer_parts[1])

    grad_residual, attention_grad, score_rows, grad_ffn_gain_part = past_units(
        experts,
        residual,
        after(sum_ffn.own(0), busy),
        sum_ffn.ahead,
        sum_ffn.behind,
        cotangent,
        feedforward_gain[None],
        head,
        routed,
        picked,
        h_sent,
    )

    gather_grad = Gather(ring, attention_grad)
    first = gather_grad.step()
    layer_parts[0] = layer_rows(0, 35, attention_grad)
    busy = out_e.chips(layer_parts[0])
    second = gather_grad.step(busy)
    busy = in_s.cores(first, busy, time=7.5)
    busy = out_s.chips(busy)
    third = gather_grad.step(busy)
    totals = in_e.total(second, busy, time=7.5)
    last = gather_grad.step(totals)
    while gather_grad.at < ring.half:
        last = gather_grad.step()
    attention_grad_parts = gather_grad.rest()
    sum_layer = Scatter(ring, layer_parts, tok_rows)
    of_layer = sum_layer.step(last)
    grad_att, *grad_split = reorder_dot(
        ring, after(attention_grad_parts, totals), output_weight
    )
    grads, biases = attend_back(ring, q_rot, k_rot, v_low, grad_att, tables)
    attn_part, gain_part = attend_in(
        after(grads, of_layer),
        (query_weight, key_weight, value_weight),
        h_attn_all,
        gain_attn[None],
    )
    sum_attn = Scatter(ring, [attn_part], tok_rows)
    first = move(ring, [sum_attn, sum_layer])

    sums = jnp.concatenate(
        [
            gain_part,
            score_rows[2 * experts : 2 * experts + 1],
            grad_ffn_gain_part,
            score_rows[:experts],
        ],
        0,
    )
    in_qkvo = PairSum([h_attn_split, grad_split], [grads, att_low])
    packed = jnp.concatenate([sums.reshape(-1), biases[0]]).reshape(-1, 128)
    for axis, moves in cube_steps("dp"):
        packed = packed + lax.ppermute(packed, axis, moves)
    totals += out_e.total(attn_part, time=6)
    busy = in_qkvo.cores(totals)
    sums = packed.reshape(-1)[: sums.size].reshape(sums.shape)
    rounds = [sum_attn, sum_layer]
    befores = [attn_part, first]
    shared_cols = shared_gate_weight.shape[1]
    while sum_layer.at:
        befores.append(move(ring, rounds, busy))
        if len(befores) == 3:
            busy = in_s.chips(befores[-2], busy, time=6)
            totals += out_s.total(busy, turned_rows=shared_cols)
            busy = totals
        elif len(befores) == 4:
            busy = in_qkvo.chips(befores[-2], totals, time=6)
    last = sum_attn.step()
    totals += in_s.total(befores[-1], busy, time=3, outs=2, turned_rows=shared_cols)
    while sum_attn.at:
        last = sum_attn.step()
    for axis, moves in cube_steps("expert"):
        sums = sums + lax.ppermute(after(sums, last), axis, moves)
    biases = packed.reshape(-1)[sums.size :].reshape(3, -1)

    layer_out = (residual + sum_layer.rest()).astype(BF)
    grad_attn_in = sum_attn.rest()
    grad_unit_attn = grad_attn_in * gain_attn
    grad_tokens = grad_residual + rms_attn * (
        grad_unit_attn - unit_attn * jnp.mean(grad_unit_attn * unit_attn, -1, keepdims=True)
    )
    qkv = in_qkvo.total(last, outs=4)
    return (
        layer_out,
        grad_tokens,
        sums[0],
        qkv[0],
        biases[0],
        qkv[1],
        biases[1],
        qkv[2],
        biases[2],
        qkv[3],
        sums[2],
        totals[3].T,
        totals[4].T,
        totals[2].T,
        sums[1],
        sums[3:].T,
        totals[0][None],
        totals[1][None],
    )


def solution(mesh):
    return jax.shard_map(
        shards,
        mesh=mesh,
        in_specs=(
            P(("dp", "expert"), None),
            P(),
            P(None, "expert"),
            P("expert"),
            P(None, "expert"),
            P("expert"),
            P(None, "expert"),
            P("expert"),
            P(None, "expert"),
            P(),
            P(None, "expert"),
            P(None, "expert"),
            P(None, "expert"),
            P(),
            P(),
            P("expert", None, None),
            P("expert", None, None),
            P(("dp", "expert"), None),
            P(("dp", "expert"), None),
        ),
        out_specs=(
            P(("dp", "expert"), None),
            P(("dp", "expert"), None),
            P(),
            P("dp", "expert"),
            P("expert"),
            P("dp", "expert"),
            P("expert"),
            P("dp", "expert"),
            P("expert"),
            P("dp", "expert"),
            P(),
            P("dp", "expert"),
            P("dp", "expert"),
            P("dp", "expert"),
            P(),
            P(),
            P("expert", "dp", None),
            P("expert", "dp", None),
        ),
        check_vma=False,
    )
```
